32 devices in a mesh: group: 2 (over x), exp: 16 (over z, y, core).
Axes of the slice: x: 2, y: 2, z: 4, core: 2. Of those that a mesh axis runs over, the one named last changes fastest.
Arguments:
- tokens: bfloat16 [4096, 3584], P(('group', 'exp')), parts along dimension 0
- norm_gain: float32 [3584], replicated, may hold values from 0.25 to 1.75
- expert_ids: int32 [4096, 8], P(('group', 'exp')), parts along dimension 0, may hold values from 0 to 255, as said below
- gate_weights: float32 [4096, 8], P(('group', 'exp')), parts along dimension 0, may hold values from 0.2 to 2.5
- w_gate: bfloat16 [16, 3584, 512], P('exp'), may hold values from -0.09375 to 0.09375
- w_up: bfloat16 [16, 3584, 512], P('exp'), may hold values from -0.09375 to 0.09375
- w_down: bfloat16 [16, 512, 3584], P('exp'), may hold values from -0.1875 to 0.1875
Outputs:
- routed_out: bfloat16 [4096, 3584], P(('group', 'exp')), parts along dimension 0
The draws below stay inside these ranges and needn't reach their ends.
There are 2 independent parts, one for each index of `group`. The reference program is written for one: setup_inputs(seed, part) draws one part's arguments, and reference() takes and returns one part's arrays. A program takes and returns all parts, laid end to end along the dimension named above; an argument that names none is the same for every part. Nothing has to cross between parts.
Inputs may be any that keep to these rules, and one draw needn't show every extreme that they name: `expert_ids`: each row names 8 different experts. Among the rows of one device an expert below 8 is named by at most 7 rows; in every draw one such expert is named by exactly 7 rows of every device.
All inputs are finite; a program needn't handle non-finite values.
Results may differ from the reference program's by a relative error of at most 0.0072.
Values may be sent and summed in bfloat16 or wider, within the bound.
No kernel may reach another device: no remote copies, remote signals or barrier semaphores. Data moves between devices by JAX's collectives and lax.ppermute only.
A program may use at most 128 MiB of HBM per device.

```python
import math
import jax
import jax.numpy as jnp
from jax import lax

D = 3584
FW = 1024
EXPERTS = 256
TOP = 8
TOK_DEV = 128
HALF = 512
SHARDS = 16
FLIGHT = 8
CAP = 7
TOKENS = 2048
N_EXP = 16


def draw_tokens(key, part):
    key = jax.random.fold_in(key, 5)
    key_rows, key_cols, key_base = jax.random.split(key, 3)
    row_scale = jnp.exp(jax.random.uniform(key_rows, (TOKENS, 1), jnp.float32, 0.0, math.log(10.0)))
    col_scale = jnp.exp(jax.random.uniform(key_cols, (1, D), jnp.float32, 0.0, math.log(10.0)))
    base_draw = jnp.clip(jax.random.normal(key_base, (TOKENS, D), jnp.float32), -6.0, 6.0)
    return (base_draw * row_scale * col_scale).astype(jnp.bfloat16)


def draw_expert_ids(key, part):
    key = jax.random.fold_in(key, 11)
    key_level, key_jitter, key_hot, key_partner, key_order = jax.random.split(key, 5)
    blocks = N_EXP
    flight = N_EXP // 2
    assign_count = TOK_DEV * TOP
    mean_load = assign_count // EXPERTS
    load_level = jax.random.randint(key_level, (flight,), -1, 3)
    jitter = jax.random.randint(key_jitter, (blocks, flight), -1, 2)
    offset = jnp.clip(load_level[None, :] + jitter, -2, 4)
    hot_expert = jax.random.randint(key_hot, (), 0, flight)
    offset = jnp.where(jnp.arange(flight)[None, :] == hot_expert, 4, offset)
    partner = jax.random.permutation(key_partner, EXPERTS - flight)[:flight] + flight
    counts = jnp.full((blocks, EXPERTS), mean_load, jnp.int32)
    counts = counts.at[:, :flight].set(mean_load - 1 + offset)
    counts = counts.at[:, partner].set(mean_load + 1 - offset)
    order_keys = jax.random.split(key_order, blocks)
    id_order = jax.vmap(lambda one_key: jax.random.permutation(one_key, EXPERTS))(order_keys).astype(jnp.int32)

    def one_block(block_order, block_counts):
        ordered_counts = block_counts[block_order]
        cum_counts = jnp.cumsum(ordered_counts)
        places = jnp.arange(assign_count, dtype=jnp.int32)
        group_index = jnp.sum((places[:, None] >= cum_counts[None, :]).astype(jnp.int32), axis=1)
        sequence = block_order[group_index]
        return sequence.reshape(TOP, TOK_DEV).T
    table = jax.vmap(one_block)(id_order, counts)
    return table.reshape(blocks * TOK_DEV, TOP).astype(jnp.int32)


def block_scale(own_key, dims, cuts, least, largest):
    def one(axis_at, shards_of):
        steps = jax.random.uniform(jax.random.fold_in(jax.random.fold_in(own_key, 6), axis_at), (shards_of,), jnp.float32, least / len(cuts), largest / len(cuts))
        return jnp.repeat(jnp.exp(steps), dims[axis_at] // shards_of).reshape((-1,) + (1,) * (len(dims) - axis_at - 1))

    factor_of = one(*cuts[0])
    for cut in cuts[1:]:
        factor_of = factor_of * one(*cut)
    return factor_of


def normal_values(rng, shape, scale, bound, cuts=(), kind=jnp.bfloat16):
    values = scale * jax.random.normal(rng, shape, jnp.float32)
    if cuts:
        values = values * block_scale(rng, shape, cuts, -0.22, 0.18)
    return jnp.clip(values, -bound, bound).astype(kind)


def setup_inputs(seed: int = 0, part: int = 0) -> dict:
    streams_of = jax.random.split(jax.random.key(seed), 8)
    part_splits = jax.random.split(jax.random.fold_in(streams_of[7], part), 8)
    tokens = draw_tokens(jax.random.fold_in(jax.random.fold_in(streams_of[7], part), 71), part)
    norm_gain = jnp.clip(1.0 + 0.15 * jax.random.normal(streams_of[1], (D,), jnp.float32), 0.25, 1.75)
    expert_ids = draw_expert_ids(jax.random.fold_in(jax.random.fold_in(streams_of[7], part), 71), part)
    gate_weights = jnp.clip(jnp.exp(math.log(2.5) - 2.5257286 * jax.random.uniform(part_splits[3], (TOKENS, TOP), jnp.float32) ** block_scale(part_splits[3], (TOKENS, TOP), ((0, 16),), -0.2, 0.2)), 0.2, 2.5)
    w_gate = normal_values(streams_of[4], (SHARDS, D, HALF), D ** -0.5, 0.09375, ((0, 16),))
    w_up = normal_values(streams_of[5], (SHARDS, D, HALF), D ** -0.5, 0.09375, ((0, 16),))
    w_down = normal_values(streams_of[6], (SHARDS, HALF, D), FW ** -0.5, 0.1875, ((0, 16),))
    return dict(tokens=tokens, norm_gain=norm_gain, expert_ids=expert_ids, gate_weights=gate_weights, w_gate=w_gate, w_up=w_up, w_down=w_down)


def reference(tokens, norm_gain, expert_ids, gate_weights, w_gate, w_up, w_down):
    wide = tokens.astype(jnp.float32)
    mean_square = lax.optimization_barrier(jnp.mean(wide * wide, axis=1, keepdims=True))
    normed = (wide * lax.rsqrt(mean_square + 1e-06) * norm_gain[None, :]).astype(jnp.bfloat16)
    flat_ids = expert_ids.reshape(-1)
    flat_gates = gate_weights.reshape(-1)
    token_index = (jnp.arange(flat_ids.shape[0], dtype=jnp.int32) // TOP).astype(jnp.int32)
    buffer_rows = N_EXP * CAP

    def one_half(picked_rows, shard):
        gate_m = lax.dynamic_index_in_dim(w_gate, shard, 0, keepdims=False)
        up_m = lax.dynamic_index_in_dim(w_up, shard, 0, keepdims=False)
        down_m = lax.dynamic_index_in_dim(w_down, shard, 0, keepdims=False)
        gate_v = jnp.dot(picked_rows, gate_m, preferred_element_type=jnp.float32)
        up_v = jnp.dot(picked_rows, up_m, preferred_element_type=jnp.float32)
        hidden = (jax.nn.silu(gate_v) * up_v).astype(jnp.bfloat16)
        return jnp.dot(hidden, down_m, preferred_element_type=jnp.float32).astype(jnp.bfloat16)

    def one_expert(accum_out, expert):
        chosen = flat_ids == expert
        order_rank = (jnp.cumsum(chosen.astype(jnp.int32)) - 1).astype(jnp.int32)
        target = jnp.where(chosen, order_rank, buffer_rows).astype(jnp.int32)
        token_rows = jnp.zeros((buffer_rows,), jnp.int32).at[target].set(token_index, mode='drop')
        row_gates = jnp.zeros((buffer_rows,), jnp.float32).at[target].set(flat_gates, mode='drop')
        picked_rows = normed[token_rows]
        first = one_half(picked_rows, (2 * expert).astype(jnp.int32))
        second = one_half(picked_rows, (2 * expert + 1).astype(jnp.int32))
        summed = first.astype(jnp.float32) + second.astype(jnp.float32)
        accum_out = accum_out.at[token_rows].add(row_gates[:, None] * summed)
        return (accum_out, None)
    start = jnp.zeros((tokens.shape[0], tokens.shape[1]), jnp.float32)
    accum_out, unused = lax.scan(one_expert, start, jnp.arange(FLIGHT, dtype=jnp.int32))
    return accum_out.astype(jnp.bfloat16)
```

```python
import functools

import jax
import jax.numpy as jnp
from jax import lax
from jax.experimental import pallas as pl
from jax.experimental.pallas import tpu as pltpu
from jax.sharding import PartitionSpec as P

CAP = 7
SLOTS = 8

VMEM = pl.BlockSpec(memory_space=pltpu.VMEM)
ANY = pl.BlockSpec(memory_space=pl.ANY)


def dispatch_kernel(flight, tok_ref, gain_ref, ids_ref, gw_ref, out_ref, mix_ref):
    count = tok_ref.shape[0]
    wide = tok_ref[...].astype(jnp.float32)
    mean_square = jnp.mean(wide * wide, axis=1, keepdims=True)
    normed = (wide * lax.rsqrt(mean_square + 1e-06) * gain_ref[...]).astype(jnp.bfloat16)

    experts = lax.broadcasted_iota(jnp.int32, (flight, count), 0)
    chosen = jnp.zeros((flight, count), jnp.float32)
    gates = jnp.zeros((flight, count), jnp.float32)
    for k in range(ids_ref.shape[0]):
        hit = ids_ref[k : k + 1, :] == experts
        chosen = jnp.where(hit, 1.0, chosen)
        gates = jnp.where(hit, gw_ref[k : k + 1, :], gates)
    before = (
        lax.broadcasted_iota(jnp.int32, (count, count), 0)
        < lax.broadcasted_iota(jnp.int32, (count, count), 1)
    ).astype(jnp.bfloat16)
    rank = jnp.dot(chosen.astype(jnp.bfloat16), before, preferred_element_type=jnp.float32)
    rank = jnp.where(chosen > 0.0, rank, -1.0)

    slot = lax.broadcasted_iota(jnp.int32, (flight, SLOTS, count), 1).astype(jnp.float32)
    taken = rank[:, None, :] == slot
    pick = jnp.where(taken, 1.0, 0.0).reshape(flight * SLOTS, count).astype(jnp.bfloat16)
    out_ref[...] = jnp.dot(pick, normed, preferred_element_type=jnp.float32).astype(jnp.bfloat16)
    mix = jnp.where(taken, gates[:, None, :], 0.0).reshape(flight * SLOTS, count)
    high = mix.astype(jnp.bfloat16)
    mix_ref[: flight * SLOTS, :] = high
    mix_ref[flight * SLOTS :, :] = (mix - high.astype(jnp.float32)).astype(jnp.bfloat16)


def expert_kernel(own_ref, other_ref, gate_ref, up_ref, down_ref, own_out, other_out):
    rows = own_ref.shape[0]
    x = jnp.concatenate([own_ref[...], other_ref[...]], axis=0)
    gate_v = jnp.dot(x, gate_ref[...], preferred_element_type=jnp.float32)
    up_v = jnp.dot(x, up_ref[...], preferred_element_type=jnp.float32)
    hidden = (gate_v / (1.0 + jnp.exp(-gate_v)) * up_v).astype(jnp.bfloat16)
    part = jnp.dot(hidden, down_ref[...], preferred_element_type=jnp.float32).astype(jnp.bfloat16)
    own_out[...] = part[:rows]
    other_out[...] = part[rows:]


def combine_kernel(mix_ref, rows_ref, out_ref):
    rows = rows_ref[...]
    both = jnp.concatenate([rows, rows], axis=0)
    out_ref[...] = lax.dot_general(
        mix_ref[...], both, (((0,), (0,)), ((), ())), preferred_element_type=jnp.float32
    ).astype(jnp.bfloat16)


def per_device(tokens, norm_gain, expert_ids, gate_weights, w_gate, w_up, w_down):
    owners = lax.axis_size("exp")
    flight = owners // 2
    count, width = tokens.shape
    packed = flight * SLOTS
    same_core = [list(range(core, owners, 2)) for core in range(2)]
    swap = [(i, i ^ 1) for i in range(owners)]
    params = pltpu.CompilerParams(vmem_limit_bytes=24 * 2**20)

    outgoing, mix = pl.pallas_call(
        functools.partial(dispatch_kernel, flight),
        out_shape=(
            jax.ShapeDtypeStruct((packed, width), jnp.bfloat16),
            jax.ShapeDtypeStruct((2 * packed, count), jnp.bfloat16),
        ),
        in_specs=[VMEM] * 4,
        out_specs=(VMEM, VMEM),
        compiler_params=params,
        name="dispatch",
    )(tokens, norm_gain[None, :], expert_ids.T, gate_weights.T)

    own = lax.all_to_all(
        outgoing, "exp", split_axis=0, concat_axis=0, axis_index_groups=same_core, tiled=True
    )
    other = lax.ppermute(own, "exp", swap)
    own_part, other_part = pl.pallas_call(
        expert_kernel,
        out_shape=(jax.ShapeDtypeStruct((packed, width), jnp.bfloat16),) * 2,
        in_specs=[VMEM] * 5,
        out_specs=(VMEM, VMEM),
        compiler_params=params,
        cost_estimate=pl.CostEstimate(
            flops=12 * packed * width * w_gate.shape[2],
            bytes_accessed=6 * width * w_gate.shape[2],
            transcendentals=0,
        ),
        name="experts",
    )(own, other, w_gate[0], w_up[0], w_down[0])
    from_other = lax.ppermute(other_part, "exp", swap)
    joined = (own_part.astype(jnp.float32) + from_other.astype(jnp.float32)).astype(jnp.bfloat16)
    returned = lax.all_to_all(
        joined, "exp", split_axis=0, concat_axis=0, axis_index_groups=same_core, tiled=True
    )
    return pl.pallas_call(
        combine_kernel,
        out_shape=jax.ShapeDtypeStruct((count, width), jnp.bfloat16),
        in_specs=[VMEM] * 2,
        out_specs=VMEM,
        compiler_params=params,
        name="combine",
    )(mix, returned)


def solution(mesh):
    placed = (
        P(("group", "exp"), None),
        P(),
        P(("group", "exp"), None),
        P(("group", "exp"), None),
        P("exp", None, None),
        P("exp", None, None),
        P("exp", None, None),
    )
    return jax.shard_map(
        per_device, mesh=mesh, in_specs=placed, out_specs=P(("group", "exp"), None), check_vma=False
    )
```

```python
import functools

import jax
import jax.numpy as jnp
from jax import lax
from jax.experimental import pallas as pl
from jax.experimental.pallas import tpu as pltpu
from jax.sharding import PartitionSpec as P

SLOTS = 8
CHUNKS = 4

VMEM = pl.BlockSpec(memory_space=pltpu.VMEM)
HBM = pl.BlockSpec(memory_space=pltpu.HBM)


def in_hbm(*arrays):
    return [pltpu.with_memory_space_constraint(a, pltpu.HBM) for a in arrays]


def relative(flight):
    return flight <= 8


def dispatch_kernel(flight, tok_hbm, gain_hbm, ids_hbm, gw_hbm, mix_ref, *rest):
    outs = rest[:flight]
    tok, gain, ids, gw, normed, sems = rest[flight:]
    count = tok.shape[0]
    part = count // CHUNKS
    small = [
        pltpu.make_async_copy(ids_hbm, ids, sems.at[0]),
        pltpu.make_async_copy(gw_hbm, gw, sems.at[1]),
        pltpu.make_async_copy(gain_hbm, gain.at[0], sems.at[2]),
    ]
    large = [
        pltpu.make_async_copy(
            tok_hbm.at[pl.ds(i * part, part)], tok.at[pl.ds(i * part, part)], sems.at[3 + i]
        )
        for i in range(CHUNKS)
    ]
    for copy in small + large:
        copy.start()
    small[0].wait()
    small[1].wait()
    chip = lax.axis_index("exp") // 2 if relative(flight) else 0
    experts = lax.broadcasted_iota(jnp.int32, (flight, count), 0) ^ chip
    chosen = jnp.zeros((flight, count), jnp.float32)
    gates = jnp.zeros((flight, count), jnp.float32)
    for k in range(ids.shape[0]):
        hit = ids[k : k + 1, :] == experts
        chosen = jnp.where(hit, 1.0, chosen)
        gates = jnp.where(hit, gw[k : k + 1, :], gates)
    before = (
        lax.broadcasted_iota(jnp.int32, (count, count), 0)
        < lax.broadcasted_iota(jnp.int32, (count, count), 1)
    ).astype(jnp.bfloat16)
    rank = jnp.dot(chosen.astype(jnp.bfloat16), before, preferred_element_type=jnp.float32)
    rank = jnp.where(chosen > 0.0, rank, -1.0)

    slot = lax.broadcasted_iota(jnp.int32, (flight, SLOTS, count), 1).astype(jnp.float32)
    taken = rank[:, None, :] == slot
    pick = jnp.where(taken, 1.0, 0.0).reshape(flight * SLOTS, count).astype(jnp.bfloat16)
    mix = jnp.where(taken, gates[:, None, :], 0.0).reshape(flight * SLOTS, count)
    high = mix.astype(jnp.bfloat16)
    mix_ref[: flight * SLOTS, :] = high
    mix_ref[flight * SLOTS :, :] = (mix - high.astype(jnp.float32)).astype(jnp.bfloat16)

    small[2].wait()
    for i in range(CHUNKS):
        large[i].wait()
        wide = tok[pl.ds(i * part, part), :].astype(jnp.float32)
        mean_square = jnp.mean(wide * wide, axis=1, keepdims=True)
        normed[pl.ds(i * part, part), :] = (
            wide * lax.rsqrt(mean_square + 1e-06) * gain[...]
        ).astype(jnp.bfloat16)
    rows = jnp.dot(pick, normed[...], preferred_element_type=jnp.float32)
    for r in range(flight):
        outs[r][...] = rows[r * SLOTS : (r + 1) * SLOTS].astype(jnp.bfloat16)


def stage_kernel(gate_hbm, up_hbm, down_hbm, gate_ref, up_ref, down_ref, sems):
    copies = [
        pltpu.make_async_copy(source, target, sems.at[i])
        for i, (source, target) in enumerate(
            ((gate_hbm, gate_ref), (up_hbm, up_ref), (down_hbm, down_ref))
        )
    ]
    for copy in copies:
        copy.start()
    for copy in copies:
        copy.wait()


def expert_kernel(flight, *refs):
    blocks = refs[: 2 * flight]
    gate_ref, up_ref, down_ref = refs[2 * flight : 2 * flight + 3]
    outs = refs[2 * flight + 3 :]
    x = jnp.concatenate([b[...].astype(jnp.float32) for b in blocks], axis=0).astype(jnp.bfloat16)
    gate_v = jnp.dot(x, gate_ref[...], preferred_element_type=jnp.float32)
    up_v = jnp.dot(x, up_ref[...], preferred_element_type=jnp.float32)
    hidden = (gate_v / (1.0 + jnp.exp(-gate_v)) * up_v).astype(jnp.bfloat16)
    part = jnp.dot(hidden, down_ref[...], preferred_element_type=jnp.float32)
    for i, out in enumerate(outs):
        out[...] = part[i * SLOTS : (i + 1) * SLOTS].astype(jnp.bfloat16)


def combine_kernel(flight, mix_ref, *refs):
    rows = jnp.concatenate([b[...].astype(jnp.float32) for b in refs[:flight]], axis=0)
    rows = rows.astype(jnp.bfloat16)
    out_ref = refs[flight]
    both = jnp.concatenate([rows, rows], axis=0)
    out_ref[...] = lax.dot_general(
        mix_ref[...], both, (((0,), (0,)), ((), ())), preferred_element_type=jnp.float32
    ).astype(jnp.bfloat16)


def per_device(tokens, norm_gain, expert_ids, gate_weights, w_gate, w_up, w_down):
    owners = lax.axis_size("exp")
    flight = owners // 2
    count, width = tokens.shape
    hidden = w_gate.shape[2]
    packed = flight * SLOTS
    block = jax.ShapeDtypeStruct((SLOTS, width), jnp.bfloat16)

    few = relative(flight)

    def exchange(blocks):
        if few:
            return [blocks[0]] + [
                lax.ppermute(blocks[r], "exp", [(i, i ^ (2 * r)) for i in range(owners)])
                for r in range(1, flight)
            ]
        groups = [list(range(core, owners, 2)) for core in range(2)]
        got = lax.all_to_all(
            jnp.stack(blocks), "exp", split_axis=0, concat_axis=0, axis_index_groups=groups, tiled=True
        )
        return [got[r] for r in range(flight)]

    def swap(blocks):
        pairs = [(i, i ^ 1) for i in range(owners)]
        if few:
            return [lax.ppermute(b, "exp", pairs) for b in blocks]
        got = lax.ppermute(jnp.stack(blocks), "exp", pairs)
        return [got[r] for r in range(flight)]

    mix, *outgoing = pl.pallas_call(
        functools.partial(dispatch_kernel, flight),
        out_shape=(jax.ShapeDtypeStruct((2 * packed, count), jnp.bfloat16),) + (block,) * flight,
        in_specs=[HBM] * 4,
        out_specs=(VMEM,) * (flight + 1),
        scratch_shapes=[
            pltpu.VMEM((count, width), jnp.bfloat16),
            pltpu.VMEM((1, width), jnp.float32),
            pltpu.VMEM(expert_ids.shape[::-1], jnp.int32),
            pltpu.VMEM(gate_weights.shape[::-1], jnp.float32),
            pltpu.VMEM((count, width), jnp.bfloat16),
            pltpu.SemaphoreType.DMA((3 + CHUNKS,)),
        ],
        compiler_params=pltpu.CompilerParams(vmem_limit_bytes=32 * 2**20),
        name="dispatch",
    )(*in_hbm(tokens, norm_gain, expert_ids.T, gate_weights.T))

    staged = pl.pallas_call(
        stage_kernel,
        out_shape=tuple(
            jax.ShapeDtypeStruct(w.shape[1:], w.dtype) for w in (w_gate, w_up, w_down)
        ),
        in_specs=[HBM] * 3,
        out_specs=(VMEM,) * 3,
        scratch_shapes=[pltpu.SemaphoreType.DMA((3,))],
        compiler_params=pltpu.CompilerParams(vmem_limit_bytes=16 * 2**20),
        cost_estimate=pl.CostEstimate(
            flops=0, bytes_accessed=12 * width * hidden, transcendentals=0
        ),
        name="stage",
    )(*in_hbm(w_gate[0], w_up[0], w_down[0]))

    own = exchange(outgoing)
    other = swap(own)
    parts = pl.pallas_call(
        functools.partial(expert_kernel, flight),
        out_shape=(block,) * (2 * flight),
        in_specs=[VMEM] * (2 * flight + 3),
        out_specs=(VMEM,) * (2 * flight),
        compiler_params=pltpu.CompilerParams(vmem_limit_bytes=24 * 2**20),
        cost_estimate=pl.CostEstimate(
            flops=12 * packed * width * hidden,
            bytes_accessed=6 * width * hidden,
            transcendentals=0,
        ),
        name="experts",
    )(*own, *other, *staged)
    from_other = swap(parts[flight:])
    joined = [
        (a.astype(jnp.float32) + b.astype(jnp.float32)).astype(jnp.bfloat16)
        for a, b in zip(parts[:flight], from_other)
    ]
    returned = exchange(joined)
    return pl.pallas_call(
        functools.partial(combine_kernel, flight),
        out_shape=jax.ShapeDtypeStruct((count, width), jnp.bfloat16),
        in_specs=[VMEM] * (flight + 1),
        out_specs=VMEM,
        compiler_params=pltpu.CompilerParams(vmem_limit_bytes=24 * 2**20),
        name="combine",
    )(mix, *returned)


def solution(mesh):
    placed = (
        P(("group", "exp"), None),
        P(),
        P(("group", "exp"), None),
        P(("group", "exp"), None),
        P("exp", None, None),
        P("exp", None, None),
        P("exp", None, None),
    )
    return jax.shard_map(
        per_device, mesh=mesh, in_specs=placed, out_specs=P(("group", "exp"), None), check_vma=False
    )
```

```python
import functools

import jax
import jax.numpy as jnp
from jax import lax
from jax.experimental import pallas as pl
from jax.experimental.pallas import tpu as pltpu
from jax.sharding import PartitionSpec as P

SLOTS = 8
CHUNKS = 4

VMEM = pl.BlockSpec(memory_space=pltpu.VMEM)
HBM = pl.BlockSpec(memory_space=pltpu.HBM)


def in_hbm(*arrays):
    return [pltpu.with_memory_space_constraint(a, pltpu.HBM) for a in arrays]


def dispatch_kernel(flight, tok_hbm, gain_hbm, ids_hbm, gw_hbm, mix_ref, *rest):
    out_ref, tok, gain, ids, gw, normed, sems = rest
    count = tok.shape[0]
    part = count // CHUNKS
    small = [
        pltpu.make_async_copy(ids_hbm, ids, sems.at[0]),
        pltpu.make_async_copy(gw_hbm, gw, sems.at[1]),
        pltpu.make_async_copy(gain_hbm, gain.at[0], sems.at[2]),
    ]
    large = [
        pltpu.make_async_copy(
            tok_hbm.at[pl.ds(i * part, part)], tok.at[pl.ds(i * part, part)], sems.at[3 + i]
        )
        for i in range(CHUNKS)
    ]
    for copy in small + large:
        copy.start()
    small[0].wait()
    small[1].wait()
    experts = lax.broadcasted_iota(jnp.int32, (flight, count), 0)
    chosen = jnp.zeros((flight, count), jnp.float32)
    gates = jnp.zeros((flight, count), jnp.float32)
    for k in range(ids.shape[0]):
        hit = ids[k : k + 1, :] == experts
        chosen = jnp.where(hit, 1.0, chosen)
        gates = jnp.where(hit, gw[k : k + 1, :], gates)
    before = (
        lax.broadcasted_iota(jnp.int32, (count, count), 0)
        < lax.broadcasted_iota(jnp.int32, (count, count), 1)
    ).astype(jnp.bfloat16)
    rank = jnp.dot(chosen.astype(jnp.bfloat16), before, preferred_element_type=jnp.float32)
    rank = jnp.where(chosen > 0.0, rank, -1.0)

    slot = lax.broadcasted_iota(jnp.int32, (flight, SLOTS, count), 1).astype(jnp.float32)
    taken = rank[:, None, :] == slot
    pick = jnp.where(taken, 1.0, 0.0).reshape(flight * SLOTS, count).astype(jnp.bfloat16)
    mix = jnp.where(taken, gates[:, None, :], 0.0).reshape(flight * SLOTS, count)
    high = mix.astype(jnp.bfloat16)
    mix_ref[: flight * SLOTS, :] = high
    mix_ref[flight * SLOTS :, :] = (mix - high.astype(jnp.float32)).astype(jnp.bfloat16)

    small[2].wait()
    for i in range(CHUNKS):
        large[i].wait()
        wide = tok[pl.ds(i * part, part), :].astype(jnp.float32)
        mean_square = jnp.mean(wide * wide, axis=1, keepdims=True)
        normed[pl.ds(i * part, part), :] = (
            wide * lax.rsqrt(mean_square + 1e-06) * gain[...]
        ).astype(jnp.bfloat16)
    out_ref[...] = jnp.dot(pick, normed[...], preferred_element_type=jnp.float32).astype(jnp.bfloat16)


def stage_kernel(gate_hbm, up_hbm, down_hbm, gate_ref, up_ref, down_ref, sems):
    copies = [
        pltpu.make_async_copy(source, target, sems.at[i])
        for i, (source, target) in enumerate(
            ((gate_hbm, gate_ref), (up_hbm, up_ref), (down_hbm, down_ref))
        )
    ]
    for copy in copies:
        copy.start()
    for copy in copies:
        copy.wait()


def expert_kernel(own_ref, other_ref, gate_ref, up_ref, down_ref, own_out, other_out):
    rows = own_ref.shape[0]
    x = jnp.concatenate([own_ref[...], other_ref[...]], axis=0)
    gate_v = jnp.dot(x, gate_ref[...], preferred_element_type=jnp.float32)
    up_v = jnp.dot(x, up_ref[...], preferred_element_type=jnp.float32)
    hidden = (gate_v / (1.0 + jnp.exp(-gate_v)) * up_v).astype(jnp.bfloat16)
    part = jnp.dot(hidden, down_ref[...], preferred_element_type=jnp.float32).astype(jnp.bfloat16)
    own_out[...] = part[:rows]
    other_out[...] = part[rows:]


def combine_kernel(mix_ref, rows_ref, out_ref):
    rows = rows_ref[...]
    both = jnp.concatenate([rows, rows], axis=0)
    out_ref[...] = lax.dot_general(
        mix_ref[...], both, (((0,), (0,)), ((), ())), preferred_element_type=jnp.float32
    ).astype(jnp.bfloat16)


def per_device(tokens, norm_gain, expert_ids, gate_weights, w_gate, w_up, w_down):
    owners = lax.axis_size("exp")
    flight = owners // 2
    count, width = tokens.shape
    hidden = w_gate.shape[2]
    packed = flight * SLOTS
    block = jax.ShapeDtypeStruct((packed, width), jnp.bfloat16)
    pairs = [(i, i ^ 1) for i in range(owners)]
    groups = [list(range(core, owners, 2)) for core in range(2)]

    def exchange(rows):
        return lax.all_to_all(
            rows, "exp", split_axis=0, concat_axis=0, axis_index_groups=groups, tiled=True
        )

    mix, outgoing = pl.pallas_call(
        functools.partial(dispatch_kernel, flight),
        out_shape=(jax.ShapeDtypeStruct((2 * packed, count), jnp.bfloat16), block),
        in_specs=[HBM] * 4,
        out_specs=(VMEM, VMEM),
        scratch_shapes=[
            pltpu.VMEM((count, width), jnp.bfloat16),
            pltpu.VMEM((1, width), jnp.float32),
            pltpu.VMEM(expert_ids.shape[::-1], jnp.int32),
            pltpu.VMEM(gate_weights.shape[::-1], jnp.float32),
            pltpu.VMEM((count, width), jnp.bfloat16),
            pltpu.SemaphoreType.DMA((3 + CHUNKS,)),
        ],
        compiler_params=pltpu.CompilerParams(vmem_limit_bytes=32 * 2**20),
        name="dispatch",
    )(*in_hbm(tokens, norm_gain, expert_ids.T, gate_weights.T))

    staged = pl.pallas_call(
        stage_kernel,
        out_shape=tuple(
            jax.ShapeDtypeStruct(w.shape[1:], w.dtype) for w in (w_gate, w_up, w_down)
        ),
        in_specs=[HBM] * 3,
        out_specs=(VMEM,) * 3,
        scratch_shapes=[pltpu.SemaphoreType.DMA((3,))],
        compiler_params=pltpu.CompilerParams(vmem_limit_bytes=16 * 2**20),
        cost_estimate=pl.CostEstimate(
            flops=0, bytes_accessed=12 * width * hidden, transcendentals=0
        ),
        name="stage",
    )(*in_hbm(w_gate[0], w_up[0], w_down[0]))

    own = exchange(outgoing)
    other = lax.ppermute(own, "exp", pairs)
    own_part, other_part = pl.pallas_call(
        expert_kernel,
        out_shape=(block, block),
        in_specs=[VMEM] * 5,
        out_specs=(VMEM, VMEM),
        compiler_params=pltpu.CompilerParams(vmem_limit_bytes=24 * 2**20),
        cost_estimate=pl.CostEstimate(
            flops=12 * packed * width * hidden,
            bytes_accessed=6 * width * hidden,
            transcendentals=0,
        ),
        name="experts",
    )(own, other, *staged)
    from_other = lax.ppermute(other_part, "exp", pairs)
    joined = (own_part.astype(jnp.float32) + from_other.astype(jnp.float32)).astype(jnp.bfloat16)
    return pl.pallas_call(
        combine_kernel,
        out_shape=jax.ShapeDtypeStruct((count, width), jnp.bfloat16),
        in_specs=[VMEM] * 2,
        out_specs=VMEM,
        compiler_params=pltpu.CompilerParams(vmem_limit_bytes=24 * 2**20),
        name="combine",
    )(mix, exchange(joined))


def solution(mesh):
    placed = (
        P(("group", "exp"), None),
        P(),
        P(("group", "exp"), None),
        P(("group", "exp"), None),
        P("exp", None, None),
        P("exp", None, None),
        P("exp", None, None),
    )
    return jax.shard_map(
        per_device, mesh=mesh, in_specs=placed, out_specs=P(("group", "exp"), None), check_vma=False
    )
```

```python
import functools

import jax
import jax.numpy as jnp
from jax import lax
from jax.experimental import pallas as pl
from jax.experimental.pallas import tpu as pltpu
from jax.sharding import PartitionSpec as P

SLOTS = 8
CHUNKS = 4

VMEM = pl.BlockSpec(memory_space=pltpu.VMEM)
HBM = pl.BlockSpec(memory_space=pltpu.HBM)


def in_hbm(*arrays):
    return [pltpu.with_memory_space_constraint(a, pltpu.HBM) for a in arrays]


def dispatch_kernel(flight, tok_hbm, gain_hbm, ids_hbm, gw_hbm, mix_ref, *rest):
    out_ref, tok, gain, ids, gw, normed, sems = rest
    count = tok.shape[0]
    part = count // CHUNKS
    small = [
        pltpu.make_async_copy(ids_hbm, ids, sems.at[0]),
        pltpu.make_async_copy(gw_hbm, gw, sems.at[1]),
        pltpu.make_async_copy(gain_hbm, gain.at[0], sems.at[2]),
    ]
    large = [
        pltpu.make_async_copy(
            tok_hbm.at[pl.ds(i * part, part)], tok.at[pl.ds(i * part, part)], sems.at[3 + i]
        )
        for i in range(CHUNKS)
    ]
    for copy in small + large:
        copy.start()
    small[0].wait()
    small[1].wait()
    experts = lax.broadcasted_iota(jnp.int32, (flight, count), 0)
    chosen = jnp.zeros((flight, count), jnp.float32)
    gates = jnp.zeros((flight, count), jnp.float32)
    for k in range(ids.shape[0]):
        hit = ids[k : k + 1, :] == experts
        chosen = jnp.where(hit, 1.0, chosen)
        gates = jnp.where(hit, gw[k : k + 1, :], gates)
    before = (
        lax.broadcasted_iota(jnp.int32, (count, count), 0)
        < lax.broadcasted_iota(jnp.int32, (count, count), 1)
    ).astype(jnp.bfloat16)
    rank = jnp.dot(chosen.astype(jnp.bfloat16), before, preferred_element_type=jnp.float32)
    rank = jnp.where(chosen > 0.0, rank, -1.0)

    slot = lax.broadcasted_iota(jnp.int32, (flight, SLOTS, count), 1).astype(jnp.float32)
    taken = rank[:, None, :] == slot
    pick = jnp.where(taken, 1.0, 0.0).reshape(flight * SLOTS, count).astype(jnp.bfloat16)
    mix = jnp.where(taken, gates[:, None, :], 0.0).reshape(flight * SLOTS, count)
    high = mix.astype(jnp.bfloat16)
    mix_ref[: flight * SLOTS, :] = high
    mix_ref[flight * SLOTS :, :] = (mix - high.astype(jnp.float32)).astype(jnp.bfloat16)

    small[2].wait()
    for i in range(CHUNKS):
        large[i].wait()
        wide = tok[pl.ds(i * part, part), :].astype(jnp.float32)
        mean_square = jnp.mean(wide * wide, axis=1, keepdims=True)
        normed[pl.ds(i * part, part), :] = (
            wide * lax.rsqrt(mean_square + 1e-06) * gain[...]
        ).astype(jnp.bfloat16)
    out_ref[...] = jnp.dot(pick, normed[...], preferred_element_type=jnp.float32).astype(jnp.bfloat16)


def stage_kernel(gate_hbm, up_hbm, down_hbm, gate_ref, up_ref, down_ref, sems):
    copies = [
        pltpu.make_async_copy(source, target, sems.at[i])
        for i, (source, target) in enumerate(
            ((gate_hbm, gate_ref), (up_hbm, up_ref), (down_hbm, down_ref))
        )
    ]
    for copy in copies:
        copy.start()
    for copy in copies:
        copy.wait()


def expert_kernel(own_ref, other_ref, gate_ref, up_ref, down_ref, own_out, other_out):
    rows = own_ref.shape[0]
    x = jnp.concatenate([own_ref[...], other_ref[...]], axis=0)
    gate_v = jnp.dot(x, gate_ref[...], preferred_element_type=jnp.float32)
    up_v = jnp.dot(x, up_ref[...], preferred_element_type=jnp.float32)
    hidden = (gate_v / (1.0 + jnp.exp(-gate_v)) * up_v).astype(jnp.bfloat16)
    part = jnp.dot(hidden, down_ref[...], preferred_element_type=jnp.float32).astype(jnp.bfloat16)
    own_out[...] = part[:rows]
    other_out[...] = part[rows:]


def combine_kernel(mix_ref, rows_ref, out_ref):
    rows = rows_ref[...]
    both = jnp.concatenate([rows, rows], axis=0)
    out_ref[...] = lax.dot_general(
        mix_ref[...], both, (((0,), (0,)), ((), ())), preferred_element_type=jnp.float32
    ).astype(jnp.bfloat16)


def per_device(tokens, norm_gain, expert_ids, gate_weights, w_gate, w_up, w_down):
    owners = lax.axis_size("exp")
    flight = owners // 2
    count, width = tokens.shape
    hidden = w_gate.shape[2]
    packed = flight * SLOTS
    block = jax.ShapeDtypeStruct((packed, width), jnp.bfloat16)
    pairs = [(i, i ^ 1) for i in range(owners)]
    groups = [list(range(core, owners, 2)) for core in range(2)]

    def exchange(rows):
        return lax.all_to_all(
            rows, "exp", split_axis=0, concat_axis=0, axis_index_groups=groups, tiled=True
        )

    mix, outgoing = pl.pallas_call(
        functools.partial(dispatch_kernel, flight),
        out_shape=(jax.ShapeDtypeStruct((2 * packed, count), jnp.bfloat16), block),
        in_specs=[HBM] * 4,
        out_specs=(VMEM, VMEM),
        scratch_shapes=[
            pltpu.VMEM((count, width), jnp.bfloat16),
            pltpu.VMEM((1, width), jnp.float32),
            pltpu.VMEM(expert_ids.shape[::-1], jnp.int32),
            pltpu.VMEM(gate_weights.shape[::-1], jnp.float32),
            pltpu.VMEM((count, width), jnp.bfloat16),
            pltpu.SemaphoreType.DMA((3 + CHUNKS,)),
        ],
        compiler_params=pltpu.CompilerParams(vmem_limit_bytes=32 * 2**20),
        name="dispatch",
    )(*in_hbm(tokens, norm_gain, expert_ids.T, gate_weights.T))

    staged = pl.pallas_call(
        stage_kernel,
        out_shape=tuple(
            jax.ShapeDtypeStruct(w.shape[1:], w.dtype) for w in (w_gate, w_up, w_down)
        ),
        in_specs=[HBM] * 3,
        out_specs=(VMEM,) * 3,
        scratch_shapes=[pltpu.SemaphoreType.DMA((3,))],
        compiler_params=pltpu.CompilerParams(vmem_limit_bytes=16 * 2**20),
        cost_estimate=pl.CostEstimate(
            flops=0, bytes_accessed=12 * width * hidden, transcendentals=0
        ),
        name="stage",
    )(*in_hbm(w_gate[0], w_up[0], w_down[0]))

    own, staged = lax.optimization_barrier((exchange(outgoing), staged))
    other = lax.ppermute(own, "exp", pairs)
    own_part, other_part = pl.pallas_call(
        expert_kernel,
        out_shape=(block, block),
        in_specs=[VMEM] * 5,
        out_specs=(VMEM, VMEM),
        compiler_params=pltpu.CompilerParams(vmem_limit_bytes=24 * 2**20),
        cost_estimate=pl.CostEstimate(
            flops=12 * packed * width * hidden,
            bytes_accessed=6 * width * hidden,
            transcendentals=0,
        ),
        name="experts",
    )(own, other, *staged)
    from_other = lax.ppermute(other_part, "exp", pairs)
    joined = (own_part.astype(jnp.float32) + from_other.astype(jnp.float32)).astype(jnp.bfloat16)
    return pl.pallas_call(
        combine_kernel,
        out_shape=jax.ShapeDtypeStruct((count, width), jnp.bfloat16),
        in_specs=[VMEM] * 2,
        out_specs=VMEM,
        compiler_params=pltpu.CompilerParams(vmem_limit_bytes=24 * 2**20),
        name="combine",
    )(mix, exchange(joined))


def solution(mesh):
    placed = (
        P(("group", "exp"), None),
        P(),
        P(("group", "exp"), None),
        P(("group", "exp"), None),
        P("exp", None, None),
        P("exp", None, None),
        P("exp", None, None),
    )
    return jax.shard_map(
        per_device, mesh=mesh, in_specs=placed, out_specs=P(("group", "exp"), None), check_vma=False
    )
```

```python
import functools

import jax
import jax.numpy as jnp
from jax import lax
from jax.experimental import pallas as pl
from jax.experimental.pallas import tpu as pltpu
from jax.sharding import PartitionSpec as P

SLOTS = 8
CHUNKS = 4

VMEM = pl.BlockSpec(memory_space=pltpu.VMEM)
HBM = pl.BlockSpec(memory_space=pltpu.HBM)


def in_hbm(*arrays):
    return [pltpu.with_memory_space_constraint(a, pltpu.HBM) for a in arrays]


def relative(flight):
    return flight <= 8


def block_order(flight):
    far = list(range(flight // 2, flight))
    return far + list(range(1, flight // 2)) + [0]


def dispatch_kernel(
    flight, tok_hbm, gain_hbm, ids_hbm, gw_hbm, gate_hbm, mix_ref, gate_ref, *rest
):
    outs = rest[:flight]
    tok, gain, ids, gw, normed, sems = rest[flight:]
    count = tok.shape[0]
    part = count // CHUNKS
    small = [
        pltpu.make_async_copy(ids_hbm, ids, sems.at[0]),
        pltpu.make_async_copy(gw_hbm, gw, sems.at[1]),
        pltpu.make_async_copy(gain_hbm, gain.at[0], sems.at[2]),
    ]
    large = [
        pltpu.make_async_copy(
            tok_hbm.at[pl.ds(i * part, part)], tok.at[pl.ds(i * part, part)], sems.at[3 + i]
        )
        for i in range(CHUNKS)
    ]
    weights = pltpu.make_async_copy(gate_hbm, gate_ref, sems.at[3 + CHUNKS])
    for copy in small + large + [weights]:
        copy.start()
    small[0].wait()
    small[1].wait()
    chip = lax.axis_index("exp") // 2 if relative(flight) else 0
    where = lax.broadcasted_iota(jnp.int32, (flight, count), 0)
    experts = jnp.zeros((flight, count), jnp.int32)
    for i, r in enumerate(block_order(flight)):
        experts = jnp.where(where == i, r ^ chip, experts)
    chosen = jnp.zeros((flight, count), jnp.float32)
    gates = jnp.zeros((flight, count), jnp.float32)
    for k in range(ids.shape[0]):
        hit = ids[k : k + 1, :] == experts
        chosen = jnp.where(hit, 1.0, chosen)
        gates = jnp.where(hit, gw[k : k + 1, :], gates)
    before = (
        lax.broadcasted_iota(jnp.int32, (count, count), 0)
        < lax.broadcasted_iota(jnp.int32, (count, count), 1)
    ).astype(jnp.bfloat16)
    rank = jnp.dot(chosen.astype(jnp.bfloat16), before, preferred_element_type=jnp.float32)
    rank = jnp.where(chosen > 0.0, rank, -1.0)

    slot = lax.broadcasted_iota(jnp.int32, (flight, SLOTS, count), 1).astype(jnp.float32)
    taken = rank[:, None, :] == slot
    pick = jnp.where(taken, 1.0, 0.0).reshape(flight * SLOTS, count).astype(jnp.bfloat16)
    mix = jnp.where(taken, gates[:, None, :], 0.0).reshape(flight * SLOTS, count)
    high = mix.astype(jnp.bfloat16)
    mix_ref[: flight * SLOTS, :] = high
    mix_ref[flight * SLOTS :, :] = (mix - high.astype(jnp.float32)).astype(jnp.bfloat16)

    small[2].wait()
    for i in range(CHUNKS):
        large[i].wait()
        wide = tok[pl.ds(i * part, part), :].astype(jnp.float32)
        mean_square = jnp.mean(wide * wide, axis=1, keepdims=True)
        normed[pl.ds(i * part, part), :] = (
            wide * lax.rsqrt(mean_square + 1e-06) * gain[...]
        ).astype(jnp.bfloat16)
    rows = jnp.dot(pick, normed[...], preferred_element_type=jnp.float32)
    for i in range(flight):
        outs[i][...] = rows[i * SLOTS : (i + 1) * SLOTS].astype(jnp.bfloat16)
    weights.wait()


def stage_kernel(source, target, sem):
    copy = pltpu.make_async_copy(source, target, sem)
    copy.start()
    copy.wait()


def together(refs):
    return jnp.concatenate([b[...].astype(jnp.float32) for b in refs], axis=0).astype(jnp.bfloat16)


def expert_kernel(flight, *refs):
    blocks = refs[: 2 * flight]
    gate_ref, up_ref, down_hbm = refs[2 * flight : 2 * flight + 3]
    outs = refs[2 * flight + 3 : 2 * flight + 7]
    down, sem = refs[2 * flight + 7 :]
    copy = pltpu.make_async_copy(down_hbm, down, sem)
    copy.start()
    x = together(blocks)
    gate_v = jnp.dot(x, gate_ref[...], preferred_element_type=jnp.float32)
    up_v = jnp.dot(x, up_ref[...], preferred_element_type=jnp.float32)
    hidden = (gate_v / (1.0 + jnp.exp(-gate_v)) * up_v).astype(jnp.bfloat16)
    copy.wait()
    part = jnp.dot(hidden, down[...], preferred_element_type=jnp.float32).astype(jnp.bfloat16)
    rows = outs[0].shape[0]
    for i, out in enumerate(outs):
        out[...] = part[i * rows : (i + 1) * rows]


def join_kernel(mine_ref, got_ref, *outs):
    joined = mine_ref[...].astype(jnp.float32) + got_ref[...].astype(jnp.float32)
    for i, out in enumerate(outs):
        out[...] = joined[i * SLOTS : (i + 1) * SLOTS].astype(jnp.bfloat16)


def combine_kernel(flight, mix_ref, *refs):
    rows = together(refs[:flight])
    both = jnp.concatenate([rows, rows], axis=0)
    refs[flight][...] = lax.dot_general(
        mix_ref[...], both, (((0,), (0,)), ((), ())), preferred_element_type=jnp.float32
    ).astype(jnp.bfloat16)


def per_device(tokens, norm_gain, expert_ids, gate_weights, w_gate, w_up, w_down):
    owners = lax.axis_size("exp")
    flight = owners // 2
    count, width = tokens.shape
    hidden = w_gate.shape[2]
    packed = flight * SLOTS
    order = block_order(flight)
    block = jax.ShapeDtypeStruct((SLOTS, width), jnp.bfloat16)
    half = jax.ShapeDtypeStruct((packed // 2, width), jnp.bfloat16)
    pairs = [(i, i ^ 1) for i in range(owners)]
    few = relative(flight)

    def exchange(blocks):
        if few:
            return [
                lax.ppermute(b, "exp", [(i, i ^ (2 * r)) for i in range(owners)]) if r else b
                for b, r in zip(blocks, order)
            ]
        groups = [list(range(core, owners, 2)) for core in range(2)]
        stacked = jnp.stack([blocks[order.index(r)] for r in range(flight)])
        got = lax.all_to_all(
            stacked, "exp", split_axis=0, concat_axis=0, axis_index_groups=groups, tiled=True
        )
        return [got[r] for r in order]

    def swap(blocks):
        if few:
            return [lax.ppermute(b, "exp", pairs) for b in blocks]
        got = lax.ppermute(jnp.stack(blocks), "exp", pairs)
        return [got[r] for r in range(flight)]

    mix, gate, *outgoing = pl.pallas_call(
        functools.partial(dispatch_kernel, flight),
        out_shape=(
            jax.ShapeDtypeStruct((2 * packed, count), jnp.bfloat16),
            jax.ShapeDtypeStruct(w_gate.shape[1:], w_gate.dtype),
        )
        + (block,) * flight,
        in_specs=[HBM] * 5,
        out_specs=(VMEM,) * (flight + 2),
        scratch_shapes=[
            pltpu.VMEM((count, width), jnp.bfloat16),
            pltpu.VMEM((1, width), jnp.float32),
            pltpu.VMEM(expert_ids.shape[::-1], jnp.int32),
            pltpu.VMEM(gate_weights.shape[::-1], jnp.float32),
            pltpu.VMEM((count, width), jnp.bfloat16),
            pltpu.SemaphoreType.DMA((4 + CHUNKS,)),
        ],
        compiler_params=pltpu.CompilerParams(vmem_limit_bytes=24 * 2**20),
        name="dispatch",
    )(*in_hbm(tokens, norm_gain, expert_ids.T, gate_weights.T, w_gate[0]))

    up = pl.pallas_call(
        stage_kernel,
        out_shape=jax.ShapeDtypeStruct(w_up.shape[1:], w_up.dtype),
        in_specs=[HBM],
        out_specs=VMEM,
        scratch_shapes=[pltpu.SemaphoreType.DMA],
        compiler_params=pltpu.CompilerParams(vmem_limit_bytes=16 * 2**20),
        cost_estimate=pl.CostEstimate(flops=0, bytes_accessed=4 * width * hidden, transcendentals=0),
        name="stage",
    )(*in_hbm(w_up[0]))

    own = exchange(outgoing)
    last = flight // 2 - 1
    own[last], up = lax.optimization_barrier((own[last], up))
    other = swap(own)
    own_far, own_near, other_far, other_near = pl.pallas_call(
        functools.partial(expert_kernel, flight),
        out_shape=(half,) * 4,
        in_specs=[VMEM] * (2 * flight + 2) + [HBM],
        out_specs=(VMEM,) * 4,
        scratch_shapes=[pltpu.VMEM(w_down.shape[1:], w_down.dtype), pltpu.SemaphoreType.DMA],
        compiler_params=pltpu.CompilerParams(vmem_limit_bytes=32 * 2**20),
        cost_estimate=pl.CostEstimate(
            flops=12 * packed * width * hidden,
            bytes_accessed=6 * width * hidden,
            transcendentals=0,
        ),
        name="experts",
    )(*own, *other, gate, up, *in_hbm(w_down[0]))

    def join(mine, theirs):
        return pl.pallas_call(
            join_kernel,
            out_shape=(block,) * (flight // 2),
            in_specs=[VMEM] * 2,
            out_specs=(VMEM,) * (flight // 2),
            compiler_params=pltpu.CompilerParams(vmem_limit_bytes=24 * 2**20),
            name="join",
        )(mine, lax.ppermute(theirs, "exp", pairs))

    returned = exchange([*join(own_far, other_far), *join(own_near, other_near)])
    return pl.pallas_call(
        functools.partial(combine_kernel, flight),
        out_shape=jax.ShapeDtypeStruct((count, width), jnp.bfloat16),
        in_specs=[VMEM] * (flight + 1),
        out_specs=VMEM,
        compiler_params=pltpu.CompilerParams(vmem_limit_bytes=24 * 2**20),
        name="combine",
    )(mix, *returned)


def solution(mesh):
    placed = (
        P(("group", "exp"), None),
        P(),
        P(("group", "exp"), None),
        P(("group", "exp"), None),
        P("exp", None, None),
        P("exp", None, None),
        P("exp", None, None),
    )
    return jax.shard_map(
        per_device, mesh=mesh, in_specs=placed, out_specs=P(("group", "exp"), None), check_vma=False
    )
```

```python
import functools

import jax
import jax.numpy as jnp
from jax import lax
from jax.experimental import pallas as pl
from jax.experimental.pallas import tpu as pltpu
from jax.sharding import PartitionSpec as P

SLOTS = 8
CHUNKS = 4
PIECES = 4

VMEM = pl.BlockSpec(memory_space=pltpu.VMEM)
HBM = pl.BlockSpec(memory_space=pltpu.HBM)


def in_hbm(*arrays):
    return [pltpu.with_memory_space_constraint(a, pltpu.HBM) for a in arrays]


def relative(flight):
    return flight <= 8


def block_order(flight):
    far = list(range(flight // 2, flight))
    return far[:1] + list(range(1, flight // 2)) + far[1:] + [0]


def group(items, flight, far):
    return [x for x, r in zip(items, block_order(flight)) if (r >= flight // 2) == far]


def dispatch_kernel(
    flight, tok_hbm, gain_hbm, ids_hbm, gw_hbm, gate_hbm, mix_ref, gate_ref, *rest
):
    outs = rest[:flight]
    tok, gain, ids, gw, normed, sems = rest[flight:]
    count = tok.shape[0]
    part = count // CHUNKS
    small = [
        pltpu.make_async_copy(ids_hbm, ids, sems.at[0]),
        pltpu.make_async_copy(gw_hbm, gw, sems.at[1]),
        pltpu.make_async_copy(gain_hbm, gain.at[0], sems.at[2]),
    ]
    large = [
        pltpu.make_async_copy(
            tok_hbm.at[pl.ds(i * part, part)], tok.at[pl.ds(i * part, part)], sems.at[3 + i]
        )
        for i in range(CHUNKS)
    ]
    weights = pltpu.make_async_copy(gate_hbm, gate_ref, sems.at[3 + CHUNKS])
    for copy in small + large + [weights]:
        copy.start()
    small[0].wait()
    small[1].wait()
    chip = lax.axis_index("exp") // 2 if relative(flight) else 0
    where = lax.broadcasted_iota(jnp.int32, (flight, count), 0)
    experts = jnp.zeros((flight, count), jnp.int32)
    for i, r in enumerate(block_order(flight)):
        experts = jnp.where(where == i, r ^ chip, experts)
    chosen = jnp.zeros((flight, count), jnp.float32)
    gates = jnp.zeros((flight, count), jnp.float32)
    for k in range(ids.shape[0]):
        hit = ids[k : k + 1, :] == experts
        chosen = jnp.where(hit, 1.0, chosen)
        gates = jnp.where(hit, gw[k : k + 1, :], gates)
    before = (
        lax.broadcasted_iota(jnp.int32, (count, count), 0)
        < lax.broadcasted_iota(jnp.int32, (count, count), 1)
    ).astype(jnp.bfloat16)
    rank = jnp.dot(chosen.astype(jnp.bfloat16), before, preferred_element_type=jnp.float32)
    rank = jnp.where(chosen > 0.0, rank, -1.0)

    slot = lax.broadcasted_iota(jnp.int32, (flight, SLOTS, count), 1).astype(jnp.float32)
    taken = rank[:, None, :] == slot
    pick = jnp.where(taken, 1.0, 0.0).reshape(flight * SLOTS, count).astype(jnp.bfloat16)
    mix = jnp.where(taken, gates[:, None, :], 0.0).reshape(flight * SLOTS, count)
    high = mix.astype(jnp.bfloat16)
    mix_ref[: flight * SLOTS, :] = high
    mix_ref[flight * SLOTS :, :] = (mix - high.astype(jnp.float32)).astype(jnp.bfloat16)

    small[2].wait()
    for i in range(CHUNKS):
        large[i].wait()
        wide = tok[pl.ds(i * part, part), :].astype(jnp.float32)
        mean_square = jnp.mean(wide * wide, axis=1, keepdims=True)
        normed[pl.ds(i * part, part), :] = (
            wide * lax.rsqrt(mean_square + 1e-06) * gain[...]
        ).astype(jnp.bfloat16)
    rows = jnp.dot(pick, normed[...], preferred_element_type=jnp.float32)
    for i in range(flight):
        outs[i][...] = rows[i * SLOTS : (i + 1) * SLOTS].astype(jnp.bfloat16)
    weights.wait()


def stage_kernel(source, target, sems):
    rows = source.shape[0] // PIECES
    copies = [
        pltpu.make_async_copy(
            source.at[pl.ds(i * rows, rows)], target.at[pl.ds(i * rows, rows)], sems.at[i]
        )
        for i in range(PIECES)
    ]
    for copy in copies:
        copy.start()
    for copy in copies:
        copy.wait()


def together(refs):
    return jnp.concatenate([b[...].astype(jnp.float32) for b in refs], axis=0).astype(jnp.bfloat16)


def gather_kernel(*refs):
    refs[-1][...] = together(refs[:-1])


def expert_kernel(own_ref, other_ref, gate_ref, up_ref, down_ref, own_out, other_out):
    rows = own_ref.shape[0]
    x = jnp.concatenate([own_ref[...], other_ref[...]], axis=0)
    gate_v = jnp.dot(x, gate_ref[...], preferred_element_type=jnp.float32)
    up_v = jnp.dot(x, up_ref[...], preferred_element_type=jnp.float32)
    hidden = (gate_v / (1.0 + jnp.exp(-gate_v)) * up_v).astype(jnp.bfloat16)
    part = jnp.dot(hidden, down_ref[...], preferred_element_type=jnp.float32).astype(jnp.bfloat16)
    own_out[...] = part[:rows]
    other_out[...] = part[rows:]


def join_kernel(mine_ref, got_ref, *outs):
    joined = mine_ref[...].astype(jnp.float32) + got_ref[...].astype(jnp.float32)
    for i, out in enumerate(outs):
        out[...] = joined[i * SLOTS : (i + 1) * SLOTS].astype(jnp.bfloat16)


def combine_kernel(flight, mix_ref, *refs):
    rows = together(refs[:flight])
    both = jnp.concatenate([rows, rows], axis=0)
    refs[flight][...] = lax.dot_general(
        mix_ref[...], both, (((0,), (0,)), ((), ())), preferred_element_type=jnp.float32
    ).astype(jnp.bfloat16)


def per_device(tokens, norm_gain, expert_ids, gate_weights, w_gate, w_up, w_down):
    owners = lax.axis_size("exp")
    flight = owners // 2
    count, width = tokens.shape
    hidden = w_gate.shape[2]
    packed = flight * SLOTS
    order = block_order(flight)
    block = jax.ShapeDtypeStruct((SLOTS, width), jnp.bfloat16)
    half = jax.ShapeDtypeStruct((packed // 2, width), jnp.bfloat16)
    few = relative(flight)

    def exchange(blocks):
        if few:
            return [
                lax.ppermute(b, "exp", [(i, i ^ (2 * r)) for i in range(owners)]) if r else b
                for b, r in zip(blocks, order)
            ]
        groups = [list(range(core, owners, 2)) for core in range(2)]
        stacked = jnp.stack([blocks[order.index(r)] for r in range(flight)])
        got = lax.all_to_all(
            stacked, "exp", split_axis=0, concat_axis=0, axis_index_groups=groups, tiled=True
        )
        return [got[r] for r in order]

    def swap(rows):
        return lax.ppermute(rows, "exp", [(i, i ^ 1) for i in range(owners)])

    def stage(weights):
        return pl.pallas_call(
            stage_kernel,
            out_shape=jax.ShapeDtypeStruct(weights.shape, weights.dtype),
            in_specs=[HBM],
            out_specs=VMEM,
            scratch_shapes=[pltpu.SemaphoreType.DMA((PIECES,))],
            compiler_params=pltpu.CompilerParams(vmem_limit_bytes=16 * 2**20),
            cost_estimate=pl.CostEstimate(
                flops=0, bytes_accessed=4 * width * hidden, transcendentals=0
            ),
            name="stage",
        )(*in_hbm(weights))

    def gather(blocks):
        return pl.pallas_call(
            gather_kernel,
            out_shape=half,
            in_specs=[VMEM] * (flight // 2),
            out_specs=VMEM,
            compiler_params=pltpu.CompilerParams(vmem_limit_bytes=16 * 2**20),
            name="gather",
        )(*blocks)

    def experts(own, other, weights):
        return pl.pallas_call(
            expert_kernel,
            out_shape=(half, half),
            in_specs=[VMEM] * 5,
            out_specs=(VMEM, VMEM),
            compiler_params=pltpu.CompilerParams(vmem_limit_bytes=24 * 2**20),
            cost_estimate=pl.CostEstimate(
                flops=6 * packed * width * hidden,
                bytes_accessed=6 * width * hidden,
                transcendentals=0,
            ),
            name="experts",
        )(own, other, *weights)

    def join(mine, theirs):
        return pl.pallas_call(
            join_kernel,
            out_shape=(block,) * (flight // 2),
            in_specs=[VMEM] * 2,
            out_specs=(VMEM,) * (flight // 2),
            compiler_params=pltpu.CompilerParams(vmem_limit_bytes=16 * 2**20),
            name="join",
        )(mine, swap(theirs))

    mix, gate, *outgoing = pl.pallas_call(
        functools.partial(dispatch_kernel, flight),
        out_shape=(
            jax.ShapeDtypeStruct((2 * packed, count), jnp.bfloat16),
            jax.ShapeDtypeStruct(w_gate.shape[1:], w_gate.dtype),
        )
        + (block,) * flight,
        in_specs=[HBM] * 5,
        out_specs=(VMEM,) * (flight + 2),
        scratch_shapes=[
            pltpu.VMEM((count, width), jnp.bfloat16),
            pltpu.VMEM((1, width), jnp.float32),
            pltpu.VMEM(expert_ids.shape[::-1], jnp.int32),
            pltpu.VMEM(gate_weights.shape[::-1], jnp.float32),
            pltpu.VMEM((count, width), jnp.bfloat16),
            pltpu.SemaphoreType.DMA((4 + CHUNKS,)),
        ],
        compiler_params=pltpu.CompilerParams(vmem_limit_bytes=24 * 2**20),
        name="dispatch",
    )(*in_hbm(tokens, norm_gain, expert_ids.T, gate_weights.T, w_gate[0]))

    up, down = stage(w_up[0]), stage(w_down[0])
    arrived = exchange(outgoing)
    *held, up, down = lax.optimization_barrier((*arrived[:-2], up, down))
    arrived = held + arrived[-2:]
    weights = (gate, up, down)

    near_own = gather(group(arrived, flight, False))
    near_other = swap(near_own)
    far_own = gather(group(arrived, flight, True))
    far_own, near_own, near_other = lax.optimization_barrier((far_own, near_own, near_other))
    far_other = swap(far_own)
    near_mine, near_theirs = experts(near_own, near_other, weights)
    far_mine, far_theirs = experts(far_own, far_other, weights)
    far_rows = iter(join(far_mine, far_theirs))
    near_rows = iter(join(near_mine, near_theirs))
    returned = exchange([next(far_rows if r >= flight // 2 else near_rows) for r in order])
    return pl.pallas_call(
        functools.partial(combine_kernel, flight),
        out_shape=jax.ShapeDtypeStruct((count, width), jnp.bfloat16),
        in_specs=[VMEM] * (flight + 1),
        out_specs=VMEM,
        compiler_params=pltpu.CompilerParams(vmem_limit_bytes=24 * 2**20),
        name="combine",
    )(mix, *returned)


def solution(mesh):
    placed = (
        P(("group", "exp"), None),
        P(),
        P(("group", "exp"), None),
        P(("group", "exp"), None),
        P("exp", None, None),
        P("exp", None, None),
        P("exp", None, None),
    )
    return jax.shard_map(
        per_device, mesh=mesh, in_specs=placed, out_specs=P(("group", "exp"), None), check_vma=False
    )
```

```python
import functools

import jax
import jax.numpy as jnp
from jax import lax
from jax.experimental import pallas as pl
from jax.experimental.pallas import tpu as pltpu
from jax.sharding import PartitionSpec as P

SLOTS = 8
CHUNKS = 4
PIECES = 4

VMEM = pl.BlockSpec(memory_space=pltpu.VMEM)
HBM = pl.BlockSpec(memory_space=pltpu.HBM)


def in_hbm(*arrays):
    return [pltpu.with_memory_space_constraint(a, pltpu.HBM) for a in arrays]


def relative(flight):
    return flight <= 8


def block_order(flight):
    far = range(flight // 2, flight)
    near = range(1, flight // 2)
    mixed = [r for pair in zip(far, near) for r in pair]
    return mixed + [flight - 1, 0]


def dispatch_kernel(
    flight, tok_hbm, gain_hbm, ids_hbm, gw_hbm, gate_hbm, mix_ref, gate_ref, *rest
):
    outs = rest[:flight]
    tok, gain, ids, gw, normed, sems = rest[flight:]
    count = tok.shape[0]
    part = count // CHUNKS
    small = [
        pltpu.make_async_copy(ids_hbm, ids, sems.at[0]),
        pltpu.make_async_copy(gw_hbm, gw, sems.at[1]),
        pltpu.make_async_copy(gain_hbm, gain.at[0], sems.at[2]),
    ]
    large = [
        pltpu.make_async_copy(
            tok_hbm.at[pl.ds(i * part, part)], tok.at[pl.ds(i * part, part)], sems.at[3 + i]
        )
        for i in range(CHUNKS)
    ]
    weights = pltpu.make_async_copy(gate_hbm, gate_ref, sems.at[3 + CHUNKS])
    for copy in small + large + [weights]:
        copy.start()
    small[0].wait()
    small[1].wait()
    chip = lax.axis_index("exp") // 2 if relative(flight) else 0
    where = lax.broadcasted_iota(jnp.int32, (flight, count), 0)
    experts = jnp.zeros((flight, count), jnp.int32)
    for i, r in enumerate(block_order(flight)):
        experts = jnp.where(where == i, r ^ chip, experts)
    chosen = jnp.zeros((flight, count), jnp.float32)
    gates = jnp.zeros((flight, count), jnp.float32)
    for k in range(ids.shape[0]):
        hit = ids[k : k + 1, :] == experts
        chosen = jnp.where(hit, 1.0, chosen)
        gates = jnp.where(hit, gw[k : k + 1, :], gates)
    before = (
        lax.broadcasted_iota(jnp.int32, (count, count), 0)
        < lax.broadcasted_iota(jnp.int32, (count, count), 1)
    ).astype(jnp.bfloat16)
    rank = jnp.dot(chosen.astype(jnp.bfloat16), before, preferred_element_type=jnp.float32)
    rank = jnp.where(chosen > 0.0, rank, -1.0)

    slot = lax.broadcasted_iota(jnp.int32, (flight, SLOTS, count), 1).astype(jnp.float32)
    taken = rank[:, None, :] == slot
    pick = jnp.where(taken, 1.0, 0.0).reshape(flight * SLOTS, count).astype(jnp.bfloat16)
    mix = jnp.where(taken, gates[:, None, :], 0.0).reshape(flight * SLOTS, count)
    high = mix.astype(jnp.bfloat16)
    mix_ref[: flight * SLOTS, :] = high
    mix_ref[flight * SLOTS :, :] = (mix - high.astype(jnp.float32)).astype(jnp.bfloat16)

    small[2].wait()
    for i in range(CHUNKS):
        large[i].wait()
        wide = tok[pl.ds(i * part, part), :].astype(jnp.float32)
        mean_square = jnp.mean(wide * wide, axis=1, keepdims=True)
        normed[pl.ds(i * part, part), :] = (
            wide * lax.rsqrt(mean_square + 1e-06) * gain[...]
        ).astype(jnp.bfloat16)
    rows = jnp.dot(pick, normed[...], preferred_element_type=jnp.float32)
    for i in range(flight):
        outs[i][...] = rows[i * SLOTS : (i + 1) * SLOTS].astype(jnp.bfloat16)
    weights.wait()


def stage_kernel(source, target, sems):
    rows = source.shape[0] // PIECES
    copies = [
        pltpu.make_async_copy(
            source.at[pl.ds(i * rows, rows)], target.at[pl.ds(i * rows, rows)], sems.at[i]
        )
        for i in range(PIECES)
    ]
    for copy in copies:
        copy.start()
    for copy in copies:
        copy.wait()


def together(refs):
    return jnp.concatenate([b[...].astype(jnp.float32) for b in refs], axis=0).astype(jnp.bfloat16)


def gather_kernel(*refs):
    refs[-1][...] = together(refs[:-1])


def expert_kernel(own_ref, other_ref, gate_ref, up_ref, down_ref, own_out, other_out):
    rows = own_ref.shape[0]
    x = jnp.concatenate([own_ref[...], other_ref[...]], axis=0)
    gate_v = jnp.dot(x, gate_ref[...], preferred_element_type=jnp.float32)
    up_v = jnp.dot(x, up_ref[...], preferred_element_type=jnp.float32)
    hidden = (gate_v / (1.0 + jnp.exp(-gate_v)) * up_v).astype(jnp.bfloat16)
    part = jnp.dot(hidden, down_ref[...], preferred_element_type=jnp.float32).astype(jnp.bfloat16)
    own_out[...] = part[:rows]
    other_out[...] = part[rows:]


def join_kernel(mine_ref, got_ref, *outs):
    joined = mine_ref[...].astype(jnp.float32) + got_ref[...].astype(jnp.float32)
    for i, out in enumerate(outs):
        out[...] = joined[i * SLOTS : (i + 1) * SLOTS].astype(jnp.bfloat16)


def combine_kernel(flight, mix_ref, *refs):
    rows = together(refs[:flight])
    both = jnp.concatenate([rows, rows], axis=0)
    refs[flight][...] = lax.dot_general(
        mix_ref[...], both, (((0,), (0,)), ((), ())), preferred_element_type=jnp.float32
    ).astype(jnp.bfloat16)


def per_device(tokens, norm_gain, expert_ids, gate_weights, w_gate, w_up, w_down):
    owners = lax.axis_size("exp")
    flight = owners // 2
    count, width = tokens.shape
    hidden = w_gate.shape[2]
    packed = flight * SLOTS
    order = block_order(flight)
    block = jax.ShapeDtypeStruct((SLOTS, width), jnp.bfloat16)
    whole = jax.ShapeDtypeStruct((packed, width), jnp.bfloat16)
    few = relative(flight)

    def exchange(blocks):
        if few:
            return [
                lax.ppermute(b, "exp", [(i, i ^ (2 * r)) for i in range(owners)]) if r else b
                for b, r in zip(blocks, order)
            ]
        groups = [list(range(core, owners, 2)) for core in range(2)]
        stacked = jnp.stack([blocks[order.index(r)] for r in range(flight)])
        got = lax.all_to_all(
            stacked, "exp", split_axis=0, concat_axis=0, axis_index_groups=groups, tiled=True
        )
        return [got[r] for r in order]

    def swap(rows):
        return lax.ppermute(rows, "exp", [(i, i ^ 1) for i in range(owners)])

    def stage(weights):
        return pl.pallas_call(
            stage_kernel,
            out_shape=jax.ShapeDtypeStruct(weights.shape, weights.dtype),
            in_specs=[HBM],
            out_specs=VMEM,
            scratch_shapes=[pltpu.SemaphoreType.DMA((PIECES,))],
            compiler_params=pltpu.CompilerParams(vmem_limit_bytes=16 * 2**20),
            cost_estimate=pl.CostEstimate(
                flops=0, bytes_accessed=4 * width * hidden, transcendentals=0
            ),
            name="stage",
        )(*in_hbm(weights))

    mix, gate, *outgoing = pl.pallas_call(
        functools.partial(dispatch_kernel, flight),
        out_shape=(
            jax.ShapeDtypeStruct((2 * packed, count), jnp.bfloat16),
            jax.ShapeDtypeStruct(w_gate.shape[1:], w_gate.dtype),
        )
        + (block,) * flight,
        in_specs=[HBM] * 5,
        out_specs=(VMEM,) * (flight + 2),
        scratch_shapes=[
            pltpu.VMEM((count, width), jnp.bfloat16),
            pltpu.VMEM((1, width), jnp.float32),
            pltpu.VMEM(expert_ids.shape[::-1], jnp.int32),
            pltpu.VMEM(gate_weights.shape[::-1], jnp.float32),
            pltpu.VMEM((count, width), jnp.bfloat16),
            pltpu.SemaphoreType.DMA((4 + CHUNKS,)),
        ],
        compiler_params=pltpu.CompilerParams(vmem_limit_bytes=24 * 2**20),
        name="dispatch",
    )(*in_hbm(tokens, norm_gain, expert_ids.T, gate_weights.T, w_gate[0]))

    up, down = stage(w_up[0]), stage(w_down[0])
    *arrived, up = lax.optimization_barrier((*exchange(outgoing), up))
    own = pl.pallas_call(
        gather_kernel,
        out_shape=whole,
        in_specs=[VMEM] * flight,
        out_specs=VMEM,
        compiler_params=pltpu.CompilerParams(vmem_limit_bytes=16 * 2**20),
        name="gather",
    )(*arrived)
    mine, theirs = pl.pallas_call(
        expert_kernel,
        out_shape=(whole, whole),
        in_specs=[VMEM] * 5,
        out_specs=(VMEM, VMEM),
        compiler_params=pltpu.CompilerParams(vmem_limit_bytes=24 * 2**20),
        cost_estimate=pl.CostEstimate(
            flops=12 * packed * width * hidden,
            bytes_accessed=6 * width * hidden,
            transcendentals=0,
        ),
        name="experts",
    )(own, swap(own), gate, up, down)
    joined = pl.pallas_call(
        join_kernel,
        out_shape=(block,) * flight,
        in_specs=[VMEM] * 2,
        out_specs=(VMEM,) * flight,
        compiler_params=pltpu.CompilerParams(vmem_limit_bytes=16 * 2**20),
        name="join",
    )(mine, swap(theirs))
    returned = exchange(joined)
    return pl.pallas_call(
        functools.partial(combine_kernel, flight),
        out_shape=jax.ShapeDtypeStruct((count, width), jnp.bfloat16),
        in_specs=[VMEM] * (flight + 1),
        out_specs=VMEM,
        compiler_params=pltpu.CompilerParams(vmem_limit_bytes=24 * 2**20),
        name="combine",
    )(mix, *returned)


def solution(mesh):
    placed = (
        P(("group", "exp"), None),
        P(),
        P(("group", "exp"), None),
        P(("group", "exp"), None),
        P("exp", None, None),
        P("exp", None, None),
        P("exp", None, None),
    )
    return jax.shard_map(
        per_device, mesh=mesh, in_specs=placed, out_specs=P(("group", "exp"), None), check_vma=False
    )
```

```python
import functools

import jax
import jax.numpy as jnp
from jax import lax
from jax.experimental import pallas as pl
from jax.experimental.pallas import tpu as pltpu
from jax.sharding import PartitionSpec as P

SLOTS = 8
CHUNKS = 4
PIECES = 4

VMEM = pl.BlockSpec(memory_space=pltpu.VMEM)
HBM = pl.BlockSpec(memory_space=pltpu.HBM)


def in_hbm(*arrays):
    return [pltpu.with_memory_space_constraint(a, pltpu.HBM) for a in arrays]


def relative(flight):
    return flight <= 8


def block_order(flight, core):
    if not relative(flight):
        return list(range(flight))
    far = list(range(flight // 2, flight))
    near = list(range(1, flight // 2))
    turns = zip(far, near) if core == 0 else zip(near, far)
    return [r for pair in turns for r in pair] + [flight - 1, 0]


def dispatch_kernel(
    flight, tok_hbm, gain_hbm, ids_hbm, gw_hbm, gate_hbm, mix_ref, gate_ref, *rest
):
    outs = rest[:flight]
    tok, gain, ids, gw, normed, sems = rest[flight:]
    count = tok.shape[0]
    part = count // CHUNKS
    small = [
        pltpu.make_async_copy(ids_hbm, ids, sems.at[0]),
        pltpu.make_async_copy(gw_hbm, gw, sems.at[1]),
        pltpu.make_async_copy(gain_hbm, gain.at[0], sems.at[2]),
    ]
    large = [
        pltpu.make_async_copy(
            tok_hbm.at[pl.ds(i * part, part)], tok.at[pl.ds(i * part, part)], sems.at[3 + i]
        )
        for i in range(CHUNKS)
    ]
    weights = pltpu.make_async_copy(gate_hbm, gate_ref, sems.at[3 + CHUNKS])
    for copy in small + large + [weights]:
        copy.start()
    small[0].wait()
    small[1].wait()
    experts = lax.broadcasted_iota(jnp.int32, (flight, count), 0)
    if relative(flight):
        place = experts
        me = lax.axis_index("exp")
        for i, (even, odd) in enumerate(zip(block_order(flight, 0), block_order(flight, 1))):
            experts = jnp.where(place == i, jnp.where(me % 2 == 0, even, odd) ^ (me // 2), experts)
    chosen = jnp.zeros((flight, count), jnp.float32)
    gates = jnp.zeros((flight, count), jnp.float32)
    for k in range(ids.shape[0]):
        hit = ids[k : k + 1, :] == experts
        chosen = jnp.where(hit, 1.0, chosen)
        gates = jnp.where(hit, gw[k : k + 1, :], gates)
    before = (
        lax.broadcasted_iota(jnp.int32, (count, count), 0)
        < lax.broadcasted_iota(jnp.int32, (count, count), 1)
    ).astype(jnp.bfloat16)
    rank = jnp.dot(chosen.astype(jnp.bfloat16), before, preferred_element_type=jnp.float32)
    rank = jnp.where(chosen > 0.0, rank, -1.0)

    slot = lax.broadcasted_iota(jnp.int32, (flight, SLOTS, count), 1).astype(jnp.float32)
    taken = rank[:, None, :] == slot
    pick = jnp.where(taken, 1.0, 0.0).reshape(flight * SLOTS, count).astype(jnp.bfloat16)
    mix = jnp.where(taken, gates[:, None, :], 0.0).reshape(flight * SLOTS, count)
    high = mix.astype(jnp.bfloat16)
    mix_ref[: flight * SLOTS, :] = high
    mix_ref[flight * SLOTS :, :] = (mix - high.astype(jnp.float32)).astype(jnp.bfloat16)

    small[2].wait()
    for i in range(CHUNKS):
        large[i].wait()
        wide = tok[pl.ds(i * part, part), :].astype(jnp.float32)
        mean_square = jnp.mean(wide * wide, axis=1, keepdims=True)
        normed[pl.ds(i * part, part), :] = (
            wide * lax.rsqrt(mean_square + 1e-06) * gain[...]
        ).astype(jnp.bfloat16)
    rows = jnp.dot(pick, normed[...], preferred_element_type=jnp.float32)
    for i in range(flight):
        outs[i][...] = rows[i * SLOTS : (i + 1) * SLOTS].astype(jnp.bfloat16)
    weights.wait()


def stage_kernel(source, target, sems):
    rows = source.shape[0] // PIECES
    copies = [
        pltpu.make_async_copy(
            source.at[pl.ds(i * rows, rows)], target.at[pl.ds(i * rows, rows)], sems.at[i]
        )
        for i in range(PIECES)
    ]
    for copy in copies:
        copy.start()
    for copy in copies:
        copy.wait()


def together(refs):
    return jnp.concatenate([b[...].astype(jnp.float32) for b in refs], axis=0).astype(jnp.bfloat16)


def gather_kernel(*refs):
    refs[-1][...] = together(refs[:-1])


def expert_kernel(own_ref, other_ref, gate_ref, up_ref, down_ref, own_out, other_out):
    rows = own_ref.shape[0]
    x = jnp.concatenate([own_ref[...], other_ref[...]], axis=0)
    gate_v = jnp.dot(x, gate_ref[...], preferred_element_type=jnp.float32)
    up_v = jnp.dot(x, up_ref[...], preferred_element_type=jnp.float32)
    hidden = (gate_v / (1.0 + jnp.exp(-gate_v)) * up_v).astype(jnp.bfloat16)
    part = jnp.dot(hidden, down_ref[...], preferred_element_type=jnp.float32).astype(jnp.bfloat16)
    own_out[...] = part[:rows]
    other_out[...] = part[rows:]


def join_kernel(mine_ref, got_ref, *outs):
    joined = mine_ref[...].astype(jnp.float32) + got_ref[...].astype(jnp.float32)
    for i, out in enumerate(outs):
        out[...] = joined[i * SLOTS : (i + 1) * SLOTS].astype(jnp.bfloat16)


def combine_kernel(flight, mix_ref, *refs):
    rows = together(refs[:flight])
    both = jnp.concatenate([rows, rows], axis=0)
    refs[flight][...] = lax.dot_general(
        mix_ref[...], both, (((0,), (0,)), ((), ())), preferred_element_type=jnp.float32
    ).astype(jnp.bfloat16)


def per_device(tokens, norm_gain, expert_ids, gate_weights, w_gate, w_up, w_down):
    owners = lax.axis_size("exp")
    flight = owners // 2
    count, width = tokens.shape
    hidden = w_gate.shape[2]
    packed = flight * SLOTS
    block = jax.ShapeDtypeStruct((SLOTS, width), jnp.bfloat16)
    whole = jax.ShapeDtypeStruct((packed, width), jnp.bfloat16)
    few = relative(flight)

    def exchange(blocks):
        if few:
            orders = block_order(flight, 0), block_order(flight, 1)
            got = [
                lax.ppermute(
                    blocks[i], "exp", [(n, n ^ (2 * orders[n % 2][i])) for n in range(owners)]
                )
                for i in range(flight - 1)
            ]
            return got + [blocks[-1]]
        groups = [list(range(core, owners, 2)) for core in range(2)]
        got = lax.all_to_all(
            jnp.stack(blocks), "exp", split_axis=0, concat_axis=0, axis_index_groups=groups, tiled=True
        )
        return [got[i] for i in range(flight)]

    def swap(rows):
        return lax.ppermute(rows, "exp", [(i, i ^ 1) for i in range(owners)])

    def stage(weights):
        return pl.pallas_call(
            stage_kernel,
            out_shape=jax.ShapeDtypeStruct(weights.shape, weights.dtype),
            in_specs=[HBM],
            out_specs=VMEM,
            scratch_shapes=[pltpu.SemaphoreType.DMA((PIECES,))],
            compiler_params=pltpu.CompilerParams(vmem_limit_bytes=16 * 2**20),
            cost_estimate=pl.CostEstimate(
                flops=0, bytes_accessed=4 * width * hidden, transcendentals=0
            ),
            name="stage",
        )(*in_hbm(weights))

    mix, gate, *outgoing = pl.pallas_call(
        functools.partial(dispatch_kernel, flight),
        out_shape=(
            jax.ShapeDtypeStruct((2 * packed, count), jnp.bfloat16),
            jax.ShapeDtypeStruct(w_gate.shape[1:], w_gate.dtype),
        )
        + (block,) * flight,
        in_specs=[HBM] * 5,
        out_specs=(VMEM,) * (flight + 2),
        scratch_shapes=[
            pltpu.VMEM((count, width), jnp.bfloat16),
            pltpu.VMEM((1, width), jnp.float32),
            pltpu.VMEM(expert_ids.shape[::-1], jnp.int32),
            pltpu.VMEM(gate_weights.shape[::-1], jnp.float32),
            pltpu.VMEM((count, width), jnp.bfloat16),
            pltpu.SemaphoreType.DMA((4 + CHUNKS,)),
        ],
        compiler_params=pltpu.CompilerParams(vmem_limit_bytes=24 * 2**20),
        name="dispatch",
    )(*in_hbm(tokens, norm_gain, expert_ids.T, gate_weights.T, w_gate[0]))

    up, down = stage(w_up[0]), stage(w_down[0])
    *arrived, up = lax.optimization_barrier((*exchange(outgoing), up))
    own = pl.pallas_call(
        gather_kernel,
        out_shape=whole,
        in_specs=[VMEM] * flight,
        out_specs=VMEM,
        compiler_params=pltpu.CompilerParams(vmem_limit_bytes=16 * 2**20),
        name="gather",
    )(*arrived)
    mine, theirs = pl.pallas_call(
        expert_kernel,
        out_shape=(whole, whole),
        in_specs=[VMEM] * 5,
        out_specs=(VMEM, VMEM),
        compiler_params=pltpu.CompilerParams(vmem_limit_bytes=24 * 2**20),
        cost_estimate=pl.CostEstimate(
            flops=12 * packed * width * hidden,
            bytes_accessed=6 * width * hidden,
            transcendentals=0,
        ),
        name="experts",
    )(own, swap(own), gate, up, down)
    joined = pl.pallas_call(
        join_kernel,
        out_shape=(block,) * flight,
        in_specs=[VMEM] * 2,
        out_specs=(VMEM,) * flight,
        compiler_params=pltpu.CompilerParams(vmem_limit_bytes=16 * 2**20),
        name="join",
    )(mine, swap(theirs))
    returned = exchange(joined)
    return pl.pallas_call(
        functools.partial(combine_kernel, flight),
        out_shape=jax.ShapeDtypeStruct((count, width), jnp.bfloat16),
        in_specs=[VMEM] * (flight + 1),
        out_specs=VMEM,
        compiler_params=pltpu.CompilerParams(vmem_limit_bytes=24 * 2**20),
        name="combine",
    )(mix, *returned)


def solution(mesh):
    placed = (
        P(("group", "exp"), None),
        P(),
        P(("group", "exp"), None),
        P(("group", "exp"), None),
        P("exp", None, None),
        P("exp", None, None),
        P("exp", None, None),
    )
    return jax.shard_map(
        per_device, mesh=mesh, in_specs=placed, out_specs=P(("group", "exp"), None), check_vma=False
    )
```

```python
import functools

import jax
import jax.numpy as jnp
from jax import lax
from jax.experimental import pallas as pl
from jax.experimental.pallas import tpu as pltpu
from jax.sharding import PartitionSpec as P

SLOTS = 8
CHUNKS = 4
PIECES = 4
LANES = 128

VMEM = pl.BlockSpec(memory_space=pltpu.VMEM)
HBM = pl.BlockSpec(memory_space=pltpu.HBM)


def in_hbm(*arrays):
    return [pltpu.with_memory_space_constraint(a, pltpu.HBM) for a in arrays]


def relative(flight):
    return 4 <= flight <= 8


def block_order(flight, core):
    if not relative(flight):
        return list(range(flight))
    far = list(range(flight // 2, flight))
    cut = len(far) // 2
    carried, given = (far[:cut], far[cut:]) if core == 0 else (far[cut:], far[:cut])
    return carried + given + list(range(1, flight // 2)) + [0]


def packed_width(width):
    return width // 7 * 6 + LANES


def pack(rows):
    blocks = rows.reshape(-1, SLOTS, rows.shape[1])
    tail = rows.shape[1] // 7
    main = blocks[:, :, : 6 * tail]
    moved = jnp.concatenate([blocks[:, j : j + 1, 6 * tail :] for j in range(6)], axis=2)
    row = lax.broadcasted_iota(jnp.int32, main.shape, 1)
    main = jnp.where(row == SLOTS - 1, moved, main)
    row = row[:, :, :LANES]
    extra = jnp.zeros(row.shape, rows.dtype)
    for k in range(tail // LANES):
        start = 6 * tail + k * LANES
        extra = jnp.where(row == k, blocks[:, 6:7, start : start + LANES], extra)
    return jnp.concatenate([main, extra], axis=2).reshape(rows.shape[0], -1)


def unpack(packed):
    blocks = packed.reshape(-1, SLOTS, packed.shape[1])
    tail = (packed.shape[1] - LANES) // 6
    main = blocks[:, :, : 6 * tail]
    last = jnp.concatenate(
        [blocks[:, k : k + 1, 6 * tail :] for k in range(tail // LANES)], axis=2
    )
    row = lax.broadcasted_iota(jnp.int32, (blocks.shape[0], SLOTS, tail), 1)
    end = jnp.where(row == 6, last, 0.0)
    for j in range(6):
        end = jnp.where(row == j, blocks[:, 7:8, j * tail : (j + 1) * tail], end)
    return jnp.concatenate([main, end], axis=2).reshape(packed.shape[0], -1)


def store(refs, rows):
    at = 0
    for ref in refs:
        ref[...] = rows[at : at + ref.shape[0]].astype(ref.dtype)
        at += ref.shape[0]


def dispatch_kernel(
    flight, tok_hbm, gain_hbm, ids_hbm, gw_hbm, gate_hbm, mix_ref, gate_ref, *rest
):
    *outs, tok, gain, ids, gw, normed, sems = rest
    count = tok.shape[0]
    part = count // CHUNKS
    small = [
        pltpu.make_async_copy(ids_hbm, ids, sems.at[0]),
        pltpu.make_async_copy(gw_hbm, gw, sems.at[1]),
        pltpu.make_async_copy(gain_hbm, gain.at[0], sems.at[2]),
    ]
    large = [
        pltpu.make_async_copy(
            tok_hbm.at[pl.ds(i * part, part)], tok.at[pl.ds(i * part, part)], sems.at[3 + i]
        )
        for i in range(CHUNKS)
    ]
    weights = pltpu.make_async_copy(gate_hbm, gate_ref, sems.at[3 + CHUNKS])
    for copy in small + large + [weights]:
        copy.start()
    small[0].wait()
    small[1].wait()
    experts = lax.broadcasted_iota(jnp.int32, (flight, count), 0)
    if relative(flight):
        place = experts
        me = lax.axis_index("exp")
        for i, (even, odd) in enumerate(zip(block_order(flight, 0), block_order(flight, 1))):
            experts = jnp.where(place == i, jnp.where(me % 2 == 0, even, odd) ^ (me // 2), experts)
    chosen = jnp.zeros((flight, count), jnp.float32)
    gates = jnp.zeros((flight, count), jnp.float32)
    for k in range(ids.shape[0]):
        hit = ids[k : k + 1, :] == experts
        chosen = jnp.where(hit, 1.0, chosen)
        gates = jnp.where(hit, gw[k : k + 1, :], gates)
    before = (
        lax.broadcasted_iota(jnp.int32, (count, count), 0)
        < lax.broadcasted_iota(jnp.int32, (count, count), 1)
    ).astype(jnp.bfloat16)
    rank = jnp.dot(chosen.astype(jnp.bfloat16), before, preferred_element_type=jnp.float32)
    rank = jnp.where(chosen > 0.0, rank, -1.0)

    slot = lax.broadcasted_iota(jnp.int32, (flight, SLOTS, count), 1).astype(jnp.float32)
    taken = rank[:, None, :] == slot
    pick = jnp.where(taken, 1.0, 0.0).reshape(flight * SLOTS, count).astype(jnp.bfloat16)
    mix = jnp.where(taken, gates[:, None, :], 0.0).reshape(flight * SLOTS, count)
    high = mix.astype(jnp.bfloat16)
    mix_ref[: flight * SLOTS, :] = high
    mix_ref[flight * SLOTS :, :] = (mix - high.astype(jnp.float32)).astype(jnp.bfloat16)

    small[2].wait()
    for i in range(CHUNKS):
        large[i].wait()
        wide = tok[pl.ds(i * part, part), :].astype(jnp.float32)
        mean_square = jnp.mean(wide * wide, axis=1, keepdims=True)
        normed[pl.ds(i * part, part), :] = (
            wide * lax.rsqrt(mean_square + 1e-06) * gain[...]
        ).astype(jnp.bfloat16)
    rows = jnp.dot(pick, normed[...], preferred_element_type=jnp.float32)
    store(outs, pack(rows))
    weights.wait()


def stage_kernel(source, target, sems):
    rows = source.shape[0] // PIECES
    copies = [
        pltpu.make_async_copy(
            source.at[pl.ds(i * rows, rows)], target.at[pl.ds(i * rows, rows)], sems.at[i]
        )
        for i in range(PIECES)
    ]
    for copy in copies:
        copy.start()
    for copy in copies:
        copy.wait()


def together(refs):
    return jnp.concatenate([b[...].astype(jnp.float32) for b in refs], axis=0)


def merge_kernel(kept_ref, got_ref, *outs):
    kept, got = kept_ref[...].astype(jnp.float32), got_ref[...].astype(jnp.float32)
    for i, out in enumerate(outs):
        here = slice(i * SLOTS, (i + 1) * SLOTS)
        out[...] = jnp.concatenate([kept[here], got[here]], axis=0).astype(jnp.bfloat16)


def gather_kernel(*refs):
    refs[-1][...] = unpack(together(refs[:-1])).astype(jnp.bfloat16)


def expert_kernel(own_ref, other_ref, gate_ref, up_ref, down_ref, own_out, other_out):
    rows = own_ref.shape[0]
    x = jnp.concatenate([own_ref[...], other_ref[...]], axis=0)
    gate_v = jnp.dot(x, gate_ref[...], preferred_element_type=jnp.float32)
    up_v = jnp.dot(x, up_ref[...], preferred_element_type=jnp.float32)
    hidden = (gate_v / (1.0 + jnp.exp(-gate_v)) * up_v).astype(jnp.bfloat16)
    part = jnp.dot(hidden, down_ref[...], preferred_element_type=jnp.float32).astype(jnp.bfloat16)
    own_out[...] = part[:rows]
    other_out[...] = part[rows:]


def join_kernel(mine_ref, got_ref, *outs):
    store(outs, pack(mine_ref[...].astype(jnp.float32) + got_ref[...].astype(jnp.float32)))


def combine_kernel(carried, mix_ref, *refs):
    *refs, out_ref = refs
    blocks = []
    for i, ref in enumerate(refs):
        rows = ref[...].astype(jnp.float32)
        if i < carried:
            rows = rows[:SLOTS]
        elif i < 2 * carried:
            rows = rows[SLOTS:]
        blocks.append(rows)
    rows = unpack(jnp.concatenate(blocks, axis=0)).astype(jnp.bfloat16)
    both = jnp.concatenate([rows, rows], axis=0)
    out_ref[...] = lax.dot_general(
        mix_ref[...], both, (((0,), (0,)), ((), ())), preferred_element_type=jnp.float32
    ).astype(jnp.bfloat16)


def per_device(tokens, norm_gain, expert_ids, gate_weights, w_gate, w_up, w_down):
    owners = lax.axis_size("exp")
    flight = owners // 2
    count, width = tokens.shape
    hidden = w_gate.shape[2]
    packed = flight * SLOTS
    whole = jax.ShapeDtypeStruct((packed, width), jnp.bfloat16)
    few = relative(flight)
    carried = flight // 4 if few else 0
    near = flight // 2 - 1
    routes = []
    for core in range(2):
        order = block_order(flight, core)
        routes.append(order[:1] + order[2 * carried : -1] + order[1:carried])

    def blocks(*counts):
        return tuple(
            jax.ShapeDtypeStruct((n * SLOTS, packed_width(width)), jnp.bfloat16) for n in counts
        )

    def exchange(arrays):
        if few:
            got = []
            for i, a in enumerate(arrays[:-1]):
                pairs = [(n, n ^ (2 * routes[n % 2][i])) for n in range(owners)]
                got.append(lax.ppermute(a, "exp", pairs))
            return got + [arrays[-1]]
        groups = [list(range(core, owners, 2)) for core in range(2)]
        return [
            lax.all_to_all(
                arrays[0], "exp", split_axis=0, concat_axis=0, axis_index_groups=groups, tiled=True
            )
        ]

    def swap(rows):
        return lax.ppermute(rows, "exp", [(i, i ^ 1) for i in range(owners)])

    def stage(weights):
        return pl.pallas_call(
            stage_kernel,
            out_shape=jax.ShapeDtypeStruct(weights.shape, weights.dtype),
            in_specs=[HBM],
            out_specs=VMEM,
            scratch_shapes=[pltpu.SemaphoreType.DMA((PIECES,))],
            compiler_params=pltpu.CompilerParams(vmem_limit_bytes=16 * 2**20),
            cost_estimate=pl.CostEstimate(
                flops=0, bytes_accessed=4 * width * hidden, transcendentals=0
            ),
            name="stage",
        )(*in_hbm(weights))

    first = blocks(carried, carried, *[1] * (near + 1)) if few else blocks(flight)
    sent = blocks(2, *[1] * near, *[2] * (carried - 1), 1) if few else blocks(flight)
    mix, gate, *outgoing = pl.pallas_call(
        functools.partial(dispatch_kernel, flight),
        out_shape=(
            jax.ShapeDtypeStruct((2 * packed, count), jnp.bfloat16),
            jax.ShapeDtypeStruct(w_gate.shape[1:], w_gate.dtype),
        )
        + first,
        in_specs=[HBM] * 5,
        out_specs=(VMEM,) * (len(first) + 2),
        scratch_shapes=[
            pltpu.VMEM((count, width), jnp.bfloat16),
            pltpu.VMEM((1, width), jnp.float32),
            pltpu.VMEM(expert_ids.shape[::-1], jnp.int32),
            pltpu.VMEM(gate_weights.shape[::-1], jnp.float32),
            pltpu.VMEM((count, width), jnp.bfloat16),
            pltpu.SemaphoreType.DMA((4 + CHUNKS,)),
        ],
        compiler_params=pltpu.CompilerParams(vmem_limit_bytes=24 * 2**20),
        name="dispatch",
    )(*in_hbm(tokens, norm_gain, expert_ids.T, gate_weights.T, w_gate[0]))

    if few:
        kept, given, *others = outgoing
        merged = pl.pallas_call(
            merge_kernel,
            out_shape=sent[:1] * carried,
            in_specs=[VMEM] * 2,
            out_specs=(VMEM,) * carried,
            compiler_params=pltpu.CompilerParams(vmem_limit_bytes=16 * 2**20),
            name="merge",
        )(kept, swap(given))
        outgoing = [merged[0], *others[:-1], *merged[1:], others[-1]]

    up, down = stage(w_up[0]), stage(w_down[0])
    *arrived, up = lax.optimization_barrier((*exchange(outgoing), up))
    own = pl.pallas_call(
        gather_kernel,
        out_shape=whole,
        in_specs=[VMEM] * len(arrived),
        out_specs=VMEM,
        compiler_params=pltpu.CompilerParams(vmem_limit_bytes=16 * 2**20),
        name="gather",
    )(*arrived)
    mine, theirs = pl.pallas_call(
        expert_kernel,
        out_shape=(whole, whole),
        in_specs=[VMEM] * 5,
        out_specs=(VMEM, VMEM),
        compiler_params=pltpu.CompilerParams(vmem_limit_bytes=24 * 2**20),
        cost_estimate=pl.CostEstimate(
            flops=12 * packed * width * hidden,
            bytes_accessed=6 * width * hidden,
            transcendentals=0,
        ),
        name="experts",
    )(own, swap(own), gate, up, down)
    joined = pl.pallas_call(
        join_kernel,
        out_shape=sent,
        in_specs=[VMEM] * 2,
        out_specs=(VMEM,) * len(sent),
        compiler_params=pltpu.CompilerParams(vmem_limit_bytes=16 * 2**20),
        name="join",
    )(mine, swap(theirs))
    returned = exchange(joined)
    if few:
        pair, *close = lax.optimization_barrier(returned[: near + 1])
        pairs = [pair, *returned[near + 1 : -1]]
        returned = [*pairs, *[swap(a) for a in pairs], *close, returned[-1]]
    return pl.pallas_call(
        functools.partial(combine_kernel, carried),
        out_shape=jax.ShapeDtypeStruct((count, width), jnp.bfloat16),
        in_specs=[VMEM] * (len(returned) + 1),
        out_specs=VMEM,
        compiler_params=pltpu.CompilerParams(vmem_limit_bytes=24 * 2**20),
        name="combine",
    )(mix, *returned)


def solution(mesh):
    placed = (
        P(("group", "exp"), None),
        P(),
        P(("group", "exp"), None),
        P(("group", "exp"), None),
        P("exp", None, None),
        P("exp", None, None),
        P("exp", None, None),
    )
    return jax.shard_map(
        per_device, mesh=mesh, in_specs=placed, out_specs=P(("group", "exp"), None), check_vma=False
    )
```

```python
import functools

import jax
import jax.numpy as jnp
from jax import lax
from jax.experimental import pallas as pl
from jax.experimental.pallas import tpu as pltpu
from jax.sharding import PartitionSpec as P

SLOTS = 8
CHUNKS = 4
PIECES = 4
LANES = 128

VMEM = pl.BlockSpec(memory_space=pltpu.VMEM)
SMALL = pl.CostEstimate(flops=1, bytes_accessed=1, transcendentals=0)
HBM = pl.BlockSpec(memory_space=pltpu.HBM)


def in_hbm(*arrays):
    return [pltpu.with_memory_space_constraint(a, pltpu.HBM) for a in arrays]


def relative(flight):
    return flight == 8


CARRIED = ((4, 5), (6, 7))
NEAR = (1, 2, 3)


def block_order(flight, core):
    if not relative(flight):
        return range(flight)
    return CARRIED[core] + CARRIED[1 - core] + NEAR + (0,)


def packed_width(width):
    return width // 7 * 6 + LANES


def pack(rows):
    blocks = rows.reshape(-1, SLOTS, rows.shape[1])
    tail = rows.shape[1] // 7
    main = blocks[:, :, : 6 * tail]
    moved = jnp.concatenate([blocks[:, j : j + 1, 6 * tail :] for j in range(6)], axis=2)
    row = lax.broadcasted_iota(jnp.int32, main.shape, 1)
    main = jnp.where(row == SLOTS - 1, moved, main)
    row = row[:, :, :LANES]
    extra = jnp.zeros(row.shape, rows.dtype)
    for k in range(tail // LANES):
        start = 6 * tail + k * LANES
        extra = jnp.where(row == k, blocks[:, 6:7, start : start + LANES], extra)
    return jnp.concatenate([main, extra], axis=2).reshape(rows.shape[0], -1)


def unpack(packed):
    blocks = packed.reshape(-1, SLOTS, packed.shape[1])
    tail = (packed.shape[1] - LANES) // 6
    main = blocks[:, :, : 6 * tail]
    last = jnp.concatenate(
        [blocks[:, k : k + 1, 6 * tail :] for k in range(tail // LANES)], axis=2
    )
    row = lax.broadcasted_iota(jnp.int32, (blocks.shape[0], SLOTS, tail), 1)
    end = jnp.where(row == 6, last, 0.0)
    for j in range(6):
        end = jnp.where(row == j, blocks[:, 7:8, j * tail : (j + 1) * tail], end)
    return jnp.concatenate([main, end], axis=2).reshape(packed.shape[0], -1)


def store(refs, rows):
    at = 0
    for ref in refs:
        ref[...] = rows[at : at + ref.shape[0]].astype(ref.dtype)
        at += ref.shape[0]


def dispatch_kernel(flight, tok_hbm, gain_hbm, ids_hbm, gw_hbm, mix_ref, *rest):
    *outs, tok, gain, ids, gw, normed, sems = rest
    count = tok.shape[0]
    part = count // CHUNKS
    small = [
        pltpu.make_async_copy(ids_hbm, ids, sems.at[0]),
        pltpu.make_async_copy(gw_hbm, gw, sems.at[1]),
        pltpu.make_async_copy(gain_hbm, gain.at[0], sems.at[2]),
    ]
    large = [
        pltpu.make_async_copy(
            tok_hbm.at[pl.ds(i * part, part)], tok.at[pl.ds(i * part, part)], sems.at[3 + i]
        )
        for i in range(CHUNKS)
    ]
    for copy in small + large:
        copy.start()
    small[0].wait()
    small[1].wait()
    experts = lax.broadcasted_iota(jnp.int32, (flight, count), 0)
    if relative(flight):
        place = experts
        me = lax.axis_index("exp")
        for i, (even, odd) in enumerate(zip(block_order(flight, 0), block_order(flight, 1))):
            experts = jnp.where(place == i, jnp.where(me % 2 == 0, even, odd) ^ (me // 2), experts)
    chosen = jnp.zeros((flight, count), jnp.float32)
    gates = jnp.zeros((flight, count), jnp.float32)
    for k in range(ids.shape[0]):
        hit = ids[k : k + 1, :] == experts
        chosen = jnp.where(hit, 1.0, chosen)
        gates = jnp.where(hit, gw[k : k + 1, :], gates)
    before = (
        lax.broadcasted_iota(jnp.int32, (count, count), 0)
        < lax.broadcasted_iota(jnp.int32, (count, count), 1)
    ).astype(jnp.bfloat16)
    rank = jnp.dot(chosen.astype(jnp.bfloat16), before, preferred_element_type=jnp.float32)
    rank = jnp.where(chosen > 0.0, rank, -1.0)

    slot = lax.broadcasted_iota(jnp.int32, (flight, SLOTS, count), 1).astype(jnp.float32)
    taken = rank[:, None, :] == slot
    pick = jnp.where(taken, 1.0, 0.0).reshape(flight * SLOTS, count).astype(jnp.bfloat16)
    mix = jnp.where(taken, gates[:, None, :], 0.0).reshape(flight * SLOTS, count)
    high = mix.astype(jnp.bfloat16)
    mix_ref[: flight * SLOTS, :] = high
    mix_ref[flight * SLOTS :, :] = (mix - high.astype(jnp.float32)).astype(jnp.bfloat16)

    small[2].wait()
    for i in range(CHUNKS):
        large[i].wait()
        wide = tok[pl.ds(i * part, part), :].astype(jnp.float32)
        mean_square = jnp.mean(wide * wide, axis=1, keepdims=True)
        normed[pl.ds(i * part, part), :] = (
            wide * lax.rsqrt(mean_square + 1e-06) * gain[...]
        ).astype(jnp.bfloat16)
    rows = jnp.dot(pick, normed[...], preferred_element_type=jnp.float32)
    store(outs, pack(rows))


def stage_kernel(source, *refs):
    target, sems = refs[-2:]
    rows = source.shape[0] // PIECES
    copies = [
        pltpu.make_async_copy(
            source.at[pl.ds(i * rows, rows)], target.at[pl.ds(i * rows, rows)], sems.at[i]
        )
        for i in range(PIECES)
    ]
    for copy in copies:
        copy.start()
    for copy in copies:
        copy.wait()


def together(refs):
    return jnp.concatenate([b[...].astype(jnp.float32) for b in refs], axis=0)


def merge_kernel(kept_ref, got_ref, *outs):
    kept, got = kept_ref[...].astype(jnp.float32), got_ref[...].astype(jnp.float32)
    for i, out in enumerate(outs):
        here = slice(i * SLOTS, (i + 1) * SLOTS)
        out[...] = jnp.concatenate([kept[here], got[here]], axis=0).astype(jnp.bfloat16)


def gather_kernel(*refs):
    refs[-1][...] = unpack(together(refs[:-1])).astype(jnp.bfloat16)


def expert_kernel(count, *refs):
    rows, weights, outs = refs[: 2 * count], refs[2 * count : 2 * count + 3], refs[2 * count + 3 :]
    gate_ref, up_ref, down_ref = weights
    x = jnp.concatenate([r[...] for r in rows], axis=0)
    gate_v = jnp.dot(x, gate_ref[...], preferred_element_type=jnp.float32)
    up_v = jnp.dot(x, up_ref[...], preferred_element_type=jnp.float32)
    hidden = (gate_v / (1.0 + jnp.exp(-gate_v)) * up_v).astype(jnp.bfloat16)
    store(outs, jnp.dot(hidden, down_ref[...], preferred_element_type=jnp.float32))


def join_kernel(mine_ref, got_ref, *outs):
    store(outs, pack(mine_ref[...].astype(jnp.float32) + got_ref[...].astype(jnp.float32)))


def weigh(mix, rows):
    rows = unpack(rows).astype(jnp.bfloat16)
    both = jnp.concatenate([rows, rows], axis=0)
    return lax.dot_general(mix, both, (((0,), (0,)), ((), ())), preferred_element_type=jnp.float32)


def mix_rows(mix_ref, start, count):
    half = mix_ref.shape[0] // 2
    return jnp.concatenate([mix_ref[at + start : at + start + count, :] for at in (0, half)], axis=0)


def close_kernel(mix_ref, *refs):
    *refs, out_ref = refs
    rows = together(refs)
    out_ref[...] = weigh(mix_rows(mix_ref, mix_ref.shape[0] // 2 - rows.shape[0], rows.shape[0]), rows)


def far_kernel(first, mix_ref, close_ref, *refs):
    *refs, out_ref = refs
    blocks = [
        r[...].astype(jnp.float32)[at * SLOTS : (at + 1) * SLOTS] for r, at in zip(refs, first)
    ]
    rows = jnp.concatenate(blocks, axis=0)
    out_ref[...] = (
        close_ref[...] + weigh(mix_rows(mix_ref, 0, rows.shape[0]), rows)
    ).astype(jnp.bfloat16)


def combine_kernel(mix_ref, rows_ref, out_ref):
    out_ref[...] = weigh(mix_ref[...], rows_ref[...].astype(jnp.float32)).astype(jnp.bfloat16)


def per_device(tokens, norm_gain, expert_ids, gate_weights, w_gate, w_up, w_down):
    owners = lax.axis_size("exp")
    flight = owners // 2
    count, width = tokens.shape
    hidden = w_gate.shape[2]
    few = relative(flight)

    def local(kernel, outs, name, *args, limit=16):
        return pl.pallas_call(
            kernel,
            out_shape=outs,
            in_specs=[VMEM] * len(args),
            out_specs=(VMEM,) * len(outs),
            compiler_params=pltpu.CompilerParams(vmem_limit_bytes=limit * 2**20),
            cost_estimate=SMALL,
            name=name,
        )(*args)

    def full(*counts):
        return tuple(jax.ShapeDtypeStruct((n * SLOTS, width), jnp.bfloat16) for n in counts)

    def packed(*counts):
        shapes = [(n * SLOTS, packed_width(width)) for n in counts]
        return tuple(jax.ShapeDtypeStruct(shape, jnp.bfloat16) for shape in shapes)

    def swap(rows):
        return lax.ppermute(rows, "exp", [(n, n ^ 1) for n in range(owners)])

    def travel(rows, distances, cross=0):
        pairs = [(n, n ^ (2 * distances[n % 2]) ^ cross) for n in range(owners)]
        return lax.ppermute(rows, "exp", pairs)

    def stage(weights, *after):
        return pl.pallas_call(
            stage_kernel,
            out_shape=jax.ShapeDtypeStruct(weights.shape, weights.dtype),
            in_specs=[HBM] + [pl.BlockSpec(memory_space=pl.ANY)] * len(after),
            out_specs=VMEM,
            scratch_shapes=[pltpu.SemaphoreType.DMA((PIECES,))],
            compiler_params=pltpu.CompilerParams(vmem_limit_bytes=16 * 2**20),
            cost_estimate=SMALL,
            name="stage",
        )(*in_hbm(weights), *after)

    def experts(own, other, weights, outs):
        return local(
            functools.partial(expert_kernel, len(own)),
            outs,
            "experts",
            *own,
            *other,
            *weights,
            limit=24,
        )

    result = (jax.ShapeDtypeStruct((count, width), jnp.bfloat16),)
    first = packed(2, 2, 1, 1, 1, 1) if few else packed(flight)
    mix, *outgoing = pl.pallas_call(
        functools.partial(dispatch_kernel, flight),
        out_shape=(jax.ShapeDtypeStruct((2 * flight * SLOTS, count), jnp.bfloat16),) + first,
        in_specs=[HBM] * 4,
        out_specs=(VMEM,) * (len(first) + 1),
        scratch_shapes=[
            pltpu.VMEM((count, width), jnp.bfloat16),
            pltpu.VMEM((1, width), jnp.float32),
            pltpu.VMEM(expert_ids.shape[::-1], jnp.int32),
            pltpu.VMEM(gate_weights.shape[::-1], jnp.float32),
            pltpu.VMEM((count, width), jnp.bfloat16),
            pltpu.SemaphoreType.DMA((3 + CHUNKS,)),
        ],
        compiler_params=pltpu.CompilerParams(vmem_limit_bytes=24 * 2**20),
        name="dispatch",
    )(*in_hbm(tokens, norm_gain, expert_ids.T, gate_weights.T))
    down = stage(w_down[0])

    if not few:
        gate, up = stage(w_gate[0]), stage(w_up[0])
        groups = [list(range(core, owners, 2)) for core in range(2)]
        exchange = functools.partial(
            lax.all_to_all,
            axis_name="exp",
            split_axis=0,
            concat_axis=0,
            axis_index_groups=groups,
            tiled=True,
        )
        (own,) = local(gather_kernel, full(flight), "gather", exchange(outgoing[0]))
        mine, theirs = experts([own], [swap(own)], (gate, up, down), full(flight, flight))
        (joined,) = local(join_kernel, packed(flight), "join", mine, swap(theirs))
        return local(combine_kernel, result, "combine", mix, exchange(joined), limit=24)[0]

    near = [(r, r) for r in NEAR]
    one, two = zip(*CARRIED)
    kept, given, *close, own = outgoing
    far = local(merge_kernel, packed(2, 2), "merge", kept, swap(given))
    gate = stage(w_gate[0], far[0])
    far_one = travel(far[0], one)
    close = [travel(a, r) for a, r in zip(close, near)]
    far_two, gate, *close = lax.optimization_barrier((far[1], gate, *close))
    up = stage(w_up[0], far_one)
    far_two = travel(far_two, two)
    far_two, up = lax.optimization_barrier((far_two, up))
    (own,) = local(gather_kernel, full(8), "gather", far_one, *close, own, far_two)
    mine_one, mine, theirs_one, theirs = experts(
        [own], [swap(own)], (gate, up, down), full(2, 6, 2, 6)
    )
    (far_one,) = local(join_kernel, packed(2), "join", mine_one, swap(theirs_one))
    far_one = travel(far_one, one)
    *close, own, far_two = local(join_kernel, packed(1, 1, 1, 1, 2), "join", mine, swap(theirs))
    close = [travel(a, r) for a, r in zip(close, near)]
    far_two, *close = lax.optimization_barrier((far_two, *close))
    far_two = travel(far_two, two)
    total = (jax.ShapeDtypeStruct((count, width), jnp.float32),)
    (total,) = local(close_kernel, total, "combine_close", mix, *close, own, limit=24)
    far_one, total = lax.optimization_barrier((far_one, total))
    arrays = [far_one, far_two, swap(far_one), swap(far_two)]
    kernel = functools.partial(far_kernel, (0, 0, 1, 1))
    return local(kernel, result, "combine_far", mix, total, *arrays, limit=24)[0]


def solution(mesh):
    placed = (
        P(("group", "exp"), None),
        P(),
        P(("group", "exp"), None),
        P(("group", "exp"), None),
        P("exp", None, None),
        P("exp", None, None),
        P("exp", None, None),
    )
    return jax.shard_map(
        per_device, mesh=mesh, in_specs=placed, out_specs=P(("group", "exp"), None), check_vma=False
    )
```

```python
import functools

import jax
import jax.numpy as jnp
from jax import lax
from jax.experimental import pallas as pl
from jax.experimental.pallas import tpu as pltpu
from jax.sharding import PartitionSpec as P

SLOTS = 8
CHUNKS = 4
PIECES = 4
OUT_PIECES = 4
LANES = 128

VMEM = pl.BlockSpec(memory_space=pltpu.VMEM)
SMALL = pl.CostEstimate(flops=1, bytes_accessed=1, transcendentals=0)
HBM = pl.BlockSpec(memory_space=pltpu.HBM)


def in_hbm(*arrays):
    return [pltpu.with_memory_space_constraint(a, pltpu.HBM) for a in arrays]


def relative(flight):
    return flight == 8


CARRIED = ((4, 1, 5), (6, 2, 7))
SHARED = 3


def block_order(flight, core):
    if not relative(flight):
        return range(flight)
    return CARRIED[core] + CARRIED[1 - core] + (SHARED, 0)


def packed_width(width):
    return width // 7 * 6 + LANES


def pack(rows):
    blocks = rows.reshape(-1, SLOTS, rows.shape[1])
    tail = rows.shape[1] // 7
    main = blocks[:, :, : 6 * tail]
    moved = jnp.concatenate([blocks[:, j : j + 1, 6 * tail :] for j in range(6)], axis=2)
    row = lax.broadcasted_iota(jnp.int32, main.shape, 1)
    main = jnp.where(row == SLOTS - 1, moved, main)
    row = row[:, :, :LANES]
    extra = jnp.zeros(row.shape, rows.dtype)
    for k in range(tail // LANES):
        start = 6 * tail + k * LANES
        extra = jnp.where(row == k, blocks[:, 6:7, start : start + LANES], extra)
    return jnp.concatenate([main, extra], axis=2).reshape(rows.shape[0], -1)


def unpack(packed):
    blocks = packed.reshape(-1, SLOTS, packed.shape[1])
    tail = (packed.shape[1] - LANES) // 6
    main = blocks[:, :, : 6 * tail]
    last = jnp.concatenate(
        [blocks[:, k : k + 1, 6 * tail :] for k in range(tail // LANES)], axis=2
    )
    row = lax.broadcasted_iota(jnp.int32, (blocks.shape[0], SLOTS, tail), 1)
    end = jnp.where(row == 6, last, 0.0)
    for j in range(6):
        end = jnp.where(row == j, blocks[:, 7:8, j * tail : (j + 1) * tail], end)
    return jnp.concatenate([main, end], axis=2).reshape(packed.shape[0], -1)


def store(refs, rows):
    at = 0
    for ref in refs:
        ref[...] = rows[at : at + ref.shape[0]].astype(ref.dtype)
        at += ref.shape[0]


def dispatch_kernel(flight, tok_hbm, gain_hbm, ids_hbm, gw_hbm, mix_ref, *rest):
    *outs, tok, gain, ids, gw, normed, sems = rest
    count = tok.shape[0]
    part = count // CHUNKS
    small = [
        pltpu.make_async_copy(ids_hbm, ids, sems.at[0]),
        pltpu.make_async_copy(gw_hbm, gw, sems.at[1]),
        pltpu.make_async_copy(gain_hbm, gain.at[0], sems.at[2]),
    ]
    large = [
        pltpu.make_async_copy(
            tok_hbm.at[pl.ds(i * part, part)], tok.at[pl.ds(i * part, part)], sems.at[3 + i]
        )
        for i in range(CHUNKS)
    ]
    for copy in small + large:
        copy.start()
    small[0].wait()
    small[1].wait()
    experts = lax.broadcasted_iota(jnp.int32, (flight, count), 0)
    if relative(flight):
        place = experts
        me = lax.axis_index("exp")
        for i, (even, odd) in enumerate(zip(block_order(flight, 0), block_order(flight, 1))):
            experts = jnp.where(place == i, jnp.where(me % 2 == 0, even, odd) ^ (me // 2), experts)
    chosen = jnp.zeros((flight, count), jnp.float32)
    gates = jnp.zeros((flight, count), jnp.float32)
    for k in range(ids.shape[0]):
        hit = ids[k : k + 1, :] == experts
        chosen = jnp.where(hit, 1.0, chosen)
        gates = jnp.where(hit, gw[k : k + 1, :], gates)
    before = (
        lax.broadcasted_iota(jnp.int32, (count, count), 0)
        < lax.broadcasted_iota(jnp.int32, (count, count), 1)
    ).astype(jnp.bfloat16)
    rank = jnp.dot(chosen.astype(jnp.bfloat16), before, preferred_element_type=jnp.float32)
    rank = jnp.where(chosen > 0.0, rank, -1.0)

    slot = lax.broadcasted_iota(jnp.int32, (flight, SLOTS, count), 1).astype(jnp.float32)
    taken = rank[:, None, :] == slot
    pick = jnp.where(taken, 1.0, 0.0).reshape(flight * SLOTS, count).astype(jnp.bfloat16)
    mix = jnp.where(taken, gates[:, None, :], 0.0).reshape(flight * SLOTS, count)
    high = mix.astype(jnp.bfloat16)
    mix_ref[: flight * SLOTS, :] = high
    mix_ref[flight * SLOTS :, :] = (mix - high.astype(jnp.float32)).astype(jnp.bfloat16)

    small[2].wait()
    for i in range(CHUNKS):
        large[i].wait()
        wide = tok[pl.ds(i * part, part), :].astype(jnp.float32)
        mean_square = jnp.mean(wide * wide, axis=1, keepdims=True)
        normed[pl.ds(i * part, part), :] = (
            wide * lax.rsqrt(mean_square + 1e-06) * gain[...]
        ).astype(jnp.bfloat16)
    rows = jnp.dot(pick, normed[...], preferred_element_type=jnp.float32)
    store(outs, pack(rows))


def stage_kernel(source, *refs):
    target, sems = refs[-2:]
    rows = source.shape[0] // PIECES
    copies = [
        pltpu.make_async_copy(
            source.at[pl.ds(i * rows, rows)], target.at[pl.ds(i * rows, rows)], sems.at[i]
        )
        for i in range(PIECES)
    ]
    for copy in copies:
        copy.start()
    for copy in copies:
        copy.wait()


def together(refs):
    return jnp.concatenate([b[...].astype(jnp.float32) for b in refs], axis=0)


def merge_kernel(kept_ref, got_ref, *outs):
    kept, got = kept_ref[...].astype(jnp.float32), got_ref[...].astype(jnp.float32)
    for i, out in enumerate(outs):
        here = slice(i * SLOTS, (i + 1) * SLOTS)
        out[...] = jnp.concatenate([kept[here], got[here]], axis=0).astype(jnp.bfloat16)


def gather_kernel(*refs):
    refs[-1][...] = unpack(together(refs[:-1])).astype(jnp.bfloat16)


def expert_kernel(count, *refs):
    rows, weights, outs = refs[: 2 * count], refs[2 * count : 2 * count + 3], refs[2 * count + 3 :]
    gate_ref, up_ref, down_ref = weights
    x = jnp.concatenate([r[...] for r in rows], axis=0)
    gate_v = jnp.dot(x, gate_ref[...], preferred_element_type=jnp.float32)
    up_v = jnp.dot(x, up_ref[...], preferred_element_type=jnp.float32)
    hidden = (gate_v / (1.0 + jnp.exp(-gate_v)) * up_v).astype(jnp.bfloat16)
    store(outs, jnp.dot(hidden, down_ref[...], preferred_element_type=jnp.float32))


def join_kernel(mine_ref, got_ref, *outs):
    store(outs, pack(mine_ref[...].astype(jnp.float32) + got_ref[...].astype(jnp.float32)))


def combine_kernel(first, mix_ref, *refs):
    *refs, out_hbm, out, sems = refs
    blocks = [r[...].astype(jnp.float32) for r in refs]
    if first:
        blocks = [b[at * SLOTS : (at + 1) * SLOTS] for b, at in zip(blocks, first)]
    rows = unpack(jnp.concatenate(blocks, axis=0)).astype(jnp.bfloat16)
    both = jnp.concatenate([rows, rows], axis=0)
    mix = mix_ref[...]
    part = out.shape[1] // OUT_PIECES
    copies = []
    for i in range(OUT_PIECES):
        here = pl.ds(i * part, part)
        out[:, here] = lax.dot_general(
            mix,
            both[:, i * part : (i + 1) * part],
            (((0,), (0,)), ((), ())),
            preferred_element_type=jnp.float32,
        ).astype(jnp.bfloat16)
        copies.append(pltpu.make_async_copy(out.at[:, here], out_hbm.at[:, here], sems.at[i]))
        copies[-1].start()
    for copy in copies:
        copy.wait()


def per_device(tokens, norm_gain, expert_ids, gate_weights, w_gate, w_up, w_down):
    owners = lax.axis_size("exp")
    flight = owners // 2
    count, width = tokens.shape
    hidden = w_gate.shape[2]
    few = relative(flight)

    def local(kernel, outs, name, *args, limit=16):
        return pl.pallas_call(
            kernel,
            out_shape=outs,
            in_specs=[VMEM] * len(args),
            out_specs=(VMEM,) * len(outs),
            compiler_params=pltpu.CompilerParams(vmem_limit_bytes=limit * 2**20),
            cost_estimate=SMALL,
            name=name,
        )(*args)

    def full(*counts):
        return tuple(jax.ShapeDtypeStruct((n * SLOTS, width), jnp.bfloat16) for n in counts)

    def packed(*counts):
        shapes = [(n * SLOTS, packed_width(width)) for n in counts]
        return tuple(jax.ShapeDtypeStruct(shape, jnp.bfloat16) for shape in shapes)

    def swap(rows):
        return lax.ppermute(rows, "exp", [(n, n ^ 1) for n in range(owners)])

    def travel(rows, distances, cross=0):
        pairs = [(n, n ^ (2 * distances[n % 2]) ^ cross) for n in range(owners)]
        return lax.ppermute(rows, "exp", pairs)

    def stage(weights, *after):
        return pl.pallas_call(
            stage_kernel,
            out_shape=jax.ShapeDtypeStruct(weights.shape, weights.dtype),
            in_specs=[HBM] + [pl.BlockSpec(memory_space=pl.ANY)] * len(after),
            out_specs=VMEM,
            scratch_shapes=[pltpu.SemaphoreType.DMA((PIECES,))],
            compiler_params=pltpu.CompilerParams(vmem_limit_bytes=16 * 2**20),
            cost_estimate=SMALL,
            name="stage",
        )(*in_hbm(weights), *after)

    def experts(own, other, weights, outs):
        return local(
            functools.partial(expert_kernel, len(own)),
            outs,
            "experts",
            *own,
            *other,
            *weights,
            limit=24,
        )

    def combine(mix, arrays, first):
        return pl.pallas_call(
            functools.partial(combine_kernel, first),
            out_shape=jax.ShapeDtypeStruct((count, width), jnp.bfloat16),
            in_specs=[VMEM] * (len(arrays) + 1),
            out_specs=HBM,
            scratch_shapes=[
                pltpu.VMEM((count, width), jnp.bfloat16),
                pltpu.SemaphoreType.DMA((OUT_PIECES,)),
            ],
            compiler_params=pltpu.CompilerParams(vmem_limit_bytes=24 * 2**20),
            name="combine",
        )(mix, *arrays)

    first = packed(3, 3, 1, 1) if few else packed(flight)
    mix, *outgoing = pl.pallas_call(
        functools.partial(dispatch_kernel, flight),
        out_shape=(jax.ShapeDtypeStruct((2 * flight * SLOTS, count), jnp.bfloat16),) + first,
        in_specs=[HBM] * 4,
        out_specs=(VMEM,) * (len(first) + 1),
        scratch_shapes=[
            pltpu.VMEM((count, width), jnp.bfloat16),
            pltpu.VMEM((1, width), jnp.float32),
            pltpu.VMEM(expert_ids.shape[::-1], jnp.int32),
            pltpu.VMEM(gate_weights.shape[::-1], jnp.float32),
            pltpu.VMEM((count, width), jnp.bfloat16),
            pltpu.SemaphoreType.DMA((3 + CHUNKS,)),
        ],
        compiler_params=pltpu.CompilerParams(vmem_limit_bytes=24 * 2**20),
        name="dispatch",
    )(*in_hbm(tokens, norm_gain, expert_ids.T, gate_weights.T))
    gate, up, down = stage(w_gate[0]), stage(w_up[0]), stage(w_down[0])

    if not few:
        groups = [list(range(core, owners, 2)) for core in range(2)]
        exchange = functools.partial(
            lax.all_to_all,
            axis_name="exp",
            split_axis=0,
            concat_axis=0,
            axis_index_groups=groups,
            tiled=True,
        )
        (own,) = local(gather_kernel, full(flight), "gather", exchange(outgoing[0]))
        mine, theirs = experts([own], [swap(own)], (gate, up, down), full(flight, flight))
        (joined,) = local(join_kernel, packed(flight), "join", mine, swap(theirs))
        return combine(mix, [exchange(joined)], None)

    one, two, three = zip(*CARRIED)
    four = (SHARED, SHARED)
    kept, given, shared, own = outgoing
    pairs = local(merge_kernel, packed(2, 2, 2), "merge", kept, swap(given))
    arrived = [travel(a, r) for a, r in zip((*pairs, shared), (one, two, three, four))]
    *arrived, gate, up = lax.optimization_barrier((*arrived, gate, up))
    (own,) = local(gather_kernel, full(8), "gather", *arrived, own)

    mine_one, mine_two, theirs_one, theirs_two = experts(
        [own], [swap(own)], (gate, up, down), full(4, 4, 4, 4)
    )
    first, second = local(join_kernel, packed(2, 2), "join", mine_one, swap(theirs_one))
    third, shared, own = local(join_kernel, packed(2, 1, 1), "join", mine_two, swap(theirs_two))
    returned = [
        travel(a, r) for a, r in zip((first, second, third, shared), (one, two, three, four))
    ]
    *pairs, shared = returned
    pairs[0], shared = lax.optimization_barrier((pairs[0], shared))
    arrays = [*pairs, *[swap(a) for a in pairs], shared, own]
    return combine(mix, arrays, (0, 0, 0, 1, 1, 1, 0, 0))


def solution(mesh):
    placed = (
        P(("group", "exp"), None),
        P(),
        P(("group", "exp"), None),
        P(("group", "exp"), None),
        P("exp", None, None),
        P("exp", None, None),
        P("exp", None, None),
    )
    return jax.shard_map(
        per_device, mesh=mesh, in_specs=placed, out_specs=P(("group", "exp"), None), check_vma=False
    )
```

```python
import functools

import jax
import jax.numpy as jnp
from jax import lax
from jax.experimental import pallas as pl
from jax.experimental.pallas import tpu as pltpu
from jax.sharding import PartitionSpec as P

SLOTS = 8
CHUNKS = 4
PIECES = 4
OUT_PIECES = 4
LANES = 128

VMEM = pl.BlockSpec(memory_space=pltpu.VMEM)
SMALL = pl.CostEstimate(flops=1, bytes_accessed=1, transcendentals=0)
HBM = pl.BlockSpec(memory_space=pltpu.HBM)


def in_hbm(*arrays):
    return [pltpu.with_memory_space_constraint(a, pltpu.HBM) for a in arrays]


def relative(flight):
    return flight == 8


CARRIED = ((4, 1, 5), (6, 2, 7))
SHARED = 3


def block_order(flight, core):
    if not relative(flight):
        return range(flight)
    return CARRIED[core] + CARRIED[1 - core] + (SHARED, 0)


def packed_width(width):
    return width // 7 * 6 + LANES


def pack(rows):
    blocks = rows.reshape(-1, SLOTS, rows.shape[1])
    tail = rows.shape[1] // 7
    main = blocks[:, :, : 6 * tail]
    moved = jnp.concatenate([blocks[:, j : j + 1, 6 * tail :] for j in range(6)], axis=2)
    row = lax.broadcasted_iota(jnp.int32, main.shape, 1)
    main = jnp.where(row == SLOTS - 1, moved, main)
    row = row[:, :, :LANES]
    extra = jnp.zeros(row.shape, rows.dtype)
    for k in range(tail // LANES):
        start = 6 * tail + k * LANES
        extra = jnp.where(row == k, blocks[:, 6:7, start : start + LANES], extra)
    return jnp.concatenate([main, extra], axis=2).reshape(rows.shape[0], -1)


def unpack(packed):
    blocks = packed.reshape(-1, SLOTS, packed.shape[1])
    tail = (packed.shape[1] - LANES) // 6
    main = blocks[:, :, : 6 * tail]
    last = jnp.concatenate(
        [blocks[:, k : k + 1, 6 * tail :] for k in range(tail // LANES)], axis=2
    )
    row = lax.broadcasted_iota(jnp.int32, (blocks.shape[0], SLOTS, tail), 1)
    end = jnp.where(row == 6, last, 0.0)
    for j in range(6):
        end = jnp.where(row == j, blocks[:, 7:8, j * tail : (j + 1) * tail], end)
    return jnp.concatenate([main, end], axis=2).reshape(packed.shape[0], -1)


def store(refs, rows):
    at = 0
    for ref in refs:
        ref[...] = rows[at : at + ref.shape[0]].astype(ref.dtype)
        at += ref.shape[0]


def dispatch_kernel(flight, tok_hbm, gain_hbm, ids_hbm, gw_hbm, mix_ref, *rest):
    *outs, tok, gain, ids, gw, normed, sems = rest
    count = tok.shape[0]
    part = count // CHUNKS
    small = [
        pltpu.make_async_copy(ids_hbm, ids, sems.at[0]),
        pltpu.make_async_copy(gw_hbm, gw, sems.at[1]),
        pltpu.make_async_copy(gain_hbm, gain.at[0], sems.at[2]),
    ]
    large = [
        pltpu.make_async_copy(
            tok_hbm.at[pl.ds(i * part, part)], tok.at[pl.ds(i * part, part)], sems.at[3 + i]
        )
        for i in range(CHUNKS)
    ]
    for copy in small + large:
        copy.start()
    small[0].wait()
    small[1].wait()
    experts = lax.broadcasted_iota(jnp.int32, (flight, count), 0)
    if relative(flight):
        place = experts
        me = lax.axis_index("exp")
        for i, (even, odd) in enumerate(zip(block_order(flight, 0), block_order(flight, 1))):
            experts = jnp.where(place == i, jnp.where(me % 2 == 0, even, odd) ^ (me // 2), experts)
    chosen = jnp.zeros((flight, count), jnp.float32)
    gates = jnp.zeros((flight, count), jnp.float32)
    for k in range(ids.shape[0]):
        hit = ids[k : k + 1, :] == experts
        chosen = jnp.where(hit, 1.0, chosen)
        gates = jnp.where(hit, gw[k : k + 1, :], gates)
    before = (
        lax.broadcasted_iota(jnp.int32, (count, count), 0)
        < lax.broadcasted_iota(jnp.int32, (count, count), 1)
    ).astype(jnp.bfloat16)
    rank = jnp.dot(chosen.astype(jnp.bfloat16), before, preferred_element_type=jnp.float32)
    rank = jnp.where(chosen > 0.0, rank, -1.0)

    slot = lax.broadcasted_iota(jnp.int32, (flight, SLOTS, count), 1).astype(jnp.float32)
    taken = rank[:, None, :] == slot
    pick = jnp.where(taken, 1.0, 0.0).reshape(flight * SLOTS, count).astype(jnp.bfloat16)
    mix = jnp.where(taken, gates[:, None, :], 0.0).reshape(flight * SLOTS, count)
    high = mix.astype(jnp.bfloat16)
    mix_ref[: flight * SLOTS, :] = high
    mix_ref[flight * SLOTS :, :] = (mix - high.astype(jnp.float32)).astype(jnp.bfloat16)

    small[2].wait()
    for i in range(CHUNKS):
        large[i].wait()
        wide = tok[pl.ds(i * part, part), :].astype(jnp.float32)
        mean_square = jnp.mean(wide * wide, axis=1, keepdims=True)
        normed[pl.ds(i * part, part), :] = (
            wide * lax.rsqrt(mean_square + 1e-06) * gain[...]
        ).astype(jnp.bfloat16)
    rows = jnp.dot(pick, normed[...], preferred_element_type=jnp.float32)
    blocks = pack(rows)
    if len(outs) == 1:
        store(outs, blocks)
    else:
        kept, given = 3 * SLOTS, 6 * SLOTS
        store(outs[:1], blocks[:kept])
        store(outs[1:2], jnp.concatenate([blocks[kept:given], blocks[given + SLOTS :]], axis=0))
        store(outs[2:], blocks[given:])


def stage_kernel(*refs):
    sources, targets, sems = refs[:3], refs[-4:-1], refs[-1]
    copies = []
    for at, (source, target) in enumerate(zip(sources, targets)):
        rows = source.shape[0] // PIECES
        for i in range(PIECES):
            here = pl.ds(i * rows, rows)
            copies.append(
                pltpu.make_async_copy(source.at[here], target.at[here], sems.at[at * PIECES + i])
            )
    for copy in copies:
        copy.start()
    for copy in copies:
        copy.wait()


def together(refs):
    return jnp.concatenate([b[...].astype(jnp.float32) for b in refs], axis=0)


def merge_kernel(kept_ref, got_ref, *outs):
    *outs, own_out = outs
    kept, got = kept_ref[...].astype(jnp.float32), got_ref[...].astype(jnp.float32)
    for i, out in enumerate(outs):
        here = slice(i * SLOTS, (i + 1) * SLOTS)
        out[...] = jnp.concatenate([kept[here], got[here]], axis=0).astype(jnp.bfloat16)
    own_out[...] = got[len(outs) * SLOTS :].astype(jnp.bfloat16)


def expert_kernel(*refs):
    *rows, gate_ref, up_ref, down_ref, own_one, own_two, other_one, other_two = refs
    x = unpack(together(rows)).astype(jnp.bfloat16)
    gate_v = jnp.dot(x, gate_ref[...], preferred_element_type=jnp.float32)
    up_v = jnp.dot(x, up_ref[...], preferred_element_type=jnp.float32)
    hidden = (gate_v / (1.0 + jnp.exp(-gate_v)) * up_v).astype(jnp.bfloat16)
    part = jnp.dot(hidden, down_ref[...], preferred_element_type=jnp.float32)
    store((own_one, own_two, other_one, other_two), part)


def join_kernel(mine_ref, got_ref, *outs):
    store(outs, pack(mine_ref[...].astype(jnp.float32) + got_ref[...].astype(jnp.float32)))


def combine_kernel(first, mix_ref, *refs):
    *refs, out_hbm, out, sems = refs
    blocks = [r[...].astype(jnp.float32) for r in refs]
    if first:
        blocks = [b[at * SLOTS : (at + 1) * SLOTS] for b, at in zip(blocks, first)]
    rows = unpack(jnp.concatenate(blocks, axis=0)).astype(jnp.bfloat16)
    both = jnp.concatenate([rows, rows], axis=0)
    mix = mix_ref[...]
    part = out.shape[1] // OUT_PIECES
    copies = []
    for i in range(OUT_PIECES):
        here = pl.ds(i * part, part)
        out[:, here] = lax.dot_general(
            mix,
            both[:, i * part : (i + 1) * part],
            (((0,), (0,)), ((), ())),
            preferred_element_type=jnp.float32,
        ).astype(jnp.bfloat16)
        copies.append(pltpu.make_async_copy(out.at[:, here], out_hbm.at[:, here], sems.at[i]))
        copies[-1].start()
    for copy in copies:
        copy.wait()


def per_device(tokens, norm_gain, expert_ids, gate_weights, w_gate, w_up, w_down):
    owners = lax.axis_size("exp")
    flight = owners // 2
    count, width = tokens.shape
    few = relative(flight)

    def local(kernel, outs, name, *args, limit=16):
        return pl.pallas_call(
            kernel,
            out_shape=outs,
            in_specs=[VMEM] * len(args),
            out_specs=(VMEM,) * len(outs),
            compiler_params=pltpu.CompilerParams(vmem_limit_bytes=limit * 2**20),
            cost_estimate=SMALL,
            name=name,
        )(*args)

    def full(*counts):
        return tuple(jax.ShapeDtypeStruct((n * SLOTS, width), jnp.bfloat16) for n in counts)

    def packed(*counts):
        shapes = [(n * SLOTS, packed_width(width)) for n in counts]
        return tuple(jax.ShapeDtypeStruct(shape, jnp.bfloat16) for shape in shapes)

    def swap(rows):
        return lax.ppermute(rows, "exp", [(n, n ^ 1) for n in range(owners)])

    def travel(rows, distances, cross=0):
        pairs = [(n, n ^ (2 * distances[n % 2]) ^ cross) for n in range(owners)]
        return lax.ppermute(rows, "exp", pairs)

    def stage(*after):
        weights = w_gate[0], w_up[0], w_down[0]
        return pl.pallas_call(
            stage_kernel,
            out_shape=tuple(jax.ShapeDtypeStruct(w.shape, w.dtype) for w in weights),
            in_specs=[HBM] * 3 + [pl.BlockSpec(memory_space=pl.ANY)] * len(after),
            out_specs=(VMEM,) * 3,
            scratch_shapes=[pltpu.SemaphoreType.DMA((3 * PIECES,))],
            compiler_params=pltpu.CompilerParams(vmem_limit_bytes=16 * 2**20),
            cost_estimate=SMALL,
            name="stage",
        )(*in_hbm(*weights), *after)

    def experts(rows, weights):
        outs = full(*[flight // 2] * 4)
        return local(expert_kernel, outs, "experts", *rows, *weights, limit=24)

    def join(outs, mine, theirs):
        return local(join_kernel, packed(*outs), "join", mine, swap(theirs))

    def combine(mix, arrays, first):
        return pl.pallas_call(
            functools.partial(combine_kernel, first),
            out_shape=jax.ShapeDtypeStruct((count, width), jnp.bfloat16),
            in_specs=[VMEM] * (len(arrays) + 1),
            out_specs=HBM,
            scratch_shapes=[
                pltpu.VMEM((count, width), jnp.bfloat16),
                pltpu.SemaphoreType.DMA((OUT_PIECES,)),
            ],
            compiler_params=pltpu.CompilerParams(vmem_limit_bytes=24 * 2**20),
            name="combine",
        )(mix, *arrays)

    first = packed(3, 4, 1, 1) if few else packed(flight)
    mix, *outgoing = pl.pallas_call(
        functools.partial(dispatch_kernel, flight),
        out_shape=(jax.ShapeDtypeStruct((2 * flight * SLOTS, count), jnp.bfloat16),) + first,
        in_specs=[HBM] * 4,
        out_specs=(VMEM,) * (len(first) + 1),
        scratch_shapes=[
            pltpu.VMEM((count, width), jnp.bfloat16),
            pltpu.VMEM((1, width), jnp.float32),
            pltpu.VMEM(expert_ids.shape[::-1], jnp.int32),
            pltpu.VMEM(gate_weights.shape[::-1], jnp.float32),
            pltpu.VMEM((count, width), jnp.bfloat16),
            pltpu.SemaphoreType.DMA((3 + CHUNKS,)),
        ],
        compiler_params=pltpu.CompilerParams(vmem_limit_bytes=24 * 2**20),
        name="dispatch",
    )(*in_hbm(tokens, norm_gain, expert_ids.T, gate_weights.T))
    if not few:
        weights = stage()
        groups = [list(range(core, owners, 2)) for core in range(2)]
        exchange = functools.partial(
            lax.all_to_all,
            axis_name="exp",
            split_axis=0,
            concat_axis=0,
            axis_index_groups=groups,
            tiled=True,
        )
        own = exchange(outgoing[0])
        mine_one, mine_two, theirs_one, theirs_two = experts([own, swap(own)], weights)
        half = flight // 2
        (joined_one,) = join([half], mine_one, theirs_one)
        (joined_two,) = join([half], mine_two, theirs_two)
        return combine(mix, [exchange(jnp.concatenate([joined_one, joined_two]))], None)

    one, two, three = zip(*CARRIED)
    four = (SHARED, SHARED)
    kept, given, shared, own = outgoing
    *pairs, other_own = local(merge_kernel, packed(2, 2, 2, 1), "merge", kept, swap(given))
    shared = travel(shared, four)
    *pairs[1:], shared = lax.optimization_barrier((*pairs[1:], shared))
    pairs = [travel(a, r) for a, r in zip(pairs, (one, two, three))]
    weights = stage(pairs[0])
    pairs[1], *weights = lax.optimization_barrier((pairs[1], *weights))
    others = [swap(pairs[0]), swap(pairs[1]), swap(shared)]
    pairs[2], others[0], others[2] = lax.optimization_barrier((pairs[2], others[0], others[2]))
    rows = [*pairs, shared, own, *others[:2], swap(pairs[2]), others[2], other_own]
    mine_one, mine_two, theirs_one, theirs_two = experts(
        [rows[i] for i in (0, 3, 4, 1, 2, 5, 8, 9, 6, 7)], weights
    )

    first, shared, own = join((2, 1, 1), mine_one, theirs_one)
    second, third = join((2, 2), mine_two, theirs_two)
    first, shared = travel(first, one), travel(shared, four)
    second, third, shared = lax.optimization_barrier((second, third, shared))
    pairs = [first, travel(second, two), travel(third, three)]
    arrays = [*pairs, *[swap(a) for a in pairs], shared, own]
    return combine(mix, arrays, (0, 0, 0, 1, 1, 1, 0, 0))


def solution(mesh):
    placed = (
        P(("group", "exp"), None),
        P(),
        P(("group", "exp"), None),
        P(("group", "exp"), None),
        P("exp", None, None),
        P("exp", None, None),
        P("exp", None, None),
    )
    return jax.shard_map(
        per_device, mesh=mesh, in_specs=placed, out_specs=P(("group", "exp"), None), check_vma=False
    )
```

```python
import functools

import jax
import jax.numpy as jnp
from jax import lax
from jax.experimental import pallas as pl
from jax.experimental.pallas import tpu as pltpu
from jax.sharding import PartitionSpec as P

SLOTS = 8
CHUNKS = 4
PIECES = 4
OUT_PIECES = 4
LANES = 128

VMEM = pl.BlockSpec(memory_space=pltpu.VMEM)
SMALL = pl.CostEstimate(flops=1, bytes_accessed=1, transcendentals=0)
HBM = pl.BlockSpec(memory_space=pltpu.HBM)


def in_hbm(*arrays):
    return [pltpu.with_memory_space_constraint(a, pltpu.HBM) for a in arrays]


def relative(flight):
    return flight == 8


CARRIED = ((4, 1, 5), (6, 2, 7))
SHARED = 3


def block_order(flight, core):
    if not relative(flight):
        return range(flight)
    return CARRIED[core] + CARRIED[1 - core] + (SHARED, 0)


def packed_width(width):
    return width // 7 * 6 + LANES


def pack(rows):
    blocks = rows.reshape(-1, SLOTS, rows.shape[1])
    tail = rows.shape[1] // 7
    main = blocks[:, :, : 6 * tail]
    moved = jnp.concatenate([blocks[:, j : j + 1, 6 * tail :] for j in range(6)], axis=2)
    row = lax.broadcasted_iota(jnp.int32, main.shape, 1)
    main = jnp.where(row == SLOTS - 1, moved, main)
    row = row[:, :, :LANES]
    extra = jnp.zeros(row.shape, rows.dtype)
    for k in range(tail // LANES):
        start = 6 * tail + k * LANES
        extra = jnp.where(row == k, blocks[:, 6:7, start : start + LANES], extra)
    return jnp.concatenate([main, extra], axis=2).reshape(rows.shape[0], -1)


def unpack(packed):
    blocks = packed.reshape(-1, SLOTS, packed.shape[1])
    tail = (packed.shape[1] - LANES) // 6
    main = blocks[:, :, : 6 * tail]
    last = jnp.concatenate(
        [blocks[:, k : k + 1, 6 * tail :] for k in range(tail // LANES)], axis=2
    )
    row = lax.broadcasted_iota(jnp.int32, (blocks.shape[0], SLOTS, tail), 1)
    end = jnp.where(row == 6, last, 0.0)
    for j in range(6):
        end = jnp.where(row == j, blocks[:, 7:8, j * tail : (j + 1) * tail], end)
    return jnp.concatenate([main, end], axis=2).reshape(packed.shape[0], -1)


def store(refs, rows):
    at = 0
    for ref in refs:
        ref[...] = rows[at : at + ref.shape[0]].astype(ref.dtype)
        at += ref.shape[0]


def dispatch_kernel(flight, tok_hbm, gain_hbm, ids_hbm, gw_hbm, mix_ref, *rest):
    *outs, tok, gain, ids, gw, normed, sems = rest
    count = tok.shape[0]
    part = count // CHUNKS
    small = [
        pltpu.make_async_copy(ids_hbm, ids, sems.at[0]),
        pltpu.make_async_copy(gw_hbm, gw, sems.at[1]),
        pltpu.make_async_copy(gain_hbm, gain.at[0], sems.at[2]),
    ]
    large = [
        pltpu.make_async_copy(
            tok_hbm.at[pl.ds(i * part, part)], tok.at[pl.ds(i * part, part)], sems.at[3 + i]
        )
        for i in range(CHUNKS)
    ]
    for copy in small + large:
        copy.start()
    small[0].wait()
    small[1].wait()
    experts = lax.broadcasted_iota(jnp.int32, (flight, count), 0)
    if relative(flight):
        place = experts
        me = lax.axis_index("exp")
        for i, (even, odd) in enumerate(zip(block_order(flight, 0), block_order(flight, 1))):
            experts = jnp.where(place == i, jnp.where(me % 2 == 0, even, odd) ^ (me // 2), experts)
    chosen = jnp.zeros((flight, count), jnp.float32)
    gates = jnp.zeros((flight, count), jnp.float32)
    for k in range(ids.shape[0]):
        hit = ids[k : k + 1, :] == experts
        chosen = jnp.where(hit, 1.0, chosen)
        gates = jnp.where(hit, gw[k : k + 1, :], gates)
    before = (
        lax.broadcasted_iota(jnp.int32, (count, count), 0)
        < lax.broadcasted_iota(jnp.int32, (count, count), 1)
    ).astype(jnp.bfloat16)
    rank = jnp.dot(chosen.astype(jnp.bfloat16), before, preferred_element_type=jnp.float32)
    rank = jnp.where(chosen > 0.0, rank, -1.0)

    slot = lax.broadcasted_iota(jnp.int32, (flight, SLOTS, count), 1).astype(jnp.float32)
    taken = rank[:, None, :] == slot
    pick = jnp.where(taken, 1.0, 0.0).reshape(flight * SLOTS, count).astype(jnp.bfloat16)
    mix = jnp.where(taken, gates[:, None, :], 0.0).reshape(flight * SLOTS, count)
    high = mix.astype(jnp.bfloat16)
    mix_ref[: flight * SLOTS, :] = high
    mix_ref[flight * SLOTS :, :] = (mix - high.astype(jnp.float32)).astype(jnp.bfloat16)

    small[2].wait()
    for i in range(CHUNKS):
        large[i].wait()
        wide = tok[pl.ds(i * part, part), :].astype(jnp.float32)
        mean_square = jnp.mean(wide * wide, axis=1, keepdims=True)
        normed[pl.ds(i * part, part), :] = (
            wide * lax.rsqrt(mean_square + 1e-06) * gain[...]
        ).astype(jnp.bfloat16)
    rows = jnp.dot(pick, normed[...], preferred_element_type=jnp.float32)
    blocks = pack(rows)
    if len(outs) == 1:
        store(outs, blocks)
    else:
        kept, given = 3 * SLOTS, 6 * SLOTS
        store(outs[:1], blocks[:kept])
        store(outs[1:2], jnp.concatenate([blocks[kept:given], blocks[given + SLOTS :]], axis=0))
        store(outs[2:], blocks[given:])


def stage_kernel(*refs):
    *refs, sems = refs
    sources, targets = refs[:3], refs[3:]
    copies = []
    for at, (source, target) in enumerate(zip(sources, targets)):
        rows = source.shape[0] // PIECES
        for i in range(PIECES):
            here = pl.ds(i * rows, rows)
            copies.append(
                pltpu.make_async_copy(source.at[here], target.at[here], sems.at[at * PIECES + i])
            )
    for copy in copies:
        copy.start()
    for copy in copies:
        copy.wait()


def together(refs):
    return jnp.concatenate([b[...].astype(jnp.float32) for b in refs], axis=0)


def merge_kernel(kept_ref, got_ref, *outs):
    *outs, own_out = outs
    kept, got = kept_ref[...].astype(jnp.float32), got_ref[...].astype(jnp.float32)
    for i, out in enumerate(outs):
        here = slice(i * SLOTS, (i + 1) * SLOTS)
        out[...] = jnp.concatenate([kept[here], got[here]], axis=0).astype(jnp.bfloat16)
    own_out[...] = got[len(outs) * SLOTS :].astype(jnp.bfloat16)


def gather_kernel(*refs):
    refs[-1][...] = together(refs[:-1]).astype(jnp.bfloat16)


def sift_kernel(*refs):
    *refs, out_ref = refs
    blocks = [r[...].astype(jnp.float32)[SLOTS:] for r in refs]
    out_ref[...] = jnp.concatenate(blocks, axis=0).astype(jnp.bfloat16)


def expert_kernel(*refs):
    *rows, gate_ref, up_ref, down_ref, own_one, own_two, other_one, other_two = refs
    x = unpack(together(rows)).astype(jnp.bfloat16)
    gate_v = jnp.dot(x, gate_ref[...], preferred_element_type=jnp.float32)
    up_v = jnp.dot(x, up_ref[...], preferred_element_type=jnp.float32)
    hidden = (gate_v / (1.0 + jnp.exp(-gate_v)) * up_v).astype(jnp.bfloat16)
    part = jnp.dot(hidden, down_ref[...], preferred_element_type=jnp.float32)
    store((own_one, own_two, other_one, other_two), part)


def join_kernel(mine_ref, got_ref, *outs):
    store(outs, pack(mine_ref[...].astype(jnp.float32) + got_ref[...].astype(jnp.float32)))


def combine_kernel(paired, mix_ref, *refs):
    *refs, out_hbm, out, sems = refs
    blocks = [r[...].astype(jnp.float32) for r in refs]
    if paired:
        blocks[:3] = [b[:SLOTS] for b in blocks[:3]]
    rows = unpack(jnp.concatenate(blocks, axis=0)).astype(jnp.bfloat16)
    both = jnp.concatenate([rows, rows], axis=0)
    mix = mix_ref[...]
    part = out.shape[1] // OUT_PIECES
    copies = []
    for i in range(OUT_PIECES):
        here = pl.ds(i * part, part)
        out[:, here] = lax.dot_general(
            mix,
            both[:, i * part : (i + 1) * part],
            (((0,), (0,)), ((), ())),
            preferred_element_type=jnp.float32,
        ).astype(jnp.bfloat16)
        copies.append(pltpu.make_async_copy(out.at[:, here], out_hbm.at[:, here], sems.at[i]))
        copies[-1].start()
    for copy in copies:
        copy.wait()


def per_device(tokens, norm_gain, expert_ids, gate_weights, w_gate, w_up, w_down):
    owners = lax.axis_size("exp")
    flight = owners // 2
    count, width = tokens.shape
    few = relative(flight)

    def local(kernel, outs, name, *args, limit=16):
        return pl.pallas_call(
            kernel,
            out_shape=outs,
            in_specs=[VMEM] * len(args),
            out_specs=(VMEM,) * len(outs),
            compiler_params=pltpu.CompilerParams(vmem_limit_bytes=limit * 2**20),
            cost_estimate=SMALL,
            name=name,
        )(*args)

    def full(*counts):
        return tuple(jax.ShapeDtypeStruct((n * SLOTS, width), jnp.bfloat16) for n in counts)

    def packed(*counts):
        shapes = [(n * SLOTS, packed_width(width)) for n in counts]
        return tuple(jax.ShapeDtypeStruct(shape, jnp.bfloat16) for shape in shapes)

    def swap(rows):
        return lax.ppermute(rows, "exp", [(n, n ^ 1) for n in range(owners)])

    def travel(rows, distances, cross=0):
        pairs = [(n, n ^ (2 * distances[n % 2]) ^ cross) for n in range(owners)]
        return lax.ppermute(rows, "exp", pairs)

    def stage():
        weights = w_gate[0], w_up[0], w_down[0]
        return pl.pallas_call(
            stage_kernel,
            out_shape=tuple(jax.ShapeDtypeStruct(w.shape, w.dtype) for w in weights),
            in_specs=[HBM] * 3,
            out_specs=(VMEM,) * 3,
            scratch_shapes=[pltpu.SemaphoreType.DMA((3 * PIECES,))],
            compiler_params=pltpu.CompilerParams(vmem_limit_bytes=16 * 2**20),
            cost_estimate=SMALL,
            name="stage",
        )(*in_hbm(*weights))

    def experts(rows, weights):
        outs = full(*[flight // 2] * 4)
        return local(expert_kernel, outs, "experts", *rows, *weights, limit=24)

    def join(outs, mine, theirs):
        return local(join_kernel, packed(*outs), "join", mine, swap(theirs))

    def combine(mix, arrays, paired):
        return pl.pallas_call(
            functools.partial(combine_kernel, paired),
            out_shape=jax.ShapeDtypeStruct((count, width), jnp.bfloat16),
            in_specs=[VMEM] * (len(arrays) + 1),
            out_specs=HBM,
            scratch_shapes=[
                pltpu.VMEM((count, width), jnp.bfloat16),
                pltpu.SemaphoreType.DMA((OUT_PIECES,)),
            ],
            compiler_params=pltpu.CompilerParams(vmem_limit_bytes=24 * 2**20),
            name="combine",
        )(mix, *arrays)

    first = packed(3, 4, 1, 1) if few else packed(flight)
    mix, *outgoing = pl.pallas_call(
        functools.partial(dispatch_kernel, flight),
        out_shape=(jax.ShapeDtypeStruct((2 * flight * SLOTS, count), jnp.bfloat16),) + first,
        in_specs=[HBM] * 4,
        out_specs=(VMEM,) * (len(first) + 1),
        scratch_shapes=[
            pltpu.VMEM((count, width), jnp.bfloat16),
            pltpu.VMEM((1, width), jnp.float32),
            pltpu.VMEM(expert_ids.shape[::-1], jnp.int32),
            pltpu.VMEM(gate_weights.shape[::-1], jnp.float32),
            pltpu.VMEM((count, width), jnp.bfloat16),
            pltpu.SemaphoreType.DMA((3 + CHUNKS,)),
        ],
        compiler_params=pltpu.CompilerParams(vmem_limit_bytes=24 * 2**20),
        name="dispatch",
    )(*in_hbm(tokens, norm_gain, expert_ids.T, gate_weights.T))
    if not few:
        weights = stage()
        groups = [list(range(core, owners, 2)) for core in range(2)]
        exchange = functools.partial(
            lax.all_to_all,
            axis_name="exp",
            split_axis=0,
            concat_axis=0,
            axis_index_groups=groups,
            tiled=True,
        )
        own = exchange(outgoing[0])
        mine_one, mine_two, theirs_one, theirs_two = experts([own, swap(own)], weights)
        half = flight // 2
        (joined_one,) = join([half], mine_one, theirs_one)
        (joined_two,) = join([half], mine_two, theirs_two)
        return combine(mix, [exchange(jnp.concatenate([joined_one, joined_two]))], False)

    one, two, three = zip(*CARRIED)
    four = (SHARED, SHARED)
    kept, given, shared, own = outgoing
    *pairs, other_own = local(merge_kernel, packed(2, 2, 2, 1), "merge", kept, swap(given))
    shared = travel(shared, four)
    arrived = [travel(a, r) for a, r in zip(pairs, (one, two, three))] + [shared]
    *arrived, gate, up, down = lax.optimization_barrier((*arrived, *stage()))
    (rows,) = local(gather_kernel, packed(7), "gather", *arrived)
    mine_one, mine_two, theirs_one, theirs_two = experts(
        (rows, own, swap(rows), other_own), (gate, up, down)
    )

    first, second = join((2, 2), mine_one, theirs_one)
    third, shared, own = join((2, 1, 1), mine_two, theirs_two)
    arrived = [
        travel(a, r) for a, r in zip((first, second, third, shared), (one, two, three, four))
    ]
    *pairs, shared = lax.optimization_barrier(tuple(arrived))
    (others,) = local(sift_kernel, packed(3), "sift", *pairs)
    return combine(mix, [*pairs, swap(others), shared, own], True)


def solution(mesh):
    placed = (
        P(("group", "exp"), None),
        P(),
        P(("group", "exp"), None),
        P(("group", "exp"), None),
        P("exp", None, None),
        P("exp", None, None),
        P("exp", None, None),
    )
    return jax.shard_map(
        per_device, mesh=mesh, in_specs=placed, out_specs=P(("group", "exp"), None), check_vma=False
    )
```

```python
import functools

import jax
import jax.numpy as jnp
from jax import lax
from jax.experimental import pallas as pl
from jax.experimental.pallas import tpu as pltpu
from jax.sharding import PartitionSpec as P

SLOTS = 8
CHUNKS = 4
PIECES = 4
OUT_PIECES = 4
LANES = 128

VMEM = pl.BlockSpec(memory_space=pltpu.VMEM)
SMALL = pl.CostEstimate(flops=1, bytes_accessed=1, transcendentals=0)
HBM = pl.BlockSpec(memory_space=pltpu.HBM)


def in_hbm(*arrays):
    return [pltpu.with_memory_space_constraint(a, pltpu.HBM) for a in arrays]


def relative(flight):
    return flight == 8


CARRIED = ((4, 5, 1), (2, 6, 7))
SHARED = 3


def block_order(flight, core):
    if not relative(flight):
        return range(flight)
    return CARRIED[core] + CARRIED[1 - core] + (SHARED, 0)


def packed_width(width):
    return width // 7 * 6 + LANES


def pack(rows):
    blocks = rows.reshape(-1, SLOTS, rows.shape[1])
    tail = rows.shape[1] // 7
    main = blocks[:, :, : 6 * tail]
    moved = jnp.concatenate([blocks[:, j : j + 1, 6 * tail :] for j in range(6)], axis=2)
    row = lax.broadcasted_iota(jnp.int32, main.shape, 1)
    main = jnp.where(row == SLOTS - 1, moved, main)
    row = row[:, :, :LANES]
    extra = jnp.zeros(row.shape, rows.dtype)
    for k in range(tail // LANES):
        start = 6 * tail + k * LANES
        extra = jnp.where(row == k, blocks[:, 6:7, start : start + LANES], extra)
    return jnp.concatenate([main, extra], axis=2).reshape(rows.shape[0], -1)


def unpack(packed):
    blocks = packed.reshape(-1, SLOTS, packed.shape[1])
    tail = (packed.shape[1] - LANES) // 6
    main = blocks[:, :, : 6 * tail]
    last = jnp.concatenate(
        [blocks[:, k : k + 1, 6 * tail :] for k in range(tail // LANES)], axis=2
    )
    row = lax.broadcasted_iota(jnp.int32, (blocks.shape[0], SLOTS, tail), 1)
    end = jnp.where(row == 6, last, 0.0)
    for j in range(6):
        end = jnp.where(row == j, blocks[:, 7:8, j * tail : (j + 1) * tail], end)
    return jnp.concatenate([main, end], axis=2).reshape(packed.shape[0], -1)


def store(refs, rows):
    at = 0
    for ref in refs:
        ref[...] = rows[at : at + ref.shape[0]].astype(ref.dtype)
        at += ref.shape[0]


def dispatch_kernel(flight, tok_hbm, gain_hbm, ids_hbm, gw_hbm, mix_ref, *rest):
    *outs, tok, gain, ids, gw, normed, sems = rest
    count = tok.shape[0]
    part = count // CHUNKS
    small = [
        pltpu.make_async_copy(ids_hbm, ids, sems.at[0]),
        pltpu.make_async_copy(gw_hbm, gw, sems.at[1]),
        pltpu.make_async_copy(gain_hbm, gain.at[0], sems.at[2]),
    ]
    large = [
        pltpu.make_async_copy(
            tok_hbm.at[pl.ds(i * part, part)], tok.at[pl.ds(i * part, part)], sems.at[3 + i]
        )
        for i in range(CHUNKS)
    ]
    for copy in small + large:
        copy.start()
    small[0].wait()
    small[1].wait()
    experts = lax.broadcasted_iota(jnp.int32, (flight, count), 0)
    if relative(flight):
        place = experts
        me = lax.axis_index("exp")
        for i, (even, odd) in enumerate(zip(block_order(flight, 0), block_order(flight, 1))):
            experts = jnp.where(place == i, jnp.where(me % 2 == 0, even, odd) ^ (me // 2), experts)
    chosen = jnp.zeros((flight, count), jnp.float32)
    gates = jnp.zeros((flight, count), jnp.float32)
    for k in range(ids.shape[0]):
        hit = ids[k : k + 1, :] == experts
        chosen = jnp.where(hit, 1.0, chosen)
        gates = jnp.where(hit, gw[k : k + 1, :], gates)
    before = (
        lax.broadcasted_iota(jnp.int32, (count, count), 0)
        < lax.broadcasted_iota(jnp.int32, (count, count), 1)
    ).astype(jnp.bfloat16)
    rank = jnp.dot(chosen.astype(jnp.bfloat16), before, preferred_element_type=jnp.float32)
    rank = jnp.where(chosen > 0.0, rank, -1.0)

    slot = lax.broadcasted_iota(jnp.int32, (flight, SLOTS, count), 1).astype(jnp.float32)
    taken = rank[:, None, :] == slot
    pick = jnp.where(taken, 1.0, 0.0).reshape(flight * SLOTS, count).astype(jnp.bfloat16)
    mix = jnp.where(taken, gates[:, None, :], 0.0).reshape(flight * SLOTS, count)
    high = mix.astype(jnp.bfloat16)
    mix_ref[: flight * SLOTS, :] = high
    mix_ref[flight * SLOTS :, :] = (mix - high.astype(jnp.float32)).astype(jnp.bfloat16)

    small[2].wait()
    for i in range(CHUNKS):
        large[i].wait()
        wide = tok[pl.ds(i * part, part), :].astype(jnp.float32)
        mean_square = jnp.mean(wide * wide, axis=1, keepdims=True)
        normed[pl.ds(i * part, part), :] = (
            wide * lax.rsqrt(mean_square + 1e-06) * gain[...]
        ).astype(jnp.bfloat16)
    rows = jnp.dot(pick, normed[...], preferred_element_type=jnp.float32)
    blocks = pack(rows)
    if len(outs) == 1:
        store(outs, blocks)
    else:
        kept, given = 3 * SLOTS, 6 * SLOTS
        store(outs[:1], blocks[:kept])
        store(outs[1:2], jnp.concatenate([blocks[kept:given], blocks[given + SLOTS :]], axis=0))
        store(outs[2:], blocks[given:])


def stage_kernel(*refs):
    *refs, sems = refs
    sources, targets = refs[:3], refs[3:]
    copies = []
    for at, (source, target) in enumerate(zip(sources, targets)):
        rows = source.shape[0] // PIECES
        for i in range(PIECES):
            here = pl.ds(i * rows, rows)
            copies.append(
                pltpu.make_async_copy(source.at[here], target.at[here], sems.at[at * PIECES + i])
            )
    for copy in copies:
        copy.start()
    for copy in copies:
        copy.wait()


def together(refs):
    return jnp.concatenate([b[...].astype(jnp.float32) for b in refs], axis=0)


def merge_kernel(kept_ref, got_ref, *outs):
    *outs, own_out = outs
    kept, got = kept_ref[...].astype(jnp.float32), got_ref[...].astype(jnp.float32)
    for i, out in enumerate(outs):
        here = slice(i * SLOTS, (i + 1) * SLOTS)
        out[...] = jnp.concatenate([kept[here], got[here]], axis=0).astype(jnp.bfloat16)
    own_out[...] = got[len(outs) * SLOTS :].astype(jnp.bfloat16)


def gather_kernel(*refs):
    refs[-1][...] = together(refs[:-1]).astype(jnp.bfloat16)


def sift_kernel(*refs):
    *refs, out_ref = refs
    blocks = [r[...].astype(jnp.float32)[SLOTS:] for r in refs]
    out_ref[...] = jnp.concatenate(blocks, axis=0).astype(jnp.bfloat16)


def expert_kernel(*refs):
    *rows, gate_ref, up_ref, down_ref, own_one, own_two, other_one, other_two = refs
    x = unpack(together(rows)).astype(jnp.bfloat16)
    gate_v = jnp.dot(x, gate_ref[...], preferred_element_type=jnp.float32)
    up_v = jnp.dot(x, up_ref[...], preferred_element_type=jnp.float32)
    hidden = (gate_v / (1.0 + jnp.exp(-gate_v)) * up_v).astype(jnp.bfloat16)
    part = jnp.dot(hidden, down_ref[...], preferred_element_type=jnp.float32)
    store((own_one, own_two, other_one, other_two), part)


def join_kernel(mine_ref, got_ref, *outs):
    store(outs, pack(mine_ref[...].astype(jnp.float32) + got_ref[...].astype(jnp.float32)))


def combine_kernel(paired, mix_ref, *refs):
    *refs, out_hbm, out, sems = refs
    blocks = [r[...].astype(jnp.float32) for r in refs]
    if paired:
        blocks[:3] = [b[:SLOTS] for b in blocks[:3]]
    rows = unpack(jnp.concatenate(blocks, axis=0)).astype(jnp.bfloat16)
    both = jnp.concatenate([rows, rows], axis=0)
    mix = mix_ref[...]
    part = out.shape[1] // OUT_PIECES
    copies = []
    for i in range(OUT_PIECES):
        here = pl.ds(i * part, part)
        out[:, here] = lax.dot_general(
            mix,
            both[:, i * part : (i + 1) * part],
            (((0,), (0,)), ((), ())),
            preferred_element_type=jnp.float32,
        ).astype(jnp.bfloat16)
        copies.append(pltpu.make_async_copy(out.at[:, here], out_hbm.at[:, here], sems.at[i]))
        copies[-1].start()
    for copy in copies:
        copy.wait()


def per_device(tokens, norm_gain, expert_ids, gate_weights, w_gate, w_up, w_down):
    owners = lax.axis_size("exp")
    flight = owners // 2
    count, width = tokens.shape
    few = relative(flight)

    def local(kernel, outs, name, *args, limit=16):
        return pl.pallas_call(
            kernel,
            out_shape=outs,
            in_specs=[VMEM] * len(args),
            out_specs=(VMEM,) * len(outs),
            compiler_params=pltpu.CompilerParams(vmem_limit_bytes=limit * 2**20),
            cost_estimate=SMALL,
            name=name,
        )(*args)

    def full(*counts):
        return tuple(jax.ShapeDtypeStruct((n * SLOTS, width), jnp.bfloat16) for n in counts)

    def packed(*counts):
        shapes = [(n * SLOTS, packed_width(width)) for n in counts]
        return tuple(jax.ShapeDtypeStruct(shape, jnp.bfloat16) for shape in shapes)

    def swap(rows):
        return lax.ppermute(rows, "exp", [(n, n ^ 1) for n in range(owners)])

    def travel(rows, distances, cross=0):
        pairs = [(n, n ^ (2 * distances[n % 2]) ^ cross) for n in range(owners)]
        return lax.ppermute(rows, "exp", pairs)

    def stage():
        weights = w_gate[0], w_up[0], w_down[0]
        return pl.pallas_call(
            stage_kernel,
            out_shape=tuple(jax.ShapeDtypeStruct(w.shape, w.dtype) for w in weights),
            in_specs=[HBM] * 3,
            out_specs=(VMEM,) * 3,
            scratch_shapes=[pltpu.SemaphoreType.DMA((3 * PIECES,))],
            compiler_params=pltpu.CompilerParams(vmem_limit_bytes=16 * 2**20),
            cost_estimate=SMALL,
            name="stage",
        )(*in_hbm(*weights))

    def experts(rows, weights):
        outs = full(*[flight // 2] * 4)
        return local(expert_kernel, outs, "experts", *rows, *weights, limit=24)

    def join(outs, mine, theirs):
        return local(join_kernel, packed(*outs), "join", mine, swap(theirs))

    def combine(mix, arrays, paired):
        return pl.pallas_call(
            functools.partial(combine_kernel, paired),
            out_shape=jax.ShapeDtypeStruct((count, width), jnp.bfloat16),
            in_specs=[VMEM] * (len(arrays) + 1),
            out_specs=HBM,
            scratch_shapes=[
                pltpu.VMEM((count, width), jnp.bfloat16),
                pltpu.SemaphoreType.DMA((OUT_PIECES,)),
            ],
            compiler_params=pltpu.CompilerParams(vmem_limit_bytes=24 * 2**20),
            name="combine",
        )(mix, *arrays)

    first = packed(3, 4, 1, 1) if few else packed(flight)
    mix, *outgoing = pl.pallas_call(
        functools.partial(dispatch_kernel, flight),
        out_shape=(jax.ShapeDtypeStruct((2 * flight * SLOTS, count), jnp.bfloat16),) + first,
        in_specs=[HBM] * 4,
        out_specs=(VMEM,) * (len(first) + 1),
        scratch_shapes=[
            pltpu.VMEM((count, width), jnp.bfloat16),
            pltpu.VMEM((1, width), jnp.float32),
            pltpu.VMEM(expert_ids.shape[::-1], jnp.int32),
            pltpu.VMEM(gate_weights.shape[::-1], jnp.float32),
            pltpu.VMEM((count, width), jnp.bfloat16),
            pltpu.SemaphoreType.DMA((3 + CHUNKS,)),
        ],
        compiler_params=pltpu.CompilerParams(vmem_limit_bytes=24 * 2**20),
        name="dispatch",
    )(*in_hbm(tokens, norm_gain, expert_ids.T, gate_weights.T))
    if not few:
        weights = stage()
        groups = [list(range(core, owners, 2)) for core in range(2)]
        exchange = functools.partial(
            lax.all_to_all,
            axis_name="exp",
            split_axis=0,
            concat_axis=0,
            axis_index_groups=groups,
            tiled=True,
        )
        own = exchange(outgoing[0])
        mine_one, mine_two, theirs_one, theirs_two = experts([own, swap(own)], weights)
        half = flight // 2
        (joined_one,) = join([half], mine_one, theirs_one)
        (joined_two,) = join([half], mine_two, theirs_two)
        return combine(mix, [exchange(jnp.concatenate([joined_one, joined_two]))], False)

    one, two, three = zip(*CARRIED)
    four = (SHARED, SHARED)
    kept, given, shared, own = outgoing
    *pairs, other_own = local(merge_kernel, packed(2, 2, 2, 1), "merge", kept, swap(given))
    shared = travel(shared, four)
    arrived = [travel(a, r) for a, r in zip(pairs, (one, two, three))] + [shared]
    *arrived, gate, up, down = lax.optimization_barrier((*arrived, *stage()))
    (rows,) = local(gather_kernel, packed(7), "gather", *arrived)
    mine_one, mine_two, theirs_one, theirs_two = experts(
        (rows, own, swap(rows), other_own), (gate, up, down)
    )

    first, second = join((2, 2), mine_one, theirs_one)
    third, shared, own = join((2, 1, 1), mine_two, theirs_two)
    arrived = [
        travel(a, r) for a, r in zip((first, second, third, shared), (one, two, three, four))
    ]
    *pairs, shared = lax.optimization_barrier(tuple(arrived))
    (others,) = local(sift_kernel, packed(3), "sift", *pairs)
    return combine(mix, [*pairs, swap(others), shared, own], True)


def solution(mesh):
    placed = (
        P(("group", "exp"), None),
        P(),
        P(("group", "exp"), None),
        P(("group", "exp"), None),
        P("exp", None, None),
        P("exp", None, None),
        P("exp", None, None),
    )
    return jax.shard_map(
        per_device, mesh=mesh, in_specs=placed, out_specs=P(("group", "exp"), None), check_vma=False
    )
```

```python
import functools

import jax
import jax.numpy as jnp
from jax import lax
from jax.experimental import pallas as pl
from jax.experimental.pallas import tpu as pltpu
from jax.sharding import PartitionSpec as P

SLOTS = 8
CHUNKS = 4
PIECES = 4
OUT_PIECES = 4
LANES = 128

VMEM = pl.BlockSpec(memory_space=pltpu.VMEM)
SMALL = pl.CostEstimate(flops=1, bytes_accessed=1, transcendentals=0)
HBM = pl.BlockSpec(memory_space=pltpu.HBM)


def in_hbm(*arrays):
    return [pltpu.with_memory_space_constraint(a, pltpu.HBM) for a in arrays]


def relative(flight):
    return flight == 8


CARRIED = ((4, 1, 5), (6, 2, 7))
SHARED = 3


def block_order(flight, core):
    if not relative(flight):
        return range(flight)
    return CARRIED[core] + CARRIED[1 - core] + (SHARED, 0)


def packed_width(width):
    return width // 7 * 6 + LANES


def pack(rows):
    blocks = rows.reshape(-1, SLOTS, rows.shape[1])
    tail = rows.shape[1] // 7
    main = blocks[:, :, : 6 * tail]
    moved = jnp.concatenate([blocks[:, j : j + 1, 6 * tail :] for j in range(6)], axis=2)
    row = lax.broadcasted_iota(jnp.int32, main.shape, 1)
    main = jnp.where(row == SLOTS - 1, moved, main)
    row = row[:, :, :LANES]
    extra = jnp.zeros(row.shape, rows.dtype)
    for k in range(tail // LANES):
        start = 6 * tail + k * LANES
        extra = jnp.where(row == k, blocks[:, 6:7, start : start + LANES], extra)
    return jnp.concatenate([main, extra], axis=2).reshape(rows.shape[0], -1)


def unpack(packed):
    blocks = packed.reshape(-1, SLOTS, packed.shape[1])
    tail = (packed.shape[1] - LANES) // 6
    main = blocks[:, :, : 6 * tail]
    last = jnp.concatenate(
        [blocks[:, k : k + 1, 6 * tail :] for k in range(tail // LANES)], axis=2
    )
    row = lax.broadcasted_iota(jnp.int32, (blocks.shape[0], SLOTS, tail), 1)
    end = jnp.where(row == 6, last, 0.0)
    for j in range(6):
        end = jnp.where(row == j, blocks[:, 7:8, j * tail : (j + 1) * tail], end)
    return jnp.concatenate([main, end], axis=2).reshape(packed.shape[0], -1)


def store(refs, rows):
    at = 0
    for ref in refs:
        ref[...] = rows[at : at + ref.shape[0]].astype(ref.dtype)
        at += ref.shape[0]


def dispatch_kernel(flight, tok_hbm, gain_hbm, ids_hbm, gw_hbm, mix_ref, *rest):
    *outs, tok, gain, ids, gw, sems = rest
    count = tok.shape[0]
    part = count // CHUNKS
    small = [
        pltpu.make_async_copy(ids_hbm, ids, sems.at[0]),
        pltpu.make_async_copy(gw_hbm, gw, sems.at[1]),
        pltpu.make_async_copy(gain_hbm, gain.at[0], sems.at[2]),
    ]
    large = [
        pltpu.make_async_copy(
            tok_hbm.at[pl.ds(i * part, part)], tok.at[pl.ds(i * part, part)], sems.at[3 + i]
        )
        for i in range(CHUNKS)
    ]
    for copy in small + large:
        copy.start()
    small[0].wait()
    small[1].wait()
    experts = lax.broadcasted_iota(jnp.int32, (flight, count), 0)
    if relative(flight):
        place = experts
        me = lax.axis_index("exp")
        for i, (even, odd) in enumerate(zip(block_order(flight, 0), block_order(flight, 1))):
            experts = jnp.where(place == i, jnp.where(me % 2 == 0, even, odd) ^ (me // 2), experts)
    chosen = jnp.zeros((flight, count), jnp.float32)
    gates = jnp.zeros((flight, count), jnp.float32)
    for k in range(ids.shape[0]):
        hit = ids[k : k + 1, :] == experts
        chosen = jnp.where(hit, 1.0, chosen)
        gates = jnp.where(hit, gw[k : k + 1, :], gates)
    before = (
        lax.broadcasted_iota(jnp.int32, (count, count), 0)
        < lax.broadcasted_iota(jnp.int32, (count, count), 1)
    ).astype(jnp.bfloat16)
    rank = jnp.dot(chosen.astype(jnp.bfloat16), before, preferred_element_type=jnp.float32)
    rank = jnp.where(chosen > 0.0, rank, -1.0)

    slot = lax.broadcasted_iota(jnp.int32, (flight, SLOTS, count), 1).astype(jnp.float32)
    taken = rank[:, None, :] == slot
    pick = jnp.where(taken, 1.0, 0.0).reshape(flight * SLOTS, count).astype(jnp.bfloat16)
    mix = jnp.where(taken, gates[:, None, :], 0.0).reshape(flight * SLOTS, count)
    high = mix.astype(jnp.bfloat16)
    mix_ref[: flight * SLOTS, :] = high
    mix_ref[flight * SLOTS :, :] = (mix - high.astype(jnp.float32)).astype(jnp.bfloat16)

    for copy in large:
        copy.wait()
    wide = jnp.dot(pick, tok[...], preferred_element_type=jnp.float32)
    mean_square = jnp.mean(wide * wide, axis=1, keepdims=True)
    small[2].wait()
    rows = (wide * lax.rsqrt(mean_square + 1e-06) * gain[...]).astype(jnp.bfloat16)
    rows = rows.astype(jnp.float32)
    blocks = pack(rows)
    if len(outs) == 1:
        store(outs, blocks)
    else:
        kept, given = 3 * SLOTS, 6 * SLOTS
        store(outs[:1], blocks[:kept])
        store(outs[1:2], jnp.concatenate([blocks[kept:given], blocks[given + SLOTS :]], axis=0))
        store(outs[2:], blocks[given:])


def stage_kernel(*refs):
    *refs, sems = refs
    sources, targets = refs[:3], refs[3:]
    copies = []
    for at, (source, target) in enumerate(zip(sources, targets)):
        rows = source.shape[0] // PIECES
        for i in range(PIECES):
            here = pl.ds(i * rows, rows)
            copies.append(
                pltpu.make_async_copy(source.at[here], target.at[here], sems.at[at * PIECES + i])
            )
    for copy in copies:
        copy.start()
    for copy in copies:
        copy.wait()


def together(refs):
    return jnp.concatenate([b[...].astype(jnp.float32) for b in refs], axis=0)


def merge_kernel(kept_ref, got_ref, *outs):
    *outs, own_out = outs
    kept, got = kept_ref[...].astype(jnp.float32), got_ref[...].astype(jnp.float32)
    for i, out in enumerate(outs):
        here = slice(i * SLOTS, (i + 1) * SLOTS)
        out[...] = jnp.concatenate([kept[here], got[here]], axis=0).astype(jnp.bfloat16)
    own_out[...] = got[len(outs) * SLOTS :].astype(jnp.bfloat16)


def gather_kernel(*refs):
    refs[-1][...] = together(refs[:-1]).astype(jnp.bfloat16)


def sift_kernel(*refs):
    *refs, out_ref = refs
    blocks = [r[...].astype(jnp.float32)[SLOTS:] for r in refs]
    out_ref[...] = jnp.concatenate(blocks, axis=0).astype(jnp.bfloat16)


def expert_kernel(*refs):
    *rows, gate_ref, up_ref, down_ref, own_one, own_two, other_one, other_two = refs
    x = unpack(together(rows)).astype(jnp.bfloat16)
    gate_v = jnp.dot(x, gate_ref[...], preferred_element_type=jnp.float32)
    up_v = jnp.dot(x, up_ref[...], preferred_element_type=jnp.float32)
    hidden = (gate_v / (1.0 + jnp.exp(-gate_v)) * up_v).astype(jnp.bfloat16)
    part = jnp.dot(hidden, down_ref[...], preferred_element_type=jnp.float32)
    store((own_one, own_two, other_one, other_two), part)


def join_kernel(mine_ref, got_ref, *outs):
    store(outs, pack(mine_ref[...].astype(jnp.float32) + got_ref[...].astype(jnp.float32)))


def combine_kernel(paired, mix_ref, *refs):
    *refs, out_hbm, out, sems = refs
    blocks = [r[...].astype(jnp.float32) for r in refs]
    if paired:
        blocks[:3] = [b[:SLOTS] for b in blocks[:3]]
    rows = unpack(jnp.concatenate(blocks, axis=0)).astype(jnp.bfloat16)
    both = jnp.concatenate([rows, rows], axis=0)
    mix = mix_ref[...]
    part = out.shape[1] // OUT_PIECES
    copies = []
    for i in range(OUT_PIECES):
        here = pl.ds(i * part, part)
        out[:, here] = lax.dot_general(
            mix,
            both[:, i * part : (i + 1) * part],
            (((0,), (0,)), ((), ())),
            preferred_element_type=jnp.float32,
        ).astype(jnp.bfloat16)
        copies.append(pltpu.make_async_copy(out.at[:, here], out_hbm.at[:, here], sems.at[i]))
        copies[-1].start()
    for copy in copies:
        copy.wait()


def per_device(tokens, norm_gain, expert_ids, gate_weights, w_gate, w_up, w_down):
    owners = lax.axis_size("exp")
    flight = owners // 2
    count, width = tokens.shape
    few = relative(flight)

    def local(kernel, outs, name, *args, limit=16):
        return pl.pallas_call(
            kernel,
            out_shape=outs,
            in_specs=[VMEM] * len(args),
            out_specs=(VMEM,) * len(outs),
            compiler_params=pltpu.CompilerParams(vmem_limit_bytes=limit * 2**20),
            cost_estimate=SMALL,
            name=name,
        )(*args)

    def full(*counts):
        return tuple(jax.ShapeDtypeStruct((n * SLOTS, width), jnp.bfloat16) for n in counts)

    def packed(*counts):
        shapes = [(n * SLOTS, packed_width(width)) for n in counts]
        return tuple(jax.ShapeDtypeStruct(shape, jnp.bfloat16) for shape in shapes)

    def swap(rows):
        return lax.ppermute(rows, "exp", [(n, n ^ 1) for n in range(owners)])

    def travel(rows, distances, cross=0):
        pairs = [(n, n ^ (2 * distances[n % 2]) ^ cross) for n in range(owners)]
        return lax.ppermute(rows, "exp", pairs)

    def stage():
        weights = w_gate[0], w_up[0], w_down[0]
        return pl.pallas_call(
            stage_kernel,
            out_shape=tuple(jax.ShapeDtypeStruct(w.shape, w.dtype) for w in weights),
            in_specs=[HBM] * 3,
            out_specs=(VMEM,) * 3,
            scratch_shapes=[pltpu.SemaphoreType.DMA((3 * PIECES,))],
            compiler_params=pltpu.CompilerParams(vmem_limit_bytes=16 * 2**20),
            cost_estimate=SMALL,
            name="stage",
        )(*in_hbm(*weights))

    def experts(rows, weights):
        outs = full(*[flight // 2] * 4)
        return local(expert_kernel, outs, "experts", *rows, *weights, limit=24)

    def join(outs, mine, theirs):
        return local(join_kernel, packed(*outs), "join", mine, swap(theirs))

    def combine(mix, arrays, paired):
        return pl.pallas_call(
            functools.partial(combine_kernel, paired),
            out_shape=jax.ShapeDtypeStruct((count, width), jnp.bfloat16),
            in_specs=[VMEM] * (len(arrays) + 1),
            out_specs=HBM,
            scratch_shapes=[
                pltpu.VMEM((count, width), jnp.bfloat16),
                pltpu.SemaphoreType.DMA((OUT_PIECES,)),
            ],
            compiler_params=pltpu.CompilerParams(vmem_limit_bytes=24 * 2**20),
            name="combine",
        )(mix, *arrays)

    first = packed(3, 4, 1, 1) if few else packed(flight)
    mix, *outgoing = pl.pallas_call(
        functools.partial(dispatch_kernel, flight),
        out_shape=(jax.ShapeDtypeStruct((2 * flight * SLOTS, count), jnp.bfloat16),) + first,
        in_specs=[HBM] * 4,
        out_specs=(VMEM,) * (len(first) + 1),
        scratch_shapes=[
            pltpu.VMEM((count, width), jnp.bfloat16),
            pltpu.VMEM((1, width), jnp.float32),
            pltpu.VMEM(expert_ids.shape[::-1], jnp.int32),
            pltpu.VMEM(gate_weights.shape[::-1], jnp.float32),
            pltpu.SemaphoreType.DMA((3 + CHUNKS,)),
        ],
        compiler_params=pltpu.CompilerParams(vmem_limit_bytes=24 * 2**20),
        name="dispatch",
    )(*in_hbm(tokens, norm_gain, expert_ids.T, gate_weights.T))
    if not few:
        weights = stage()
        groups = [list(range(core, owners, 2)) for core in range(2)]
        exchange = functools.partial(
            lax.all_to_all,
            axis_name="exp",
            split_axis=0,
            concat_axis=0,
            axis_index_groups=groups,
            tiled=True,
        )
        own = exchange(outgoing[0])
        mine_one, mine_two, theirs_one, theirs_two = experts([own, swap(own)], weights)
        half = flight // 2
        (joined_one,) = join([half], mine_one, theirs_one)
        (joined_two,) = join([half], mine_two, theirs_two)
        return combine(mix, [exchange(jnp.concatenate([joined_one, joined_two]))], False)

    one, two, three = zip(*CARRIED)
    four = (SHARED, SHARED)
    kept, given, shared, own = outgoing
    *pairs, other_own = local(merge_kernel, packed(2, 2, 2, 1), "merge", kept, swap(given))
    shared = travel(shared, four)
    arrived = [travel(a, r) for a, r in zip(pairs, (one, two, three))] + [shared]
    *arrived, gate, up, down = lax.optimization_barrier((*arrived, *stage()))
    (rows,) = local(gather_kernel, packed(7), "gather", *arrived)
    mine_one, mine_two, theirs_one, theirs_two = experts(
        (rows, own, swap(rows), other_own), (gate, up, down)
    )

    first, second = join((2, 2), mine_one, theirs_one)
    third, shared, own = join((2, 1, 1), mine_two, theirs_two)
    arrived = [
        travel(a, r) for a, r in zip((first, second, third, shared), (one, two, three, four))
    ]
    *pairs, shared = lax.optimization_barrier(tuple(arrived))
    (others,) = local(sift_kernel, packed(3), "sift", *pairs)
    return combine(mix, [*pairs, swap(others), shared, own], True)


def solution(mesh):
    placed = (
        P(("group", "exp"), None),
        P(),
        P(("group", "exp"), None),
        P(("group", "exp"), None),
        P("exp", None, None),
        P("exp", None, None),
        P("exp", None, None),
    )
    return jax.shard_map(
        per_device, mesh=mesh, in_specs=placed, out_specs=P(("group", "exp"), None), check_vma=False
    )
```

```python
import functools

import jax
import jax.numpy as jnp
from jax import lax
from jax.experimental import pallas as pl
from jax.experimental.pallas import tpu as pltpu
from jax.sharding import PartitionSpec as P

SLOTS = 8
CHUNKS = 4
PIECES = 4
OUT_PIECES = 4
LANES = 128

VMEM = pl.BlockSpec(memory_space=pltpu.VMEM)
SMALL = pl.CostEstimate(flops=1, bytes_accessed=1, transcendentals=0)
HBM = pl.BlockSpec(memory_space=pltpu.HBM)


def in_hbm(*arrays):
    return [pltpu.with_memory_space_constraint(a, pltpu.HBM) for a in arrays]


def relative(flight):
    return flight == 8


CARRIED = ((4, 5, 1), (6, 7, 2))
SHARED = 3


def block_order(flight, core):
    if not relative(flight):
        return range(flight)
    return CARRIED[core] + CARRIED[1 - core] + (SHARED, 0)


def packed_width(width):
    return width // 7 * 6 + LANES


def pack(rows):
    blocks = rows.reshape(-1, SLOTS, rows.shape[1])
    tail = rows.shape[1] // 7
    main = blocks[:, :, : 6 * tail]
    moved = jnp.concatenate([blocks[:, j : j + 1, 6 * tail :] for j in range(6)], axis=2)
    row = lax.broadcasted_iota(jnp.int32, main.shape, 1)
    main = jnp.where(row == SLOTS - 1, moved, main)
    row = row[:, :, :LANES]
    extra = jnp.zeros(row.shape, rows.dtype)
    for k in range(tail // LANES):
        start = 6 * tail + k * LANES
        extra = jnp.where(row == k, blocks[:, 6:7, start : start + LANES], extra)
    return jnp.concatenate([main, extra], axis=2).reshape(rows.shape[0], -1)


def unpack(packed):
    blocks = packed.reshape(-1, SLOTS, packed.shape[1])
    tail = (packed.shape[1] - LANES) // 6
    main = blocks[:, :, : 6 * tail]
    last = jnp.concatenate(
        [blocks[:, k : k + 1, 6 * tail :] for k in range(tail // LANES)], axis=2
    )
    row = lax.broadcasted_iota(jnp.int32, (blocks.shape[0], SLOTS, tail), 1)
    end = jnp.where(row == 6, last, 0.0)
    for j in range(6):
        end = jnp.where(row == j, blocks[:, 7:8, j * tail : (j + 1) * tail], end)
    return jnp.concatenate([main, end], axis=2).reshape(packed.shape[0], -1)


def store(refs, rows):
    at = 0
    for ref in refs:
        ref[...] = rows[at : at + ref.shape[0]].astype(ref.dtype)
        at += ref.shape[0]


def dispatch_kernel(flight, tok_hbm, gain_hbm, ids_hbm, gw_hbm, mix_ref, *rest):
    *outs, tok, gain, ids, gw, sems = rest
    count = tok.shape[0]
    part = count // CHUNKS
    small = [
        pltpu.make_async_copy(ids_hbm, ids, sems.at[0]),
        pltpu.make_async_copy(gw_hbm, gw, sems.at[1]),
        pltpu.make_async_copy(gain_hbm, gain.at[0], sems.at[2]),
    ]
    large = [
        pltpu.make_async_copy(
            tok_hbm.at[pl.ds(i * part, part)], tok.at[pl.ds(i * part, part)], sems.at[3 + i]
        )
        for i in range(CHUNKS)
    ]
    for copy in small + large:
        copy.start()
    small[0].wait()
    small[1].wait()
    experts = lax.broadcasted_iota(jnp.int32, (flight, count), 0)
    if relative(flight):
        place = experts
        me = lax.axis_index("exp")
        for i, (even, odd) in enumerate(zip(block_order(flight, 0), block_order(flight, 1))):
            experts = jnp.where(place == i, jnp.where(me % 2 == 0, even, odd) ^ (me // 2), experts)
    chosen = jnp.zeros((flight, count), jnp.float32)
    gates = jnp.zeros((flight, count), jnp.float32)
    for k in range(ids.shape[0]):
        hit = ids[k : k + 1, :] == experts
        chosen = jnp.where(hit, 1.0, chosen)
        gates = jnp.where(hit, gw[k : k + 1, :], gates)
    before = (
        lax.broadcasted_iota(jnp.int32, (count, count), 0)
        < lax.broadcasted_iota(jnp.int32, (count, count), 1)
    ).astype(jnp.bfloat16)
    rank = jnp.dot(chosen.astype(jnp.bfloat16), before, preferred_element_type=jnp.float32)
    rank = jnp.where(chosen > 0.0, rank, -1.0)

    slot = lax.broadcasted_iota(jnp.int32, (flight, SLOTS, count), 1).astype(jnp.float32)
    taken = rank[:, None, :] == slot
    pick = jnp.where(taken, 1.0, 0.0).reshape(flight * SLOTS, count).astype(jnp.bfloat16)
    mix = jnp.where(taken, gates[:, None, :], 0.0).reshape(flight * SLOTS, count)
    high = mix.astype(jnp.bfloat16)
    mix_ref[: flight * SLOTS, :] = high
    mix_ref[flight * SLOTS :, :] = (mix - high.astype(jnp.float32)).astype(jnp.bfloat16)

    for copy in large:
        copy.wait()
    wide = jnp.dot(pick, tok[...], preferred_element_type=jnp.float32)
    mean_square = jnp.mean(wide * wide, axis=1, keepdims=True)
    small[2].wait()
    rows = (wide * lax.rsqrt(mean_square + 1e-06) * gain[...]).astype(jnp.bfloat16)
    rows = rows.astype(jnp.float32)
    blocks = pack(rows)
    if len(outs) == 1:
        store(outs, blocks)
    else:
        kept, given = 3 * SLOTS, 6 * SLOTS
        store(outs[:2], blocks[:kept])
        store(outs[2:3], jnp.concatenate([blocks[kept:given], blocks[given + SLOTS :]], axis=0))
        store(outs[3:], blocks[given:])


def stage_kernel(*refs):
    *refs, sems = refs
    sources, targets = refs[:3], refs[3:]
    copies = []
    for at, (source, target) in enumerate(zip(sources, targets)):
        rows = source.shape[0] // PIECES
        for i in range(PIECES):
            here = pl.ds(i * rows, rows)
            copies.append(
                pltpu.make_async_copy(source.at[here], target.at[here], sems.at[at * PIECES + i])
            )
    for copy in copies:
        copy.start()
    for copy in copies:
        copy.wait()


def together(refs):
    return jnp.concatenate([b[...].astype(jnp.float32) for b in refs], axis=0)


def merge_kernel(kept_ref, got_ref, first_out, *outs):
    *outs, own_out = outs
    kept, got = kept_ref[...].astype(jnp.float32), got_ref[...].astype(jnp.float32)
    first_out[...] = got[:SLOTS].astype(jnp.bfloat16)
    for i, out in enumerate(outs):
        one, two = i * SLOTS, (i + 1) * SLOTS
        pair = [kept[one : one + SLOTS], got[two : two + SLOTS]]
        out[...] = jnp.concatenate(pair, axis=0).astype(jnp.bfloat16)
    own_out[...] = got[(len(outs) + 1) * SLOTS :].astype(jnp.bfloat16)


def gather_kernel(*refs):
    refs[-1][...] = together(refs[:-1]).astype(jnp.bfloat16)


def sift_kernel(*refs):
    *refs, out_ref = refs
    blocks = [r[...].astype(jnp.float32)[SLOTS:] for r in refs]
    out_ref[...] = jnp.concatenate(blocks, axis=0).astype(jnp.bfloat16)


def expert_kernel(*refs):
    *rows, gate_ref, up_ref, down_ref, own_one, own_two, other_one, other_two = refs
    x = unpack(together(rows)).astype(jnp.bfloat16)
    gate_v = jnp.dot(x, gate_ref[...], preferred_element_type=jnp.float32)
    up_v = jnp.dot(x, up_ref[...], preferred_element_type=jnp.float32)
    hidden = (gate_v / (1.0 + jnp.exp(-gate_v)) * up_v).astype(jnp.bfloat16)
    part = jnp.dot(hidden, down_ref[...], preferred_element_type=jnp.float32)
    store((own_one, own_two, other_one, other_two), part)


def join_kernel(mine_ref, got_ref, *outs):
    store(outs, pack(mine_ref[...].astype(jnp.float32) + got_ref[...].astype(jnp.float32)))


def combine_kernel(paired, mix_ref, *refs):
    *refs, out_hbm, out, sems = refs
    blocks = [r[...].astype(jnp.float32) for r in refs]
    if paired:
        blocks[:3] = [b[:SLOTS] for b in blocks[:3]]
    rows = unpack(jnp.concatenate(blocks, axis=0)).astype(jnp.bfloat16)
    both = jnp.concatenate([rows, rows], axis=0)
    mix = mix_ref[...]
    part = out.shape[1] // OUT_PIECES
    copies = []
    for i in range(OUT_PIECES):
        here = pl.ds(i * part, part)
        out[:, here] = lax.dot_general(
            mix,
            both[:, i * part : (i + 1) * part],
            (((0,), (0,)), ((), ())),
            preferred_element_type=jnp.float32,
        ).astype(jnp.bfloat16)
        copies.append(pltpu.make_async_copy(out.at[:, here], out_hbm.at[:, here], sems.at[i]))
        copies[-1].start()
    for copy in copies:
        copy.wait()


def per_device(tokens, norm_gain, expert_ids, gate_weights, w_gate, w_up, w_down):
    owners = lax.axis_size("exp")
    flight = owners // 2
    count, width = tokens.shape
    few = relative(flight)

    def local(kernel, outs, name, *args, limit=16):
        return pl.pallas_call(
            kernel,
            out_shape=outs,
            in_specs=[VMEM] * len(args),
            out_specs=(VMEM,) * len(outs),
            compiler_params=pltpu.CompilerParams(vmem_limit_bytes=limit * 2**20),
            cost_estimate=SMALL,
            name=name,
        )(*args)

    def full(*counts):
        return tuple(jax.ShapeDtypeStruct((n * SLOTS, width), jnp.bfloat16) for n in counts)

    def packed(*counts):
        shapes = [(n * SLOTS, packed_width(width)) for n in counts]
        return tuple(jax.ShapeDtypeStruct(shape, jnp.bfloat16) for shape in shapes)

    def swap(rows):
        return lax.ppermute(rows, "exp", [(n, n ^ 1) for n in range(owners)])

    def travel(rows, distances, cross=0):
        pairs = [(n, n ^ (2 * distances[n % 2]) ^ cross) for n in range(owners)]
        return lax.ppermute(rows, "exp", pairs)

    def stage():
        weights = w_gate[0], w_up[0], w_down[0]
        return pl.pallas_call(
            stage_kernel,
            out_shape=tuple(jax.ShapeDtypeStruct(w.shape, w.dtype) for w in weights),
            in_specs=[HBM] * 3,
            out_specs=(VMEM,) * 3,
            scratch_shapes=[pltpu.SemaphoreType.DMA((3 * PIECES,))],
            compiler_params=pltpu.CompilerParams(vmem_limit_bytes=16 * 2**20),
            cost_estimate=SMALL,
            name="stage",
        )(*in_hbm(*weights))

    def experts(rows, weights):
        outs = full(*[flight // 2] * 4)
        return local(expert_kernel, outs, "experts", *rows, *weights, limit=24)

    def join(outs, mine, theirs):
        return local(join_kernel, packed(*outs), "join", mine, swap(theirs))

    def combine(mix, arrays, paired):
        return pl.pallas_call(
            functools.partial(combine_kernel, paired),
            out_shape=jax.ShapeDtypeStruct((count, width), jnp.bfloat16),
            in_specs=[VMEM] * (len(arrays) + 1),
            out_specs=HBM,
            scratch_shapes=[
                pltpu.VMEM((count, width), jnp.bfloat16),
                pltpu.SemaphoreType.DMA((OUT_PIECES,)),
            ],
            compiler_params=pltpu.CompilerParams(vmem_limit_bytes=24 * 2**20),
            name="combine",
        )(mix, *arrays)

    first = packed(1, 2, 4, 1, 1) if few else packed(flight)
    mix, *outgoing = pl.pallas_call(
        functools.partial(dispatch_kernel, flight),
        out_shape=(jax.ShapeDtypeStruct((2 * flight * SLOTS, count), jnp.bfloat16),) + first,
        in_specs=[HBM] * 4,
        out_specs=(VMEM,) * (len(first) + 1),
        scratch_shapes=[
            pltpu.VMEM((count, width), jnp.bfloat16),
            pltpu.VMEM((1, width), jnp.float32),
            pltpu.VMEM(expert_ids.shape[::-1], jnp.int32),
            pltpu.VMEM(gate_weights.shape[::-1], jnp.float32),
            pltpu.SemaphoreType.DMA((3 + CHUNKS,)),
        ],
        compiler_params=pltpu.CompilerParams(vmem_limit_bytes=24 * 2**20),
        name="dispatch",
    )(*in_hbm(tokens, norm_gain, expert_ids.T, gate_weights.T))
    if not few:
        weights = stage()
        groups = [list(range(core, owners, 2)) for core in range(2)]
        exchange = functools.partial(
            lax.all_to_all,
            axis_name="exp",
            split_axis=0,
            concat_axis=0,
            axis_index_groups=groups,
            tiled=True,
        )
        own = exchange(outgoing[0])
        mine_one, mine_two, theirs_one, theirs_two = experts([own, swap(own)], weights)
        half = flight // 2
        (joined_one,) = join([half], mine_one, theirs_one)
        (joined_two,) = join([half], mine_two, theirs_two)
        return combine(mix, [exchange(jnp.concatenate([joined_one, joined_two]))], False)

    one, two, three = zip(*CARRIED)
    four = (SHARED, SHARED)
    lead, kept, given, shared, own = outgoing
    follow, second, third, other_own = local(
        merge_kernel, packed(1, 2, 2, 1), "merge", kept, swap(given)
    )
    lead = travel(lead, one)
    shared, lead = lax.optimization_barrier((shared, lead))
    arrived = [
        travel(a, r)
        for a, r in zip((follow, second, third, shared), (one, two, three, four))
    ]
    arrived = [lead, *arrived]
    *arrived, gate, up, down = lax.optimization_barrier((*arrived, *stage()))
    (rows,) = local(gather_kernel, packed(7), "gather", *arrived)
    mine_one, mine_two, theirs_one, theirs_two = experts(
        (rows, own, swap(rows), other_own), (gate, up, down)
    )

    first, second = join((2, 2), mine_one, theirs_one)
    third, shared, own = join((2, 1, 1), mine_two, theirs_two)
    arrived = [
        travel(a, r) for a, r in zip((first, second, third, shared), (one, two, three, four))
    ]
    *pairs, shared = lax.optimization_barrier(tuple(arrived))
    (others,) = local(sift_kernel, packed(3), "sift", *pairs)
    return combine(mix, [*pairs, swap(others), shared, own], True)


def solution(mesh):
    placed = (
        P(("group", "exp"), None),
        P(),
        P(("group", "exp"), None),
        P(("group", "exp"), None),
        P("exp", None, None),
        P("exp", None, None),
        P("exp", None, None),
    )
    return jax.shard_map(
        per_device, mesh=mesh, in_specs=placed, out_specs=P(("group", "exp"), None), check_vma=False
    )
```

```python
import functools

import jax
import jax.numpy as jnp
from jax import lax
from jax.experimental import pallas as pl
from jax.experimental.pallas import tpu as pltpu
from jax.sharding import PartitionSpec as P

SLOTS = 8
CHUNKS = 4
PIECES = 4
OUT_PIECES = 4
LANES = 128

VMEM = pl.BlockSpec(memory_space=pltpu.VMEM)
SMALL = pl.CostEstimate(flops=1, bytes_accessed=1, transcendentals=0)
HBM = pl.BlockSpec(memory_space=pltpu.HBM)


def in_hbm(*arrays):
    return [pltpu.with_memory_space_constraint(a, pltpu.HBM) for a in arrays]


def relative(flight):
    return flight == 8


CARRIED = ((4, 1, 5), (6, 2, 7))
SHARED = 3


def block_order(flight, core):
    if not relative(flight):
        return range(flight)
    return CARRIED[core] + CARRIED[1 - core] + (SHARED, 0)


def packed_width(width):
    return width // 7 * 6 + LANES


def pack(rows):
    blocks = rows.reshape(-1, SLOTS, rows.shape[1])
    tail = rows.shape[1] // 7
    main = blocks[:, :, : 6 * tail]
    moved = jnp.concatenate([blocks[:, j : j + 1, 6 * tail :] for j in range(6)], axis=2)
    row = lax.broadcasted_iota(jnp.int32, main.shape, 1)
    main = jnp.where(row == SLOTS - 1, moved, main)
    row = row[:, :, :LANES]
    extra = jnp.zeros(row.shape, rows.dtype)
    for k in range(tail // LANES):
        start = 6 * tail + k * LANES
        extra = jnp.where(row == k, blocks[:, 6:7, start : start + LANES], extra)
    return jnp.concatenate([main, extra], axis=2).reshape(rows.shape[0], -1)


def unpack(packed):
    blocks = packed.reshape(-1, SLOTS, packed.shape[1])
    tail = (packed.shape[1] - LANES) // 6
    main = blocks[:, :, : 6 * tail]
    last = jnp.concatenate(
        [blocks[:, k : k + 1, 6 * tail :] for k in range(tail // LANES)], axis=2
    )
    row = lax.broadcasted_iota(jnp.int32, (blocks.shape[0], SLOTS, tail), 1)
    end = jnp.where(row == 6, last, 0.0)
    for j in range(6):
        end = jnp.where(row == j, blocks[:, 7:8, j * tail : (j + 1) * tail], end)
    return jnp.concatenate([main, end], axis=2).reshape(packed.shape[0], -1)


def store(refs, rows):
    at = 0
    for ref in refs:
        ref[...] = rows[at : at + ref.shape[0]].astype(ref.dtype)
        at += ref.shape[0]


def dispatch_kernel(flight, tok_hbm, gain_hbm, ids_hbm, gw_hbm, mix_ref, *rest):
    *outs, tok, gain, ids, gw, sems = rest
    count = tok.shape[0]
    part = count // CHUNKS
    small = [
        pltpu.make_async_copy(ids_hbm, ids, sems.at[0]),
        pltpu.make_async_copy(gw_hbm, gw, sems.at[1]),
        pltpu.make_async_copy(gain_hbm, gain.at[0], sems.at[2]),
    ]
    large = [
        pltpu.make_async_copy(
            tok_hbm.at[pl.ds(i * part, part)], tok.at[pl.ds(i * part, part)], sems.at[3 + i]
        )
        for i in range(CHUNKS)
    ]
    for copy in small + large:
        copy.start()
    small[0].wait()
    small[1].wait()
    experts = lax.broadcasted_iota(jnp.int32, (flight, count), 0)
    if relative(flight):
        place = experts
        me = lax.axis_index("exp")
        for i, (even, odd) in enumerate(zip(block_order(flight, 0), block_order(flight, 1))):
            experts = jnp.where(place == i, jnp.where(me % 2 == 0, even, odd) ^ (me // 2), experts)
    chosen = jnp.zeros((flight, count), jnp.float32)
    gates = jnp.zeros((flight, count), jnp.float32)
    for k in range(ids.shape[0]):
        hit = ids[k : k + 1, :] == experts
        chosen = jnp.where(hit, 1.0, chosen)
        gates = jnp.where(hit, gw[k : k + 1, :], gates)
    before = (
        lax.broadcasted_iota(jnp.int32, (count, count), 0)
        < lax.broadcasted_iota(jnp.int32, (count, count), 1)
    ).astype(jnp.bfloat16)
    rank = jnp.dot(chosen.astype(jnp.bfloat16), before, preferred_element_type=jnp.float32)
    rank = jnp.where(chosen > 0.0, rank, -1.0)

    slot = lax.broadcasted_iota(jnp.int32, (flight, SLOTS, count), 1).astype(jnp.float32)
    taken = rank[:, None, :] == slot
    pick = jnp.where(taken, 1.0, 0.0).reshape(flight * SLOTS, count).astype(jnp.bfloat16)
    mix = jnp.where(taken, gates[:, None, :], 0.0).reshape(flight * SLOTS, count)
    high = mix.astype(jnp.bfloat16)
    mix_ref[: flight * SLOTS, :] = high
    mix_ref[flight * SLOTS :, :] = (mix - high.astype(jnp.float32)).astype(jnp.bfloat16)

    for copy in large:
        copy.wait()
    wide = jnp.dot(pick, tok[...], preferred_element_type=jnp.float32)
    mean_square = jnp.mean(wide * wide, axis=1, keepdims=True)
    small[2].wait()
    rows = (wide * lax.rsqrt(mean_square + 1e-06) * gain[...]).astype(jnp.bfloat16)
    rows = rows.astype(jnp.float32)
    blocks = pack(rows)
    if len(outs) == 1:
        store(outs, blocks)
    else:
        kept, given = 3 * SLOTS, 6 * SLOTS
        store(outs[:1], blocks[:kept])
        store(outs[1:2], jnp.concatenate([blocks[kept:given], blocks[given + SLOTS :]], axis=0))
        store(outs[2:], blocks[given:])


def stage_kernel(*refs):
    *refs, sems = refs
    sources, targets = refs[:3], refs[3:]
    copies = []
    for at, (source, target) in enumerate(zip(sources, targets)):
        rows = source.shape[0] // PIECES
        for i in range(PIECES):
            here = pl.ds(i * rows, rows)
            copies.append(
                pltpu.make_async_copy(source.at[here], target.at[here], sems.at[at * PIECES + i])
            )
    for copy in copies:
        copy.start()
    for copy in copies:
        copy.wait()


def together(refs):
    return jnp.concatenate([b[...].astype(jnp.float32) for b in refs], axis=0)


def merge_kernel(kept_ref, got_ref, *outs):
    *outs, own_out = outs
    kept, got = kept_ref[...].astype(jnp.float32), got_ref[...].astype(jnp.float32)
    for i, out in enumerate(outs):
        here = slice(i * SLOTS, (i + 1) * SLOTS)
        out[...] = jnp.concatenate([kept[here], got[here]], axis=0).astype(jnp.bfloat16)
    own_out[...] = got[len(outs) * SLOTS :].astype(jnp.bfloat16)


def gather_kernel(*refs):
    refs[-1][...] = together(refs[:-1]).astype(jnp.bfloat16)


def sift_kernel(*refs):
    *refs, out_ref = refs
    blocks = [r[...].astype(jnp.float32)[SLOTS:] for r in refs]
    out_ref[...] = jnp.concatenate(blocks, axis=0).astype(jnp.bfloat16)


def expert_kernel(*refs):
    *rows, gate_ref, up_ref, down_ref, own_one, own_two, other_one, other_two = refs
    x = unpack(together(rows)).astype(jnp.bfloat16)
    gate_v = jnp.dot(x, gate_ref[...], preferred_element_type=jnp.float32)
    up_v = jnp.dot(x, up_ref[...], preferred_element_type=jnp.float32)
    hidden = (gate_v / (1.0 + jnp.exp(-gate_v)) * up_v).astype(jnp.bfloat16)
    part = jnp.dot(hidden, down_ref[...], preferred_element_type=jnp.float32)
    store((own_one, own_two, other_one, other_two), part)


def join_kernel(mine_ref, got_ref, *outs):
    store(outs, pack(mine_ref[...].astype(jnp.float32) + got_ref[...].astype(jnp.float32)))


def combine_kernel(paired, mix_ref, *refs):
    *refs, out_hbm, out, sems = refs
    blocks = [r[...].astype(jnp.float32) for r in refs]
    if paired:
        blocks[:3] = [b[:SLOTS] for b in blocks[:3]]
    rows = unpack(jnp.concatenate(blocks, axis=0)).astype(jnp.bfloat16)
    both = jnp.concatenate([rows, rows], axis=0)
    mix = mix_ref[...]
    part = out.shape[1] // OUT_PIECES
    copies = []
    for i in range(OUT_PIECES):
        here = pl.ds(i * part, part)
        out[:, here] = lax.dot_general(
            mix,
            both[:, i * part : (i + 1) * part],
            (((0,), (0,)), ((), ())),
            preferred_element_type=jnp.float32,
        ).astype(jnp.bfloat16)
        copies.append(pltpu.make_async_copy(out.at[:, here], out_hbm.at[:, here], sems.at[i]))
        copies[-1].start()
    for copy in copies:
        copy.wait()


def per_device(*args):
    groups = range(lax.axis_size("group"))
    if not relative(lax.axis_size("exp") // 2):
        return work(groups, *args)
    branches = [functools.partial(work, [group]) for group in groups]
    return lax.switch(lax.axis_index("group"), branches, *args)


def work(groups, tokens, norm_gain, expert_ids, gate_weights, w_gate, w_up, w_down):
    owners = lax.axis_size("exp")
    bases = [group * owners for group in groups]
    flight = owners // 2
    count, width = tokens.shape
    few = relative(flight)

    def local(kernel, outs, name, *args, limit=16):
        return pl.pallas_call(
            kernel,
            out_shape=outs,
            in_specs=[VMEM] * len(args),
            out_specs=(VMEM,) * len(outs),
            compiler_params=pltpu.CompilerParams(vmem_limit_bytes=limit * 2**20),
            cost_estimate=SMALL,
            name=name,
        )(*args)

    def full(*counts):
        return tuple(jax.ShapeDtypeStruct((n * SLOTS, width), jnp.bfloat16) for n in counts)

    def packed(*counts):
        shapes = [(n * SLOTS, packed_width(width)) for n in counts]
        return tuple(jax.ShapeDtypeStruct(shape, jnp.bfloat16) for shape in shapes)

    def swap(rows):
        pairs = [(base + n, base + (n ^ 1)) for base in bases for n in range(owners)]
        return lax.ppermute(rows, ("group", "exp"), pairs)

    def travel(rows, distances):
        pairs = [
            (base + n, base + (n ^ (2 * distances[n % 2]))) for base in bases for n in range(owners)
        ]
        return lax.ppermute(rows, ("group", "exp"), pairs)

    def stage():
        weights = w_gate[0], w_up[0], w_down[0]
        return pl.pallas_call(
            stage_kernel,
            out_shape=tuple(jax.ShapeDtypeStruct(w.shape, w.dtype) for w in weights),
            in_specs=[HBM] * 3,
            out_specs=(VMEM,) * 3,
            scratch_shapes=[pltpu.SemaphoreType.DMA((3 * PIECES,))],
            compiler_params=pltpu.CompilerParams(vmem_limit_bytes=16 * 2**20),
            cost_estimate=SMALL,
            name="stage",
        )(*in_hbm(*weights))

    def experts(rows, weights):
        outs = full(*[flight // 2] * 4)
        return local(expert_kernel, outs, "experts", *rows, *weights, limit=24)

    def join(outs, mine, theirs):
        return local(join_kernel, packed(*outs), "join", mine, swap(theirs))

    def combine(mix, arrays, paired):
        return pl.pallas_call(
            functools.partial(combine_kernel, paired),
            out_shape=jax.ShapeDtypeStruct((count, width), jnp.bfloat16),
            in_specs=[VMEM] * (len(arrays) + 1),
            out_specs=HBM,
            scratch_shapes=[
                pltpu.VMEM((count, width), jnp.bfloat16),
                pltpu.SemaphoreType.DMA((OUT_PIECES,)),
            ],
            compiler_params=pltpu.CompilerParams(vmem_limit_bytes=24 * 2**20),
            name="combine",
        )(mix, *arrays)

    first = packed(3, 4, 1, 1) if few else packed(flight)
    mix, *outgoing = pl.pallas_call(
        functools.partial(dispatch_kernel, flight),
        out_shape=(jax.ShapeDtypeStruct((2 * flight * SLOTS, count), jnp.bfloat16),) + first,
        in_specs=[HBM] * 4,
        out_specs=(VMEM,) * (len(first) + 1),
        scratch_shapes=[
            pltpu.VMEM((count, width), jnp.bfloat16),
            pltpu.VMEM((1, width), jnp.float32),
            pltpu.VMEM(expert_ids.shape[::-1], jnp.int32),
            pltpu.VMEM(gate_weights.shape[::-1], jnp.float32),
            pltpu.SemaphoreType.DMA((3 + CHUNKS,)),
        ],
        compiler_params=pltpu.CompilerParams(vmem_limit_bytes=24 * 2**20),
        name="dispatch",
    )(*in_hbm(tokens, norm_gain, expert_ids.T, gate_weights.T))
    if not few:
        weights = stage()
        cores = [list(range(core, owners, 2)) for core in range(2)]
        exchange = functools.partial(
            lax.all_to_all,
            axis_name="exp",
            split_axis=0,
            concat_axis=0,
            axis_index_groups=cores,
            tiled=True,
        )
        own = exchange(outgoing[0])
        mine_one, mine_two, theirs_one, theirs_two = experts([own, swap(own)], weights)
        half = flight // 2
        (joined_one,) = join([half], mine_one, theirs_one)
        (joined_two,) = join([half], mine_two, theirs_two)
        return combine(mix, [exchange(jnp.concatenate([joined_one, joined_two]))], False)

    one, two, three = zip(*CARRIED)
    four = (SHARED, SHARED)
    kept, given, shared, own = outgoing
    *pairs, other_own = local(merge_kernel, packed(2, 2, 2, 1), "merge", kept, swap(given))
    shared = travel(shared, four)
    arrived = [travel(a, r) for a, r in zip(pairs, (one, two, three))] + [shared]
    *arrived, gate, up, down = lax.optimization_barrier((*arrived, *stage()))
    (rows,) = local(gather_kernel, packed(7), "gather", *arrived)
    mine_one, mine_two, theirs_one, theirs_two = experts(
        (rows, own, swap(rows), other_own), (gate, up, down)
    )

    first, second = join((2, 2), mine_one, theirs_one)
    third, shared, own = join((2, 1, 1), mine_two, theirs_two)
    arrived = [
        travel(a, r) for a, r in zip((first, second, third, shared), (one, two, three, four))
    ]
    *pairs, shared = lax.optimization_barrier(tuple(arrived))
    (others,) = local(sift_kernel, packed(3), "sift", *pairs)
    return combine(mix, [*pairs, swap(others), shared, own], True)


def solution(mesh):
    placed = (
        P(("group", "exp"), None),
        P(),
        P(("group", "exp"), None),
        P(("group", "exp"), None),
        P("exp", None, None),
        P("exp", None, None),
        P("exp", None, None),
    )
    return jax.shard_map(
        per_device, mesh=mesh, in_specs=placed, out_specs=P(("group", "exp"), None), check_vma=False
    )
```

```python
import functools

import jax
import jax.numpy as jnp
from jax import lax
from jax.experimental import pallas as pl
from jax.experimental.pallas import tpu as pltpu
from jax.sharding import PartitionSpec as P

SLOTS = 8
CHUNKS = 4
PIECES = 4
LANES = 128

VMEM = pl.BlockSpec(memory_space=pltpu.VMEM)
SMALL = pl.CostEstimate(flops=1, bytes_accessed=1, transcendentals=0)
HBM = pl.BlockSpec(memory_space=pltpu.HBM)


def in_hbm(*arrays):
    return [pltpu.with_memory_space_constraint(a, pltpu.HBM) for a in arrays]


def relative(flight):
    return flight == 8


CARRIED = ((4, 1, 5), (6, 2, 7))
SHARED = 3


def block_order(flight, core):
    if not relative(flight):
        return range(flight)
    return CARRIED[core] + CARRIED[1 - core] + (SHARED, 0)


def packed_width(width):
    return width // 7 * 6 + LANES


def pack(rows):
    blocks = rows.reshape(-1, SLOTS, rows.shape[1])
    tail = rows.shape[1] // 7
    main = blocks[:, :, : 6 * tail]
    moved = jnp.concatenate([blocks[:, j : j + 1, 6 * tail :] for j in range(6)], axis=2)
    row = lax.broadcasted_iota(jnp.int32, main.shape, 1)
    main = jnp.where(row == SLOTS - 1, moved, main)
    row = row[:, :, :LANES]
    extra = jnp.zeros(row.shape, rows.dtype)
    for k in range(tail // LANES):
        start = 6 * tail + k * LANES
        extra = jnp.where(row == k, blocks[:, 6:7, start : start + LANES], extra)
    return jnp.concatenate([main, extra], axis=2).reshape(rows.shape[0], -1)


def unpack_tail(packed):
    blocks = packed.reshape(-1, SLOTS, packed.shape[1])
    tail = (packed.shape[1] - LANES) // 6
    last = jnp.concatenate(
        [blocks[:, k : k + 1, 6 * tail :] for k in range(tail // LANES)], axis=2
    )
    row = lax.broadcasted_iota(jnp.int32, (blocks.shape[0], SLOTS, tail), 1)
    end = jnp.where(row == 6, last, 0.0)
    for j in range(6):
        end = jnp.where(row == j, blocks[:, 7:8, j * tail : (j + 1) * tail], end)
    return end.reshape(packed.shape[0], -1)


def unpack(packed):
    return jnp.concatenate([packed[:, : packed.shape[1] - LANES], unpack_tail(packed)], axis=1)


def store(refs, rows):
    at = 0
    for ref in refs:
        ref[...] = rows[at : at + ref.shape[0]].astype(ref.dtype)
        at += ref.shape[0]


def dispatch_kernel(flight, tok_hbm, gain_hbm, ids_hbm, gw_hbm, mix_ref, *rest):
    *outs, tok, gain, ids, gw, sems = rest
    count = tok.shape[0]
    part = count // CHUNKS
    small = [
        pltpu.make_async_copy(ids_hbm, ids, sems.at[0]),
        pltpu.make_async_copy(gw_hbm, gw, sems.at[1]),
        pltpu.make_async_copy(gain_hbm, gain.at[0], sems.at[2]),
    ]
    large = [
        pltpu.make_async_copy(
            tok_hbm.at[pl.ds(i * part, part)], tok.at[pl.ds(i * part, part)], sems.at[3 + i]
        )
        for i in range(CHUNKS)
    ]
    for copy in small + large:
        copy.start()
    small[0].wait()
    small[1].wait()
    experts = lax.broadcasted_iota(jnp.int32, (flight, count), 0)
    if relative(flight):
        place = experts
        me = lax.axis_index("exp")
        for i, (even, odd) in enumerate(zip(block_order(flight, 0), block_order(flight, 1))):
            experts = jnp.where(place == i, jnp.where(me % 2 == 0, even, odd) ^ (me // 2), experts)
    chosen = jnp.zeros((flight, count), jnp.float32)
    gates = jnp.zeros((flight, count), jnp.float32)
    for k in range(ids.shape[0]):
        hit = ids[k : k + 1, :] == experts
        chosen = jnp.where(hit, 1.0, chosen)
        gates = jnp.where(hit, gw[k : k + 1, :], gates)
    before = (
        lax.broadcasted_iota(jnp.int32, (count, count), 0)
        < lax.broadcasted_iota(jnp.int32, (count, count), 1)
    ).astype(jnp.bfloat16)
    rank = jnp.dot(chosen.astype(jnp.bfloat16), before, preferred_element_type=jnp.float32)
    rank = jnp.where(chosen > 0.0, rank, -1.0)

    slot = lax.broadcasted_iota(jnp.int32, (flight, SLOTS, count), 1).astype(jnp.float32)
    taken = rank[:, None, :] == slot
    pick = jnp.where(taken, 1.0, 0.0).reshape(flight * SLOTS, count).astype(jnp.bfloat16)
    mix = jnp.where(taken, gates[:, None, :], 0.0).reshape(flight * SLOTS, count)
    high = mix.astype(jnp.bfloat16)
    mix_ref[: flight * SLOTS, :] = high
    mix_ref[flight * SLOTS :, :] = (mix - high.astype(jnp.float32)).astype(jnp.bfloat16)

    for copy in large:
        copy.wait()
    wide = jnp.dot(pick, tok[...], preferred_element_type=jnp.float32)
    mean_square = jnp.mean(wide * wide, axis=1, keepdims=True)
    small[2].wait()
    rows = (wide * lax.rsqrt(mean_square + 1e-06) * gain[...]).astype(jnp.bfloat16)
    rows = rows.astype(jnp.float32)
    blocks = pack(rows)
    if len(outs) == 1:
        store(outs, blocks)
    else:
        kept, given = 3 * SLOTS, 6 * SLOTS
        store(outs[:1], blocks[:kept])
        store(outs[1:2], jnp.concatenate([blocks[kept:given], blocks[given + SLOTS :]], axis=0))
        store(outs[2:], blocks[given:])


def stage_kernel(mix_ref, *refs):
    *refs, turned_ref, sems = refs
    sources, targets = refs[:3], refs[3:]
    copies = []
    for at, (source, target) in enumerate(zip(sources, targets)):
        rows = source.shape[0] // PIECES
        for i in range(PIECES):
            here = pl.ds(i * rows, rows)
            copies.append(
                pltpu.make_async_copy(source.at[here], target.at[here], sems.at[at * PIECES + i])
            )
    for copy in copies:
        copy.start()
    turned_ref[...] = mix_ref[...].T
    for copy in copies:
        copy.wait()


def together(refs):
    return jnp.concatenate([b[...].astype(jnp.float32) for b in refs], axis=0)


def merge_kernel(kept_ref, got_ref, *outs):
    *outs, own_out = outs
    kept, got = kept_ref[...].astype(jnp.float32), got_ref[...].astype(jnp.float32)
    for i, out in enumerate(outs):
        here = slice(i * SLOTS, (i + 1) * SLOTS)
        out[...] = jnp.concatenate([kept[here], got[here]], axis=0).astype(jnp.bfloat16)
    own_out[...] = got[len(outs) * SLOTS :].astype(jnp.bfloat16)


def gather_kernel(count, *refs):
    store(refs[-count:], together(refs[:-count]))


def sift_kernel(*refs):
    *refs, out_ref = refs
    blocks = [r[...].astype(jnp.float32)[SLOTS:] for r in refs]
    out_ref[...] = jnp.concatenate(blocks, axis=0).astype(jnp.bfloat16)


def expert_kernel(*refs):
    *rows, gate_ref, up_ref, down_ref, own_one, own_two, other_one, other_two = refs
    x = unpack(together(rows)).astype(jnp.bfloat16)
    gate_v = jnp.dot(x, gate_ref[...], preferred_element_type=jnp.float32)
    up_v = jnp.dot(x, up_ref[...], preferred_element_type=jnp.float32)
    hidden = (gate_v / (1.0 + jnp.exp(-gate_v)) * up_v).astype(jnp.bfloat16)
    part = jnp.dot(hidden, down_ref[...], preferred_element_type=jnp.float32)
    store((own_one, own_two, other_one, other_two), part)


def join_kernel(mine_ref, got_ref, *outs):
    store(outs, pack(mine_ref[...].astype(jnp.float32) + got_ref[...].astype(jnp.float32)))


def combine_kernel(paired, mix_ref, *refs):
    *refs, out_hbm, out, sems = refs
    blocks = [r[...].astype(jnp.float32) for r in refs]
    rows = jnp.concatenate([b[:SLOTS] for b in blocks[:paired]] + blocks[paired:], axis=0)
    mix = mix_ref[...]
    tail = out.shape[1] // 7
    copies = []
    for i in range(7):
        here = pl.ds(i * tail, tail)
        piece = rows[:, i * tail : (i + 1) * tail] if i < 6 else unpack_tail(rows)
        piece = piece.astype(jnp.bfloat16)
        both = jnp.concatenate([piece, piece], axis=0)
        out[:, here] = jnp.dot(mix, both, preferred_element_type=jnp.float32).astype(jnp.bfloat16)
        copies.append(pltpu.make_async_copy(out.at[:, here], out_hbm.at[:, here], sems.at[i]))
        copies[-1].start()
    for copy in copies:
        copy.wait()


def per_device(tokens, norm_gain, expert_ids, gate_weights, w_gate, w_up, w_down):
    owners = lax.axis_size("exp")
    flight = owners // 2
    count, width = tokens.shape
    few = relative(flight)

    def local(kernel, outs, name, *args, limit=16):
        return pl.pallas_call(
            kernel,
            out_shape=outs,
            in_specs=[VMEM] * len(args),
            out_specs=(VMEM,) * len(outs),
            compiler_params=pltpu.CompilerParams(vmem_limit_bytes=limit * 2**20),
            cost_estimate=SMALL,
            name=name,
        )(*args)

    def full(*counts):
        return tuple(jax.ShapeDtypeStruct((n * SLOTS, width), jnp.bfloat16) for n in counts)

    def packed(*counts):
        shapes = [(n * SLOTS, packed_width(width)) for n in counts]
        return tuple(jax.ShapeDtypeStruct(shape, jnp.bfloat16) for shape in shapes)

    def swap(rows):
        return lax.ppermute(rows, "exp", [(n, n ^ 1) for n in range(owners)])

    def travel(rows, distances, cross=0):
        pairs = [(n, n ^ (2 * distances[n % 2]) ^ cross) for n in range(owners)]
        return lax.ppermute(rows, "exp", pairs)

    def stage(mix):
        weights = w_gate[0], w_up[0], w_down[0]
        outs = [jax.ShapeDtypeStruct(w.shape, w.dtype) for w in weights]
        return pl.pallas_call(
            stage_kernel,
            out_shape=(*outs, jax.ShapeDtypeStruct(mix.shape[::-1], mix.dtype)),
            in_specs=[VMEM] + [HBM] * 3,
            out_specs=(VMEM,) * 4,
            scratch_shapes=[pltpu.SemaphoreType.DMA((3 * PIECES,))],
            compiler_params=pltpu.CompilerParams(vmem_limit_bytes=16 * 2**20),
            cost_estimate=SMALL,
            name="stage",
        )(mix, *in_hbm(*weights))

    def experts(rows, weights):
        outs = full(*[flight // 2] * 4)
        return local(expert_kernel, outs, "experts", *rows, *weights, limit=24)

    def join(outs, mine, theirs):
        return local(join_kernel, packed(*outs), "join", mine, swap(theirs))

    def combine(mix, arrays, paired):
        return pl.pallas_call(
            functools.partial(combine_kernel, paired),
            out_shape=jax.ShapeDtypeStruct((count, width), jnp.bfloat16),
            in_specs=[VMEM] * (len(arrays) + 1),
            out_specs=HBM,
            scratch_shapes=[
                pltpu.VMEM((count, width), jnp.bfloat16),
                pltpu.SemaphoreType.DMA((7,)),
            ],
            compiler_params=pltpu.CompilerParams(vmem_limit_bytes=24 * 2**20),
            name="combine",
        )(mix, *arrays)

    first = packed(3, 4, 1, 1) if few else packed(flight)
    mix, *outgoing = pl.pallas_call(
        functools.partial(dispatch_kernel, flight),
        out_shape=(jax.ShapeDtypeStruct((2 * flight * SLOTS, count), jnp.bfloat16),) + first,
        in_specs=[HBM] * 4,
        out_specs=(VMEM,) * (len(first) + 1),
        scratch_shapes=[
            pltpu.VMEM((count, width), jnp.bfloat16),
            pltpu.VMEM((1, width), jnp.float32),
            pltpu.VMEM(expert_ids.shape[::-1], jnp.int32),
            pltpu.VMEM(gate_weights.shape[::-1], jnp.float32),
            pltpu.SemaphoreType.DMA((3 + CHUNKS,)),
        ],
        compiler_params=pltpu.CompilerParams(vmem_limit_bytes=24 * 2**20),
        name="dispatch",
    )(*in_hbm(tokens, norm_gain, expert_ids.T, gate_weights.T))
    if not few:
        *weights, mix = stage(mix)
        groups = [list(range(core, owners, 2)) for core in range(2)]
        exchange = functools.partial(
            lax.all_to_all,
            axis_name="exp",
            split_axis=0,
            concat_axis=0,
            axis_index_groups=groups,
            tiled=True,
        )
        own = exchange(outgoing[0])
        mine_one, mine_two, theirs_one, theirs_two = experts([own, swap(own)], weights)
        half = flight // 2
        (joined_one,) = join([half], mine_one, theirs_one)
        (joined_two,) = join([half], mine_two, theirs_two)
        return combine(mix, [exchange(jnp.concatenate([joined_one, joined_two]))], 0)

    one, two, three = zip(*CARRIED)
    four = (SHARED, SHARED)
    kept, given, shared, own = outgoing
    *pairs, other_own = local(merge_kernel, packed(2, 2, 2, 1), "merge", kept, swap(given))
    shared = travel(shared, four)
    arrived = [travel(a, r) for a, r in zip(pairs, (one, two, three))] + [shared]
    *arrived, gate, up, down, mix = lax.optimization_barrier((*arrived, *stage(mix)))
    kernel = functools.partial(gather_kernel, 2)
    rows = local(kernel, packed(4, 3), "gather", *arrived)
    mine_one, mine_two, theirs_one, theirs_two = experts(
        (*rows, own, *[swap(a) for a in rows], other_own), (gate, up, down)
    )

    first, second = join((2, 2), mine_one, theirs_one)
    third, shared, own = join((2, 1, 1), mine_two, theirs_two)
    arrived = [
        travel(a, r) for a, r in zip((first, second, third, shared), (one, two, three, four))
    ]
    *pairs, shared = lax.optimization_barrier(tuple(arrived))
    (others,) = local(sift_kernel, packed(3), "sift", *pairs)
    return combine(mix, [*pairs, swap(others), shared, own], 3)


def solution(mesh):
    placed = (
        P(("group", "exp"), None),
        P(),
        P(("group", "exp"), None),
        P(("group", "exp"), None),
        P("exp", None, None),
        P("exp", None, None),
        P("exp", None, None),
    )
    return jax.shard_map(
        per_device, mesh=mesh, in_specs=placed, out_specs=P(("group", "exp"), None), check_vma=False
    )
```

```python
import functools

import jax
import jax.numpy as jnp
from jax import lax
from jax.experimental import pallas as pl
from jax.experimental.pallas import tpu as pltpu
from jax.sharding import PartitionSpec as P

SLOTS = 8
CHUNKS = 4
PIECES = 4
LANES = 128

VMEM = pl.BlockSpec(memory_space=pltpu.VMEM)
SMALL = pl.CostEstimate(flops=1, bytes_accessed=1, transcendentals=0)
HBM = pl.BlockSpec(memory_space=pltpu.HBM)


def in_hbm(*arrays):
    return [pltpu.with_memory_space_constraint(a, pltpu.HBM) for a in arrays]


def relative(flight):
    return flight == 8


CARRIED = ((4, 1, 5), (6, 2, 7))
SHARED = 3


def block_order(flight, core):
    if not relative(flight):
        return range(flight)
    return CARRIED[core] + CARRIED[1 - core] + (SHARED, 0)


def packed_width(width):
    return width // 7 * 6 + LANES


def pack(rows):
    blocks = rows.reshape(-1, SLOTS, rows.shape[1])
    tail = rows.shape[1] // 7
    main = blocks[:, :, : 6 * tail]
    moved = jnp.concatenate([blocks[:, j : j + 1, 6 * tail :] for j in range(6)], axis=2)
    row = lax.broadcasted_iota(jnp.int32, main.shape, 1)
    main = jnp.where(row == SLOTS - 1, moved, main)
    row = row[:, :, :LANES]
    extra = jnp.zeros(row.shape, rows.dtype)
    for k in range(tail // LANES):
        start = 6 * tail + k * LANES
        extra = jnp.where(row == k, blocks[:, 6:7, start : start + LANES], extra)
    return jnp.concatenate([main, extra], axis=2).reshape(rows.shape[0], -1)


def unpack_tail(packed):
    blocks = packed.reshape(-1, SLOTS, packed.shape[1])
    tail = (packed.shape[1] - LANES) // 6
    last = jnp.concatenate(
        [blocks[:, k : k + 1, 6 * tail :] for k in range(tail // LANES)], axis=2
    )
    row = lax.broadcasted_iota(jnp.int32, (blocks.shape[0], SLOTS, tail), 1)
    end = jnp.where(row == 6, last, 0.0)
    for j in range(6):
        end = jnp.where(row == j, blocks[:, 7:8, j * tail : (j + 1) * tail], end)
    return end.reshape(packed.shape[0], -1)


def unpack(packed):
    return jnp.concatenate([packed[:, : packed.shape[1] - LANES], unpack_tail(packed)], axis=1)


def store(refs, rows):
    at = 0
    for ref in refs:
        ref[...] = rows[at : at + ref.shape[0]].astype(ref.dtype)
        at += ref.shape[0]


def dispatch_kernel(flight, tok_hbm, gain_hbm, ids_hbm, gw_hbm, mix_ref, *rest):
    *outs, tok, gain, ids, gw, sems = rest
    count = tok.shape[0]
    part = count // CHUNKS
    small = [
        pltpu.make_async_copy(ids_hbm, ids, sems.at[0]),
        pltpu.make_async_copy(gw_hbm, gw, sems.at[1]),
        pltpu.make_async_copy(gain_hbm, gain.at[0], sems.at[2]),
    ]
    large = [
        pltpu.make_async_copy(
            tok_hbm.at[pl.ds(i * part, part)], tok.at[pl.ds(i * part, part)], sems.at[3 + i]
        )
        for i in range(CHUNKS)
    ]
    for copy in small + large:
        copy.start()
    small[0].wait()
    small[1].wait()
    experts = lax.broadcasted_iota(jnp.int32, (flight, count), 0)
    if relative(flight):
        place = experts
        me = lax.axis_index("exp")
        for i, (even, odd) in enumerate(zip(block_order(flight, 0), block_order(flight, 1))):
            experts = jnp.where(place == i, jnp.where(me % 2 == 0, even, odd) ^ (me // 2), experts)
    chosen = jnp.zeros((flight, count), jnp.float32)
    gates = jnp.zeros((flight, count), jnp.float32)
    for k in range(ids.shape[0]):
        hit = ids[k : k + 1, :] == experts
        chosen = jnp.where(hit, 1.0, chosen)
        gates = jnp.where(hit, gw[k : k + 1, :], gates)
    before = (
        lax.broadcasted_iota(jnp.int32, (count, count), 0)
        < lax.broadcasted_iota(jnp.int32, (count, count), 1)
    ).astype(jnp.bfloat16)
    rank = jnp.dot(chosen.astype(jnp.bfloat16), before, preferred_element_type=jnp.float32)
    rank = jnp.where(chosen > 0.0, rank, -1.0)

    slot = lax.broadcasted_iota(jnp.int32, (flight, SLOTS, count), 1).astype(jnp.float32)
    taken = rank[:, None, :] == slot
    pick = jnp.where(taken, 1.0, 0.0).reshape(flight * SLOTS, count).astype(jnp.bfloat16)
    mix = jnp.where(taken, gates[:, None, :], 0.0).reshape(flight * SLOTS, count)
    high = mix.astype(jnp.bfloat16)
    mix_ref[: flight * SLOTS, :] = high
    mix_ref[flight * SLOTS :, :] = (mix - high.astype(jnp.float32)).astype(jnp.bfloat16)

    for copy in large:
        copy.wait()
    wide = jnp.dot(pick, tok[...], preferred_element_type=jnp.float32)
    mean_square = jnp.mean(wide * wide, axis=1, keepdims=True)
    small[2].wait()
    rows = (wide * lax.rsqrt(mean_square + 1e-06) * gain[...]).astype(jnp.bfloat16)
    rows = rows.astype(jnp.float32)
    blocks = pack(rows)
    if len(outs) == 1:
        store(outs, blocks)
    else:
        kept, given = 3 * SLOTS, 6 * SLOTS
        store(outs[:1], blocks[:kept])
        store(outs[1:2], jnp.concatenate([blocks[kept:given], blocks[given + SLOTS :]], axis=0))
        store(outs[2:], blocks[given:])


def stage_kernel(mix_ref, *refs):
    *refs, turned_ref, sems = refs
    sources, targets = refs[:3], refs[3:]
    copies = []
    for at, (source, target) in enumerate(zip(sources, targets)):
        rows = source.shape[0] // PIECES
        for i in range(PIECES):
            here = pl.ds(i * rows, rows)
            copies.append(
                pltpu.make_async_copy(source.at[here], target.at[here], sems.at[at * PIECES + i])
            )
    for copy in copies:
        copy.start()
    turned_ref[...] = mix_ref[...].T
    for copy in copies:
        copy.wait()


def together(refs):
    return jnp.concatenate([b[...].astype(jnp.float32) for b in refs], axis=0)


def merge_kernel(kept_ref, got_ref, *outs):
    *outs, own_out = outs
    kept, got = kept_ref[...].astype(jnp.float32), got_ref[...].astype(jnp.float32)
    for i, out in enumerate(outs):
        here = slice(i * SLOTS, (i + 1) * SLOTS)
        out[...] = jnp.concatenate([kept[here], got[here]], axis=0).astype(jnp.bfloat16)
    own_out[...] = got[len(outs) * SLOTS :].astype(jnp.bfloat16)


def gather_kernel(count, *refs):
    store(refs[-count:], together(refs[:-count]))


def sift_kernel(*refs):
    count = len(refs) // 2
    for ref, out in zip(refs[:count], refs[count:]):
        out[...] = ref[...].astype(jnp.float32)[SLOTS:].astype(jnp.bfloat16)


def expert_kernel(*refs):
    *rows, gate_ref, up_ref, down_ref, own_one, own_two, other_one, other_two = refs
    x = unpack(together(rows)).astype(jnp.bfloat16)
    gate_v = jnp.dot(x, gate_ref[...], preferred_element_type=jnp.float32)
    up_v = jnp.dot(x, up_ref[...], preferred_element_type=jnp.float32)
    hidden = (gate_v / (1.0 + jnp.exp(-gate_v)) * up_v).astype(jnp.bfloat16)
    part = jnp.dot(hidden, down_ref[...], preferred_element_type=jnp.float32)
    store((own_one, own_two, other_one, other_two), part)


def join_kernel(mine_ref, got_ref, *outs):
    store(outs, pack(mine_ref[...].astype(jnp.float32) + got_ref[...].astype(jnp.float32)))


def combine_kernel(paired, mix_ref, *refs):
    *refs, out_hbm, out, sems = refs
    blocks = [r[...].astype(jnp.float32) for r in refs]
    rows = jnp.concatenate([b[:SLOTS] for b in blocks[:paired]] + blocks[paired:], axis=0)
    mix = mix_ref[...]
    tail = out.shape[1] // 7
    copies = []
    for i in range(7):
        here = pl.ds(i * tail, tail)
        piece = rows[:, i * tail : (i + 1) * tail] if i < 6 else unpack_tail(rows)
        piece = piece.astype(jnp.bfloat16)
        both = jnp.concatenate([piece, piece], axis=0)
        out[:, here] = jnp.dot(mix, both, preferred_element_type=jnp.float32).astype(jnp.bfloat16)
        copies.append(pltpu.make_async_copy(out.at[:, here], out_hbm.at[:, here], sems.at[i]))
        copies[-1].start()
    for copy in copies:
        copy.wait()


def per_device(tokens, norm_gain, expert_ids, gate_weights, w_gate, w_up, w_down):
    owners = lax.axis_size("exp")
    flight = owners // 2
    count, width = tokens.shape
    few = relative(flight)

    def local(kernel, outs, name, *args, limit=16):
        return pl.pallas_call(
            kernel,
            out_shape=outs,
            in_specs=[VMEM] * len(args),
            out_specs=(VMEM,) * len(outs),
            compiler_params=pltpu.CompilerParams(vmem_limit_bytes=limit * 2**20),
            cost_estimate=SMALL,
            name=name,
        )(*args)

    def full(*counts):
        return tuple(jax.ShapeDtypeStruct((n * SLOTS, width), jnp.bfloat16) for n in counts)

    def packed(*counts):
        shapes = [(n * SLOTS, packed_width(width)) for n in counts]
        return tuple(jax.ShapeDtypeStruct(shape, jnp.bfloat16) for shape in shapes)

    def swap(rows):
        return lax.ppermute(rows, "exp", [(n, n ^ 1) for n in range(owners)])

    def travel(rows, distances, across=0):
        pairs = [(n, n ^ (2 * distances[n % 2]) ^ across) for n in range(owners)]
        return lax.ppermute(rows, "exp", pairs)

    def stage(mix):
        weights = w_gate[0], w_up[0], w_down[0]
        outs = [jax.ShapeDtypeStruct(w.shape, w.dtype) for w in weights]
        return pl.pallas_call(
            stage_kernel,
            out_shape=(*outs, jax.ShapeDtypeStruct(mix.shape[::-1], mix.dtype)),
            in_specs=[VMEM] + [HBM] * 3,
            out_specs=(VMEM,) * 4,
            scratch_shapes=[pltpu.SemaphoreType.DMA((3 * PIECES,))],
            compiler_params=pltpu.CompilerParams(vmem_limit_bytes=16 * 2**20),
            cost_estimate=SMALL,
            name="stage",
        )(mix, *in_hbm(*weights))

    def experts(rows, weights):
        outs = full(*[flight // 2] * 4)
        return local(expert_kernel, outs, "experts", *rows, *weights, limit=24)

    def join(outs, mine, theirs):
        return local(join_kernel, packed(*outs), "join", mine, swap(theirs))

    def combine(mix, arrays, paired):
        return pl.pallas_call(
            functools.partial(combine_kernel, paired),
            out_shape=jax.ShapeDtypeStruct((count, width), jnp.bfloat16),
            in_specs=[VMEM] * (len(arrays) + 1),
            out_specs=HBM,
            scratch_shapes=[
                pltpu.VMEM((count, width), jnp.bfloat16),
                pltpu.SemaphoreType.DMA((7,)),
            ],
            compiler_params=pltpu.CompilerParams(vmem_limit_bytes=24 * 2**20),
            name="combine",
        )(mix, *arrays)

    first = packed(3, 4, 1, 1) if few else packed(flight)
    mix, *outgoing = pl.pallas_call(
        functools.partial(dispatch_kernel, flight),
        out_shape=(jax.ShapeDtypeStruct((2 * flight * SLOTS, count), jnp.bfloat16),) + first,
        in_specs=[HBM] * 4,
        out_specs=(VMEM,) * (len(first) + 1),
        scratch_shapes=[
            pltpu.VMEM((count, width), jnp.bfloat16),
            pltpu.VMEM((1, width), jnp.float32),
            pltpu.VMEM(expert_ids.shape[::-1], jnp.int32),
            pltpu.VMEM(gate_weights.shape[::-1], jnp.float32),
            pltpu.SemaphoreType.DMA((3 + CHUNKS,)),
        ],
        compiler_params=pltpu.CompilerParams(vmem_limit_bytes=24 * 2**20),
        name="dispatch",
    )(*in_hbm(tokens, norm_gain, expert_ids.T, gate_weights.T))
    if not few:
        *weights, mix = stage(mix)
        groups = [list(range(core, owners, 2)) for core in range(2)]
        exchange = functools.partial(
            lax.all_to_all,
            axis_name="exp",
            split_axis=0,
            concat_axis=0,
            axis_index_groups=groups,
            tiled=True,
        )
        own = exchange(outgoing[0])
        mine_one, mine_two, theirs_one, theirs_two = experts([own, swap(own)], weights)
        half = flight // 2
        (joined_one,) = join([half], mine_one, theirs_one)
        (joined_two,) = join([half], mine_two, theirs_two)
        return combine(mix, [exchange(jnp.concatenate([joined_one, joined_two]))], 0)

    one, two, three = zip(*CARRIED)
    four = (SHARED, SHARED)
    kept, given, shared, own = outgoing
    *pairs, other_own = local(merge_kernel, packed(2, 2, 2, 1), "merge", kept, swap(given))
    shared = travel(shared, four)
    arrived = [travel(a, r) for a, r in zip(pairs, (one, two, three))] + [shared]
    *arrived, gate, up, down, mix = lax.optimization_barrier((*arrived, *stage(mix)))
    kernel = functools.partial(gather_kernel, 2)
    rows = local(kernel, packed(4, 3), "gather", *arrived)
    mine_one, mine_two, theirs_one, theirs_two = experts(
        (*rows, own, *[swap(a) for a in rows], other_own), (gate, up, down)
    )

    first, second = join((2, 2), mine_one, theirs_one)
    third, third_across, shared, own = join((1, 1, 1, 1), mine_two, theirs_two)
    first, second, shared = travel(first, one), travel(second, two), travel(shared, four)
    third, third_across = travel(third, three), travel(third_across, three, 1)
    others = local(sift_kernel, packed(1, 1), "sift", first, second)
    others = [swap(a) for a in others]
    return combine(mix, [first, second, third, *others, third_across, shared, own], 2)


def solution(mesh):
    placed = (
        P(("group", "exp"), None),
        P(),
        P(("group", "exp"), None),
        P(("group", "exp"), None),
        P("exp", None, None),
        P("exp", None, None),
        P("exp", None, None),
    )
    return jax.shard_map(
        per_device, mesh=mesh, in_specs=placed, out_specs=P(("group", "exp"), None), check_vma=False
    )
```

```python
import functools

import jax
import jax.numpy as jnp
from jax import lax
from jax.experimental import pallas as pl
from jax.experimental.pallas import tpu as pltpu
from jax.sharding import PartitionSpec as P

SLOTS = 8
CHUNKS = 4
PIECES = 4
LANES = 128

VMEM = pl.BlockSpec(memory_space=pltpu.VMEM)
SMALL = pl.CostEstimate(flops=1, bytes_accessed=1, transcendentals=0)
HBM = pl.BlockSpec(memory_space=pltpu.HBM)


def in_hbm(*arrays):
    return [pltpu.with_memory_space_constraint(a, pltpu.HBM) for a in arrays]


def relative(flight):
    return flight == 8


CARRIED = ((4, 1, 5), (6, 2, 7))
SHARED = 3


def block_order(flight, core):
    if not relative(flight):
        return range(flight)
    return CARRIED[core] + CARRIED[1 - core] + (SHARED, 0)


def packed_width(width):
    return width // 7 * 6 + LANES


def pack(rows):
    blocks = rows.reshape(-1, SLOTS, rows.shape[1])
    tail = rows.shape[1] // 7
    main = blocks[:, :, : 6 * tail]
    moved = jnp.concatenate([blocks[:, j : j + 1, 6 * tail :] for j in range(6)], axis=2)
    row = lax.broadcasted_iota(jnp.int32, main.shape, 1)
    main = jnp.where(row == SLOTS - 1, moved, main)
    row = row[:, :, :LANES]
    extra = jnp.zeros(row.shape, rows.dtype)
    for k in range(tail // LANES):
        start = 6 * tail + k * LANES
        extra = jnp.where(row == k, blocks[:, 6:7, start : start + LANES], extra)
    return jnp.concatenate([main, extra], axis=2).reshape(rows.shape[0], -1)


def unpack_tail(packed):
    blocks = packed.reshape(-1, SLOTS, packed.shape[1])
    tail = (packed.shape[1] - LANES) // 6
    last = jnp.concatenate(
        [blocks[:, k : k + 1, 6 * tail :] for k in range(tail // LANES)], axis=2
    )
    row = lax.broadcasted_iota(jnp.int32, (blocks.shape[0], SLOTS, tail), 1)
    end = jnp.where(row == 6, last, 0.0)
    for j in range(6):
        end = jnp.where(row == j, blocks[:, 7:8, j * tail : (j + 1) * tail], end)
    return end.reshape(packed.shape[0], -1)


def unpack(packed):
    return jnp.concatenate([packed[:, : packed.shape[1] - LANES], unpack_tail(packed)], axis=1)


def store(refs, rows):
    at = 0
    for ref in refs:
        ref[...] = rows[at : at + ref.shape[0]].astype(ref.dtype)
        at += ref.shape[0]


def dispatch_kernel(flight, tok_hbm, gain_hbm, ids_hbm, gw_hbm, mix_ref, *rest):
    *outs, tok, gain, ids, gw, sems = rest
    count = tok.shape[0]
    part = count // CHUNKS
    small = [
        pltpu.make_async_copy(ids_hbm, ids, sems.at[0]),
        pltpu.make_async_copy(gw_hbm, gw, sems.at[1]),
        pltpu.make_async_copy(gain_hbm, gain.at[0], sems.at[2]),
    ]
    large = [
        pltpu.make_async_copy(
            tok_hbm.at[pl.ds(i * part, part)], tok.at[pl.ds(i * part, part)], sems.at[3 + i]
        )
        for i in range(CHUNKS)
    ]
    for copy in small + large:
        copy.start()
    small[0].wait()
    small[1].wait()
    experts = lax.broadcasted_iota(jnp.int32, (flight, count), 0)
    if relative(flight):
        place = experts
        me = lax.axis_index("exp")
        for i, (even, odd) in enumerate(zip(block_order(flight, 0), block_order(flight, 1))):
            experts = jnp.where(place == i, jnp.where(me % 2 == 0, even, odd) ^ (me // 2), experts)
    chosen = jnp.zeros((flight, count), jnp.float32)
    gates = jnp.zeros((flight, count), jnp.float32)
    for k in range(ids.shape[0]):
        hit = ids[k : k + 1, :] == experts
        chosen = jnp.where(hit, 1.0, chosen)
        gates = jnp.where(hit, gw[k : k + 1, :], gates)
    before = (
        lax.broadcasted_iota(jnp.int32, (count, count), 0)
        < lax.broadcasted_iota(jnp.int32, (count, count), 1)
    ).astype(jnp.bfloat16)
    rank = jnp.dot(chosen.astype(jnp.bfloat16), before, preferred_element_type=jnp.float32)
    rank = jnp.where(chosen > 0.0, rank, -1.0)

    slot = lax.broadcasted_iota(jnp.int32, (flight, SLOTS, count), 1).astype(jnp.float32)
    taken = rank[:, None, :] == slot
    pick = jnp.where(taken, 1.0, 0.0).reshape(flight * SLOTS, count).astype(jnp.bfloat16)
    mix = jnp.where(taken, gates[:, None, :], 0.0).reshape(flight * SLOTS, count)
    high = mix.astype(jnp.bfloat16)
    mix_ref[: flight * SLOTS, :] = high
    mix_ref[flight * SLOTS :, :] = (mix - high.astype(jnp.float32)).astype(jnp.bfloat16)

    for copy in large:
        copy.wait()
    wide = jnp.dot(pick, tok[...], preferred_element_type=jnp.float32)
    mean_square = jnp.mean(wide * wide, axis=1, keepdims=True)
    small[2].wait()
    rows = (wide * lax.rsqrt(mean_square + 1e-06) * gain[...]).astype(jnp.bfloat16)
    rows = rows.astype(jnp.float32)
    store(outs, pack(rows))


def stage_kernel(mix_ref, *refs):
    *refs, turned_ref, sems = refs
    sources, targets = refs[:3], refs[3:]
    copies = []
    for at, (source, target) in enumerate(zip(sources, targets)):
        rows = source.shape[0] // PIECES
        for i in range(PIECES):
            here = pl.ds(i * rows, rows)
            copies.append(
                pltpu.make_async_copy(source.at[here], target.at[here], sems.at[at * PIECES + i])
            )
    for copy in copies:
        copy.start()
    turned_ref[...] = mix_ref[...].T
    for copy in copies:
        copy.wait()


def together(refs):
    return jnp.concatenate([b[...].astype(jnp.float32) for b in refs], axis=0)


def gather_kernel(count, *refs):
    store(refs[-count:], together(refs[:-count]))


def sift_kernel(*refs):
    count = len(refs) // 2
    for ref, out in zip(refs[:count], refs[count:]):
        out[...] = ref[...].astype(jnp.float32)[SLOTS:].astype(jnp.bfloat16)


def expert_kernel(*refs):
    *rows, gate_ref, up_ref, down_ref, own_one, own_two, other_one, other_two = refs
    x = unpack(together(rows)).astype(jnp.bfloat16)
    gate_v = jnp.dot(x, gate_ref[...], preferred_element_type=jnp.float32)
    up_v = jnp.dot(x, up_ref[...], preferred_element_type=jnp.float32)
    hidden = (gate_v / (1.0 + jnp.exp(-gate_v)) * up_v).astype(jnp.bfloat16)
    part = jnp.dot(hidden, down_ref[...], preferred_element_type=jnp.float32)
    store((own_one, own_two, other_one, other_two), part)


def join_kernel(mine_ref, got_ref, *outs):
    store(outs, pack(mine_ref[...].astype(jnp.float32) + got_ref[...].astype(jnp.float32)))


def combine_kernel(paired, mix_ref, *refs):
    *refs, out_hbm, out, sems = refs
    blocks = [r[...].astype(jnp.float32) for r in refs]
    rows = jnp.concatenate([b[:SLOTS] for b in blocks[:paired]] + blocks[paired:], axis=0)
    mix = mix_ref[...]
    tail = out.shape[1] // 7
    copies = []
    for i in range(7):
        here = pl.ds(i * tail, tail)
        piece = rows[:, i * tail : (i + 1) * tail] if i < 6 else unpack_tail(rows)
        piece = piece.astype(jnp.bfloat16)
        both = jnp.concatenate([piece, piece], axis=0)
        out[:, here] = jnp.dot(mix, both, preferred_element_type=jnp.float32).astype(jnp.bfloat16)
        copies.append(pltpu.make_async_copy(out.at[:, here], out_hbm.at[:, here], sems.at[i]))
        copies[-1].start()
    for copy in copies:
        copy.wait()


def per_device(tokens, norm_gain, expert_ids, gate_weights, w_gate, w_up, w_down):
    owners = lax.axis_size("exp")
    flight = owners // 2
    count, width = tokens.shape
    few = relative(flight)

    def local(kernel, outs, name, *args, limit=16):
        return pl.pallas_call(
            kernel,
            out_shape=outs,
            in_specs=[VMEM] * len(args),
            out_specs=(VMEM,) * len(outs),
            compiler_params=pltpu.CompilerParams(vmem_limit_bytes=limit * 2**20),
            cost_estimate=SMALL,
            name=name,
        )(*args)

    def full(*counts):
        return tuple(jax.ShapeDtypeStruct((n * SLOTS, width), jnp.bfloat16) for n in counts)

    def packed(*counts):
        shapes = [(n * SLOTS, packed_width(width)) for n in counts]
        return tuple(jax.ShapeDtypeStruct(shape, jnp.bfloat16) for shape in shapes)

    def swap(rows):
        return lax.ppermute(rows, "exp", [(n, n ^ 1) for n in range(owners)])

    def travel(rows, distances, across=0):
        pairs = [(n, n ^ (2 * distances[n % 2]) ^ across) for n in range(owners)]
        return lax.ppermute(rows, "exp", pairs)

    def stage(mix):
        weights = w_gate[0], w_up[0], w_down[0]
        outs = [jax.ShapeDtypeStruct(w.shape, w.dtype) for w in weights]
        return pl.pallas_call(
            stage_kernel,
            out_shape=(*outs, jax.ShapeDtypeStruct(mix.shape[::-1], mix.dtype)),
            in_specs=[VMEM] + [HBM] * 3,
            out_specs=(VMEM,) * 4,
            scratch_shapes=[pltpu.SemaphoreType.DMA((3 * PIECES,))],
            compiler_params=pltpu.CompilerParams(vmem_limit_bytes=16 * 2**20),
            cost_estimate=SMALL,
            name="stage",
        )(mix, *in_hbm(*weights))

    def experts(rows, weights):
        outs = full(*[flight // 2] * 4)
        return local(expert_kernel, outs, "experts", *rows, *weights, limit=24)

    def join(outs, mine, theirs):
        return local(join_kernel, packed(*outs), "join", mine, swap(theirs))

    def combine(mix, arrays, paired):
        return pl.pallas_call(
            functools.partial(combine_kernel, paired),
            out_shape=jax.ShapeDtypeStruct((count, width), jnp.bfloat16),
            in_specs=[VMEM] * (len(arrays) + 1),
            out_specs=HBM,
            scratch_shapes=[
                pltpu.VMEM((count, width), jnp.bfloat16),
                pltpu.SemaphoreType.DMA((7,)),
            ],
            compiler_params=pltpu.CompilerParams(vmem_limit_bytes=24 * 2**20),
            name="combine",
        )(mix, *arrays)

    first = packed(*[1] * flight) if few else packed(flight)
    mix, *outgoing = pl.pallas_call(
        functools.partial(dispatch_kernel, flight),
        out_shape=(jax.ShapeDtypeStruct((2 * flight * SLOTS, count), jnp.bfloat16),) + first,
        in_specs=[HBM] * 4,
        out_specs=(VMEM,) * (len(first) + 1),
        scratch_shapes=[
            pltpu.VMEM((count, width), jnp.bfloat16),
            pltpu.VMEM((1, width), jnp.float32),
            pltpu.VMEM(expert_ids.shape[::-1], jnp.int32),
            pltpu.VMEM(gate_weights.shape[::-1], jnp.float32),
            pltpu.SemaphoreType.DMA((3 + CHUNKS,)),
        ],
        compiler_params=pltpu.CompilerParams(vmem_limit_bytes=24 * 2**20),
        name="dispatch",
    )(*in_hbm(tokens, norm_gain, expert_ids.T, gate_weights.T))
    if not few:
        *weights, mix = stage(mix)
        groups = [list(range(core, owners, 2)) for core in range(2)]
        exchange = functools.partial(
            lax.all_to_all,
            axis_name="exp",
            split_axis=0,
            concat_axis=0,
            axis_index_groups=groups,
            tiled=True,
        )
        own = exchange(outgoing[0])
        mine_one, mine_two, theirs_one, theirs_two = experts([own, swap(own)], weights)
        half = flight // 2
        (joined_one,) = join([half], mine_one, theirs_one)
        (joined_two,) = join([half], mine_two, theirs_two)
        return combine(mix, [exchange(jnp.concatenate([joined_one, joined_two]))], 0)

    one, two, three = zip(*CARRIED)
    four = (SHARED, SHARED)
    first, second, third, first_across, second_across, third_across, shared, own = outgoing
    arrived = [
        travel(first, one),
        travel(second, two),
        travel(first_across, one[::-1], 1),
        travel(second_across, two[::-1], 1),
        travel(third, three),
        travel(third_across, three[::-1], 1),
        travel(shared, four),
    ]
    order = (1, 3, 0, 2, 4, 5, 6)
    arrived = [arrived[i] for i in order]
    *arrived, gate, up, down, mix = lax.optimization_barrier((*arrived, *stage(mix)))
    first, second, first_across, second_across, third, third_across, shared = (
        arrived[order.index(i)] for i in range(7)
    )
    rows = (first, first_across, second, second_across, third, third_across, shared, own)
    (rows,) = local(functools.partial(gather_kernel, 1), packed(flight), "gather", *rows)
    mine_one, mine_two, theirs_one, theirs_two = experts((rows, swap(rows)), (gate, up, down))
    first, second = join((2, 2), mine_one, theirs_one)
    third, third_across, shared, own = join((1, 1, 1, 1), mine_two, theirs_two)
    first, second, shared = travel(first, one), travel(second, two), travel(shared, four)
    third, third_across = travel(third, three), travel(third_across, three, 1)
    others = local(sift_kernel, packed(1, 1), "sift", first, second)
    others = [swap(a) for a in others]
    return combine(mix, [first, second, third, *others, third_across, shared, own], 2)


def solution(mesh):
    placed = (
        P(("group", "exp"), None),
        P(),
        P(("group", "exp"), None),
        P(("group", "exp"), None),
        P("exp", None, None),
        P("exp", None, None),
        P("exp", None, None),
    )
    return jax.shard_map(
        per_device, mesh=mesh, in_specs=placed, out_specs=P(("group", "exp"), None), check_vma=False
    )
```

```python
import functools

import jax
import jax.numpy as jnp
from jax import lax
from jax.experimental import pallas as pl
from jax.experimental.pallas import tpu as pltpu
from jax.sharding import PartitionSpec as P

SLOTS = 8
CHUNKS = 4
PIECES = 4
LANES = 128

VMEM = pl.BlockSpec(memory_space=pltpu.VMEM)
SMALL = pl.CostEstimate(flops=1, bytes_accessed=1, transcendentals=0)
HBM = pl.BlockSpec(memory_space=pltpu.HBM)


def in_hbm(*arrays):
    return [pltpu.with_memory_space_constraint(a, pltpu.HBM) for a in arrays]


def relative(flight):
    return flight == 8


CARRIED = ((4, 1, 5), (6, 2, 7))
SHARED = 3


def block_order(flight, core):
    if not relative(flight):
        return range(flight)
    return CARRIED[core] + CARRIED[1 - core] + (SHARED, 0)


def packed_width(width):
    return width // 7 * 6 + LANES


def pack(rows):
    blocks = rows.reshape(-1, SLOTS, rows.shape[1])
    tail = rows.shape[1] // 7
    main = blocks[:, :, : 6 * tail]
    moved = jnp.concatenate([blocks[:, j : j + 1, 6 * tail :] for j in range(6)], axis=2)
    row = lax.broadcasted_iota(jnp.int32, main.shape, 1)
    main = jnp.where(row == SLOTS - 1, moved, main)
    row = row[:, :, :LANES]
    extra = jnp.zeros(row.shape, rows.dtype)
    for k in range(tail // LANES):
        start = 6 * tail + k * LANES
        extra = jnp.where(row == k, blocks[:, 6:7, start : start + LANES], extra)
    return jnp.concatenate([main, extra], axis=2).reshape(rows.shape[0], -1)


def unpack_tail(packed):
    blocks = packed.reshape(-1, SLOTS, packed.shape[1])
    tail = (packed.shape[1] - LANES) // 6
    last = jnp.concatenate(
        [blocks[:, k : k + 1, 6 * tail :] for k in range(tail // LANES)], axis=2
    )
    row = lax.broadcasted_iota(jnp.int32, (blocks.shape[0], SLOTS, tail), 1)
    end = jnp.where(row == 6, last, 0.0)
    for j in range(6):
        end = jnp.where(row == j, blocks[:, 7:8, j * tail : (j + 1) * tail], end)
    return end.reshape(packed.shape[0], -1)


def unpack(packed):
    return jnp.concatenate([packed[:, : packed.shape[1] - LANES], unpack_tail(packed)], axis=1)


def store(refs, rows):
    at = 0
    for ref in refs:
        ref[...] = rows[at : at + ref.shape[0]].astype(ref.dtype)
        at += ref.shape[0]


def dispatch_kernel(flight, tok_hbm, gain_hbm, ids_hbm, gw_hbm, mix_ref, *rest):
    *outs, tok, gain, ids, gw, sems = rest
    count = tok.shape[0]
    part = count // CHUNKS
    small = [
        pltpu.make_async_copy(ids_hbm, ids, sems.at[0]),
        pltpu.make_async_copy(gw_hbm, gw, sems.at[1]),
        pltpu.make_async_copy(gain_hbm, gain.at[0], sems.at[2]),
    ]
    large = [
        pltpu.make_async_copy(
            tok_hbm.at[pl.ds(i * part, part)], tok.at[pl.ds(i * part, part)], sems.at[3 + i]
        )
        for i in range(CHUNKS)
    ]
    for copy in small + large:
        copy.start()
    small[0].wait()
    small[1].wait()
    experts = lax.broadcasted_iota(jnp.int32, (flight, count), 0)
    if relative(flight):
        place = experts
        me = lax.axis_index("exp")
        for i, (even, odd) in enumerate(zip(block_order(flight, 0), block_order(flight, 1))):
            experts = jnp.where(place == i, jnp.where(me % 2 == 0, even, odd) ^ (me // 2), experts)
    chosen = jnp.zeros((flight, count), jnp.float32)
    gates = jnp.zeros((flight, count), jnp.float32)
    for k in range(ids.shape[0]):
        hit = ids[k : k + 1, :] == experts
        chosen = jnp.where(hit, 1.0, chosen)
        gates = jnp.where(hit, gw[k : k + 1, :], gates)
    before = (
        lax.broadcasted_iota(jnp.int32, (count, count), 0)
        < lax.broadcasted_iota(jnp.int32, (count, count), 1)
    ).astype(jnp.bfloat16)
    rank = jnp.dot(chosen.astype(jnp.bfloat16), before, preferred_element_type=jnp.float32)
    rank = jnp.where(chosen > 0.0, rank, -1.0)

    slot = lax.broadcasted_iota(jnp.int32, (flight, SLOTS, count), 1).astype(jnp.float32)
    taken = rank[:, None, :] == slot
    pick = jnp.where(taken, 1.0, 0.0).reshape(flight * SLOTS, count).astype(jnp.bfloat16)
    mix = jnp.where(taken, gates[:, None, :], 0.0).reshape(flight * SLOTS, count)
    high = mix.astype(jnp.bfloat16)
    mix_ref[: flight * SLOTS, :] = high
    mix_ref[flight * SLOTS :, :] = (mix - high.astype(jnp.float32)).astype(jnp.bfloat16)

    for copy in large:
        copy.wait()
    wide = jnp.dot(pick, tok[...], preferred_element_type=jnp.float32)
    mean_square = jnp.mean(wide * wide, axis=1, keepdims=True)
    small[2].wait()
    rows = (wide * lax.rsqrt(mean_square + 1e-06) * gain[...]).astype(jnp.bfloat16)
    rows = rows.astype(jnp.float32)
    blocks = pack(rows)
    if len(outs) == 1:
        store(outs, blocks)
    else:
        order = [0, 3, 1, 2, 4, 5, 7, 6, 7]
        blocks = [blocks[i * SLOTS : (i + 1) * SLOTS] for i in order]
        store(outs, jnp.concatenate(blocks, axis=0))


def stage_kernel(mix_ref, *refs):
    *refs, turned_ref, sems = refs
    sources, targets = refs[:3], refs[3:]
    copies = []
    for at, (source, target) in enumerate(zip(sources, targets)):
        rows = source.shape[0] // PIECES
        for i in range(PIECES):
            here = pl.ds(i * rows, rows)
            copies.append(
                pltpu.make_async_copy(source.at[here], target.at[here], sems.at[at * PIECES + i])
            )
    for copy in copies:
        copy.start()
    turned_ref[...] = mix_ref[...].T
    for copy in copies:
        copy.wait()


def together(refs):
    return jnp.concatenate([b[...].astype(jnp.float32) for b in refs], axis=0)


def merge_kernel(kept_ref, got_ref, *outs):
    *outs, own_out = outs
    kept, got = kept_ref[...].astype(jnp.float32), got_ref[...].astype(jnp.float32)
    for i, out in enumerate(outs):
        here = slice(i * SLOTS, (i + 1) * SLOTS)
        out[...] = jnp.concatenate([kept[here], got[here]], axis=0).astype(jnp.bfloat16)
    own_out[...] = got[len(outs) * SLOTS :].astype(jnp.bfloat16)


def gather_kernel(count, *refs):
    store(refs[-count:], together(refs[:-count]))


def sift_kernel(*refs):
    count = len(refs) // 2
    for ref, out in zip(refs[:count], refs[count:]):
        out[...] = ref[...].astype(jnp.float32)[SLOTS:].astype(jnp.bfloat16)


def expert_kernel(*refs):
    *rows, gate_ref, up_ref, down_ref, own_one, own_two, other_one, other_two = refs
    x = unpack(together(rows)).astype(jnp.bfloat16)
    gate_v = jnp.dot(x, gate_ref[...], preferred_element_type=jnp.float32)
    up_v = jnp.dot(x, up_ref[...], preferred_element_type=jnp.float32)
    hidden = (gate_v / (1.0 + jnp.exp(-gate_v)) * up_v).astype(jnp.bfloat16)
    part = jnp.dot(hidden, down_ref[...], preferred_element_type=jnp.float32)
    store((own_one, own_two, other_one, other_two), part)


def join_kernel(mine_ref, got_ref, *outs):
    store(outs, pack(mine_ref[...].astype(jnp.float32) + got_ref[...].astype(jnp.float32)))


def combine_kernel(paired, mix_ref, *refs):
    *refs, out_hbm, out, sems = refs
    blocks = [r[...].astype(jnp.float32) for r in refs]
    rows = jnp.concatenate([b[:SLOTS] for b in blocks[:paired]] + blocks[paired:], axis=0)
    mix = mix_ref[...]
    tail = out.shape[1] // 7
    copies = []
    for i in range(7):
        here = pl.ds(i * tail, tail)
        piece = rows[:, i * tail : (i + 1) * tail] if i < 6 else unpack_tail(rows)
        piece = piece.astype(jnp.bfloat16)
        both = jnp.concatenate([piece, piece], axis=0)
        out[:, here] = jnp.dot(mix, both, preferred_element_type=jnp.float32).astype(jnp.bfloat16)
        copies.append(pltpu.make_async_copy(out.at[:, here], out_hbm.at[:, here], sems.at[i]))
        copies[-1].start()
    for copy in copies:
        copy.wait()


def per_device(tokens, norm_gain, expert_ids, gate_weights, w_gate, w_up, w_down):
    owners = lax.axis_size("exp")
    flight = owners // 2
    count, width = tokens.shape
    few = relative(flight)

    def local(kernel, outs, name, *args, limit=16):
        return pl.pallas_call(
            kernel,
            out_shape=outs,
            in_specs=[VMEM] * len(args),
            out_specs=(VMEM,) * len(outs),
            compiler_params=pltpu.CompilerParams(vmem_limit_bytes=limit * 2**20),
            cost_estimate=SMALL,
            name=name,
        )(*args)

    def full(*counts):
        return tuple(jax.ShapeDtypeStruct((n * SLOTS, width), jnp.bfloat16) for n in counts)

    def packed(*counts):
        shapes = [(n * SLOTS, packed_width(width)) for n in counts]
        return tuple(jax.ShapeDtypeStruct(shape, jnp.bfloat16) for shape in shapes)

    def swap(rows):
        return lax.ppermute(rows, "exp", [(n, n ^ 1) for n in range(owners)])

    def travel(rows, distances, across=0):
        pairs = [(n, n ^ (2 * distances[n % 2]) ^ across) for n in range(owners)]
        return lax.ppermute(rows, "exp", pairs)

    def stage(mix):
        weights = w_gate[0], w_up[0], w_down[0]
        outs = [jax.ShapeDtypeStruct(w.shape, w.dtype) for w in weights]
        return pl.pallas_call(
            stage_kernel,
            out_shape=(*outs, jax.ShapeDtypeStruct(mix.shape[::-1], mix.dtype)),
            in_specs=[VMEM] + [HBM] * 3,
            out_specs=(VMEM,) * 4,
            scratch_shapes=[pltpu.SemaphoreType.DMA((3 * PIECES,))],
            compiler_params=pltpu.CompilerParams(vmem_limit_bytes=16 * 2**20),
            cost_estimate=SMALL,
            name="stage",
        )(mix, *in_hbm(*weights))

    def experts(rows, weights):
        outs = full(*[flight // 2] * 4)
        return local(expert_kernel, outs, "experts", *rows, *weights, limit=24)

    def join(outs, mine, theirs):
        return local(join_kernel, packed(*outs), "join", mine, swap(theirs))

    def combine(mix, arrays, paired):
        return pl.pallas_call(
            functools.partial(combine_kernel, paired),
            out_shape=jax.ShapeDtypeStruct((count, width), jnp.bfloat16),
            in_specs=[VMEM] * (len(arrays) + 1),
            out_specs=HBM,
            scratch_shapes=[
                pltpu.VMEM((count, width), jnp.bfloat16),
                pltpu.SemaphoreType.DMA((7,)),
            ],
            compiler_params=pltpu.CompilerParams(vmem_limit_bytes=24 * 2**20),
            name="combine",
        )(mix, *arrays)

    first = packed(1, 1, 2, 3, 1, 1) if few else packed(flight)
    mix, *outgoing = pl.pallas_call(
        functools.partial(dispatch_kernel, flight),
        out_shape=(jax.ShapeDtypeStruct((2 * flight * SLOTS, count), jnp.bfloat16),) + first,
        in_specs=[HBM] * 4,
        out_specs=(VMEM,) * (len(first) + 1),
        scratch_shapes=[
            pltpu.VMEM((count, width), jnp.bfloat16),
            pltpu.VMEM((1, width), jnp.float32),
            pltpu.VMEM(expert_ids.shape[::-1], jnp.int32),
            pltpu.VMEM(gate_weights.shape[::-1], jnp.float32),
            pltpu.SemaphoreType.DMA((3 + CHUNKS,)),
        ],
        compiler_params=pltpu.CompilerParams(vmem_limit_bytes=24 * 2**20),
        name="dispatch",
    )(*in_hbm(tokens, norm_gain, expert_ids.T, gate_weights.T))
    if not few:
        *weights, mix = stage(mix)
        groups = [list(range(core, owners, 2)) for core in range(2)]
        exchange = functools.partial(
            lax.all_to_all,
            axis_name="exp",
            split_axis=0,
            concat_axis=0,
            axis_index_groups=groups,
            tiled=True,
        )
        own = exchange(outgoing[0])
        mine_one, mine_two, theirs_one, theirs_two = experts([own, swap(own)], weights)
        half = flight // 2
        (joined_one,) = join([half], mine_one, theirs_one)
        (joined_two,) = join([half], mine_two, theirs_two)
        return combine(mix, [exchange(jnp.concatenate([joined_one, joined_two]))], 0)

    one, two, three = zip(*CARRIED)
    four = (SHARED, SHARED)
    first, first_across, kept, given, shared, own = outgoing
    second, third, other_own = local(merge_kernel, packed(2, 2, 1), "merge", kept, swap(given))
    first, first_across = travel(first, one), travel(first_across, one[::-1], 1)
    shared, first, first_across, gate, up, down, mix = lax.optimization_barrier(
        (shared, first, first_across, *stage(mix))
    )
    second, third, shared = travel(second, two), travel(third, three), travel(shared, four)
    arrived = lax.optimization_barrier((first, first_across, second, third, shared))
    kernel = functools.partial(gather_kernel, 2)
    rows = local(kernel, packed(4, 3), "gather", *arrived)
    mine_one, mine_two, theirs_one, theirs_two = experts(
        (*rows, own, *[swap(a) for a in rows], other_own), (gate, up, down)
    )

    first, second = join((2, 2), mine_one, theirs_one)
    third, third_across, shared, own = join((1, 1, 1, 1), mine_two, theirs_two)
    first, second, shared = travel(first, one), travel(second, two), travel(shared, four)
    third, third_across = travel(third, three), travel(third_across, three, 1)
    others = local(sift_kernel, packed(1, 1), "sift", first, second)
    others = [swap(a) for a in others]
    return combine(mix, [first, second, third, *others, third_across, shared, own], 2)


def solution(mesh):
    placed = (
        P(("group", "exp"), None),
        P(),
        P(("group", "exp"), None),
        P(("group", "exp"), None),
        P("exp", None, None),
        P("exp", None, None),
        P("exp", None, None),
    )
    return jax.shard_map(
        per_device, mesh=mesh, in_specs=placed, out_specs=P(("group", "exp"), None), check_vma=False
    )
```

```python
import functools

import jax
import jax.numpy as jnp
from jax import lax
from jax.experimental import pallas as pl
from jax.experimental.pallas import tpu as pltpu
from jax.sharding import PartitionSpec as P

SLOTS = 8
CHUNKS = 4
PIECES = 4
LANES = 128

VMEM = pl.BlockSpec(memory_space=pltpu.VMEM)
SMALL = pl.CostEstimate(flops=1, bytes_accessed=1, transcendentals=0)
HBM = pl.BlockSpec(memory_space=pltpu.HBM)


def in_hbm(*arrays):
    return [pltpu.with_memory_space_constraint(a, pltpu.HBM) for a in arrays]


def relative(flight):
    return flight == 8


CARRIED = ((4, 1, 5), (6, 2, 7))
SHARED = 3


def block_order(flight, core):
    if not relative(flight):
        return range(flight)
    return CARRIED[core] + CARRIED[1 - core] + (SHARED, 0)


def packed_width(width):
    return width // 7 * 6 + LANES


def pack(rows):
    blocks = rows.reshape(-1, SLOTS, rows.shape[1])
    tail = rows.shape[1] // 7
    main = blocks[:, :, : 6 * tail]
    moved = jnp.concatenate([blocks[:, j : j + 1, 6 * tail :] for j in range(6)], axis=2)
    row = lax.broadcasted_iota(jnp.int32, main.shape, 1)
    main = jnp.where(row == SLOTS - 1, moved, main)
    row = row[:, :, :LANES]
    extra = jnp.zeros(row.shape, rows.dtype)
    for k in range(tail // LANES):
        start = 6 * tail + k * LANES
        extra = jnp.where(row == k, blocks[:, 6:7, start : start + LANES], extra)
    return jnp.concatenate([main, extra], axis=2).reshape(rows.shape[0], -1)


def unpack_tail(packed):
    blocks = packed.reshape(-1, SLOTS, packed.shape[1])
    tail = (packed.shape[1] - LANES) // 6
    last = jnp.concatenate(
        [blocks[:, k : k + 1, 6 * tail :] for k in range(tail // LANES)], axis=2
    )
    row = lax.broadcasted_iota(jnp.int32, (blocks.shape[0], SLOTS, tail), 1)
    end = jnp.where(row == 6, last, 0.0)
    for j in range(6):
        end = jnp.where(row == j, blocks[:, 7:8, j * tail : (j + 1) * tail], end)
    return end.reshape(packed.shape[0], -1)


def unpack(packed):
    return jnp.concatenate([packed[:, : packed.shape[1] - LANES], unpack_tail(packed)], axis=1)


def store(refs, rows):
    at = 0
    for ref in refs:
        ref[...] = rows[at : at + ref.shape[0]].astype(ref.dtype)
        at += ref.shape[0]


def dispatch_kernel(flight, tok_hbm, gain_hbm, ids_hbm, gw_hbm, mix_ref, *rest):
    *outs, tok, gain, ids, gw, sems = rest
    count = tok.shape[0]
    part = count // CHUNKS
    small = [
        pltpu.make_async_copy(ids_hbm, ids, sems.at[0]),
        pltpu.make_async_copy(gw_hbm, gw, sems.at[1]),
        pltpu.make_async_copy(gain_hbm, gain.at[0], sems.at[2]),
    ]
    large = [
        pltpu.make_async_copy(
            tok_hbm.at[pl.ds(i * part, part)], tok.at[pl.ds(i * part, part)], sems.at[3 + i]
        )
        for i in range(CHUNKS)
    ]
    for copy in small + large:
        copy.start()
    small[0].wait()
    small[1].wait()
    experts = lax.broadcasted_iota(jnp.int32, (flight, count), 0)
    if relative(flight):
        place = experts
        me = lax.axis_index("exp")
        for i, (even, odd) in enumerate(zip(block_order(flight, 0), block_order(flight, 1))):
            experts = jnp.where(place == i, jnp.where(me % 2 == 0, even, odd) ^ (me // 2), experts)
    chosen = jnp.zeros((flight, count), jnp.float32)
    gates = jnp.zeros((flight, count), jnp.float32)
    for k in range(ids.shape[0]):
        hit = ids[k : k + 1, :] == experts
        chosen = jnp.where(hit, 1.0, chosen)
        gates = jnp.where(hit, gw[k : k + 1, :], gates)
    before = (
        lax.broadcasted_iota(jnp.int32, (count, count), 0)
        < lax.broadcasted_iota(jnp.int32, (count, count), 1)
    ).astype(jnp.bfloat16)
    rank = jnp.dot(chosen.astype(jnp.bfloat16), before, preferred_element_type=jnp.float32)
    rank = jnp.where(chosen > 0.0, rank, -1.0)

    slot = lax.broadcasted_iota(jnp.int32, (flight, SLOTS, count), 1).astype(jnp.float32)
    taken = rank[:, None, :] == slot
    pick = jnp.where(taken, 1.0, 0.0).reshape(flight * SLOTS, count).astype(jnp.bfloat16)
    mix = jnp.where(taken, gates[:, None, :], 0.0).reshape(flight * SLOTS, count)
    high = mix.astype(jnp.bfloat16)
    mix_ref[: flight * SLOTS, :] = high
    mix_ref[flight * SLOTS :, :] = (mix - high.astype(jnp.float32)).astype(jnp.bfloat16)

    for copy in large:
        copy.wait()
    wide = jnp.dot(pick, tok[...], preferred_element_type=jnp.float32)
    mean_square = jnp.mean(wide * wide, axis=1, keepdims=True)
    small[2].wait()
    rows = (wide * lax.rsqrt(mean_square + 1e-06) * gain[...]).astype(jnp.bfloat16)
    rows = rows.astype(jnp.float32)
    blocks = pack(rows)
    if len(outs) == 1:
        store(outs, blocks)
    else:
        order = [0, 1, 3, 4, 7, 2, 5, 6, 7]
        blocks = [blocks[i * SLOTS : (i + 1) * SLOTS] for i in order]
        store(outs, jnp.concatenate(blocks, axis=0))


def stage_kernel(mix_ref, *refs):
    *refs, turned_ref, sems = refs
    sources, targets = refs[:3], refs[3:]
    copies = []
    for at, (source, target) in enumerate(zip(sources, targets)):
        rows = source.shape[0] // PIECES
        for i in range(PIECES):
            here = pl.ds(i * rows, rows)
            copies.append(
                pltpu.make_async_copy(source.at[here], target.at[here], sems.at[at * PIECES + i])
            )
    for copy in copies:
        copy.start()
    turned_ref[...] = mix_ref[...].T
    for copy in copies:
        copy.wait()


def together(refs):
    return jnp.concatenate([b[...].astype(jnp.float32) for b in refs], axis=0)


def merge_kernel(kept_ref, got_ref, *outs):
    *outs, own_out = outs
    kept, got = kept_ref[...].astype(jnp.float32), got_ref[...].astype(jnp.float32)
    for i, out in enumerate(outs):
        here = slice(i * SLOTS, (i + 1) * SLOTS)
        out[...] = jnp.concatenate([kept[here], got[here]], axis=0).astype(jnp.bfloat16)
    own_out[...] = got[len(outs) * SLOTS :].astype(jnp.bfloat16)


def gather_kernel(count, *refs):
    store(refs[-count:], together(refs[:-count]))


def sift_kernel(*refs):
    count = len(refs) // 2
    for ref, out in zip(refs[:count], refs[count:]):
        out[...] = ref[...].astype(jnp.float32)[SLOTS:].astype(jnp.bfloat16)


def expert_kernel(*refs):
    *rows, gate_ref, up_ref, down_ref, own_one, own_two, other_one, other_two = refs
    x = unpack(together(rows)).astype(jnp.bfloat16)
    gate_v = jnp.dot(x, gate_ref[...], preferred_element_type=jnp.float32)
    up_v = jnp.dot(x, up_ref[...], preferred_element_type=jnp.float32)
    hidden = (gate_v / (1.0 + jnp.exp(-gate_v)) * up_v).astype(jnp.bfloat16)
    part = jnp.dot(hidden, down_ref[...], preferred_element_type=jnp.float32)
    store((own_one, own_two, other_one, other_two), part)


def join_kernel(mine_ref, got_ref, *outs):
    store(outs, pack(mine_ref[...].astype(jnp.float32) + got_ref[...].astype(jnp.float32)))


def combine_kernel(paired, mix_ref, *refs):
    *refs, out_hbm, out, sems = refs
    blocks = [r[...].astype(jnp.float32) for r in refs]
    rows = jnp.concatenate([b[:SLOTS] for b in blocks[:paired]] + blocks[paired:], axis=0)
    mix = mix_ref[...]
    tail = out.shape[1] // 7
    copies = []
    for i in range(7):
        here = pl.ds(i * tail, tail)
        piece = rows[:, i * tail : (i + 1) * tail] if i < 6 else unpack_tail(rows)
        piece = piece.astype(jnp.bfloat16)
        both = jnp.concatenate([piece, piece], axis=0)
        out[:, here] = jnp.dot(mix, both, preferred_element_type=jnp.float32).astype(jnp.bfloat16)
        copies.append(pltpu.make_async_copy(out.at[:, here], out_hbm.at[:, here], sems.at[i]))
        copies[-1].start()
    for copy in copies:
        copy.wait()


def per_device(tokens, norm_gain, expert_ids, gate_weights, w_gate, w_up, w_down):
    owners = lax.axis_size("exp")
    flight = owners // 2
    count, width = tokens.shape
    few = relative(flight)

    def local(kernel, outs, name, *args, limit=16):
        return pl.pallas_call(
            kernel,
            out_shape=outs,
            in_specs=[VMEM] * len(args),
            out_specs=(VMEM,) * len(outs),
            compiler_params=pltpu.CompilerParams(vmem_limit_bytes=limit * 2**20),
            cost_estimate=SMALL,
            name=name,
        )(*args)

    def full(*counts):
        return tuple(jax.ShapeDtypeStruct((n * SLOTS, width), jnp.bfloat16) for n in counts)

    def packed(*counts):
        shapes = [(n * SLOTS, packed_width(width)) for n in counts]
        return tuple(jax.ShapeDtypeStruct(shape, jnp.bfloat16) for shape in shapes)

    def swap(rows):
        return lax.ppermute(rows, "exp", [(n, n ^ 1) for n in range(owners)])

    def travel(rows, distances, across=0):
        pairs = [(n, n ^ (2 * distances[n % 2]) ^ across) for n in range(owners)]
        return lax.ppermute(rows, "exp", pairs)

    def stage(mix):
        weights = w_gate[0], w_up[0], w_down[0]
        outs = [jax.ShapeDtypeStruct(w.shape, w.dtype) for w in weights]
        return pl.pallas_call(
            stage_kernel,
            out_shape=(*outs, jax.ShapeDtypeStruct(mix.shape[::-1], mix.dtype)),
            in_specs=[VMEM] + [HBM] * 3,
            out_specs=(VMEM,) * 4,
            scratch_shapes=[pltpu.SemaphoreType.DMA((3 * PIECES,))],
            compiler_params=pltpu.CompilerParams(vmem_limit_bytes=16 * 2**20),
            cost_estimate=SMALL,
            name="stage",
        )(mix, *in_hbm(*weights))

    def experts(rows, weights):
        outs = full(*[flight // 2] * 4)
        return local(expert_kernel, outs, "experts", *rows, *weights, limit=24)

    def join(outs, mine, theirs):
        return local(join_kernel, packed(*outs), "join", mine, swap(theirs))

    def combine(mix, arrays, paired):
        return pl.pallas_call(
            functools.partial(combine_kernel, paired),
            out_shape=jax.ShapeDtypeStruct((count, width), jnp.bfloat16),
            in_specs=[VMEM] * (len(arrays) + 1),
            out_specs=HBM,
            scratch_shapes=[
                pltpu.VMEM((count, width), jnp.bfloat16),
                pltpu.SemaphoreType.DMA((7,)),
            ],
            compiler_params=pltpu.CompilerParams(vmem_limit_bytes=24 * 2**20),
            name="combine",
        )(mix, *arrays)

    first = packed(2, 3, 1, 1, 1, 1) if few else packed(flight)
    mix, *outgoing = pl.pallas_call(
        functools.partial(dispatch_kernel, flight),
        out_shape=(jax.ShapeDtypeStruct((2 * flight * SLOTS, count), jnp.bfloat16),) + first,
        in_specs=[HBM] * 4,
        out_specs=(VMEM,) * (len(first) + 1),
        scratch_shapes=[
            pltpu.VMEM((count, width), jnp.bfloat16),
            pltpu.VMEM((1, width), jnp.float32),
            pltpu.VMEM(expert_ids.shape[::-1], jnp.int32),
            pltpu.VMEM(gate_weights.shape[::-1], jnp.float32),
            pltpu.SemaphoreType.DMA((3 + CHUNKS,)),
        ],
        compiler_params=pltpu.CompilerParams(vmem_limit_bytes=24 * 2**20),
        name="dispatch",
    )(*in_hbm(tokens, norm_gain, expert_ids.T, gate_weights.T))
    if not few:
        *weights, mix = stage(mix)
        groups = [list(range(core, owners, 2)) for core in range(2)]
        exchange = functools.partial(
            lax.all_to_all,
            axis_name="exp",
            split_axis=0,
            concat_axis=0,
            axis_index_groups=groups,
            tiled=True,
        )
        own = exchange(outgoing[0])
        mine_one, mine_two, theirs_one, theirs_two = experts([own, swap(own)], weights)
        half = flight // 2
        (joined_one,) = join([half], mine_one, theirs_one)
        (joined_two,) = join([half], mine_two, theirs_two)
        return combine(mix, [exchange(jnp.concatenate([joined_one, joined_two]))], 0)

    one, two, three = zip(*CARRIED)
    four = (SHARED, SHARED)
    kept, given, third, third_across, shared, own = outgoing
    first, second, other_own = local(merge_kernel, packed(2, 2, 1), "merge", kept, swap(given))
    arrived = (
        travel(first, one),
        travel(second, two),
        travel(third, three),
        travel(third_across, three[::-1], 1),
        travel(shared, four),
    )
    *arrived, gate, up, down, mix = lax.optimization_barrier((*arrived, *stage(mix)))
    kernel = functools.partial(gather_kernel, 2)
    rows = local(kernel, packed(4, 3), "gather", *arrived)
    mine_one, mine_two, theirs_one, theirs_two = experts(
        (*rows, own, *[swap(a) for a in rows], other_own), (gate, up, down)
    )

    first, second = join((2, 2), mine_one, theirs_one)
    third, third_across, shared, own = join((1, 1, 1, 1), mine_two, theirs_two)
    first, second, shared = travel(first, one), travel(second, two), travel(shared, four)
    third, third_across = travel(third, three), travel(third_across, three, 1)
    others = local(sift_kernel, packed(1, 1), "sift", first, second)
    others = [swap(a) for a in others]
    return combine(mix, [first, second, third, *others, third_across, shared, own], 2)


def solution(mesh):
    placed = (
        P(("group", "exp"), None),
        P(),
        P(("group", "exp"), None),
        P(("group", "exp"), None),
        P("exp", None, None),
        P("exp", None, None),
        P("exp", None, None),
    )
    return jax.shard_map(
        per_device, mesh=mesh, in_specs=placed, out_specs=P(("group", "exp"), None), check_vma=False
    )
```

```python
import functools

import jax
import jax.numpy as jnp
from jax import lax
from jax.experimental import pallas as pl
from jax.experimental.pallas import tpu as pltpu
from jax.sharding import PartitionSpec as P

SLOTS = 8
CHUNKS = 4
PIECES = 4
LANES = 128

VMEM = pl.BlockSpec(memory_space=pltpu.VMEM)
SMALL = pl.CostEstimate(flops=1, bytes_accessed=1, transcendentals=0)
HBM = pl.BlockSpec(memory_space=pltpu.HBM)


def in_hbm(*arrays):
    return [pltpu.with_memory_space_constraint(a, pltpu.HBM) for a in arrays]


def relative(flight):
    return flight == 8


CARRIED = ((4, 1, 5), (6, 2, 7))
SHARED = 3


def block_order(flight, core):
    if not relative(flight):
        return range(flight)
    return CARRIED[core] + CARRIED[1 - core] + (SHARED, 0)


def packed_width(width):
    return width // 7 * 6 + LANES


def pack(rows):
    blocks = rows.reshape(-1, SLOTS, rows.shape[1])
    tail = rows.shape[1] // 7
    main = blocks[:, :, : 6 * tail]
    moved = jnp.concatenate([blocks[:, j : j + 1, 6 * tail :] for j in range(6)], axis=2)
    row = lax.broadcasted_iota(jnp.int32, main.shape, 1)
    main = jnp.where(row == SLOTS - 1, moved, main)
    row = row[:, :, :LANES]
    extra = jnp.zeros(row.shape, rows.dtype)
    for k in range(tail // LANES):
        start = 6 * tail + k * LANES
        extra = jnp.where(row == k, blocks[:, 6:7, start : start + LANES], extra)
    return jnp.concatenate([main, extra], axis=2).reshape(rows.shape[0], -1)


def unpack_tail(packed):
    blocks = packed.reshape(-1, SLOTS, packed.shape[1])
    tail = (packed.shape[1] - LANES) // 6
    last = jnp.concatenate(
        [blocks[:, k : k + 1, 6 * tail :] for k in range(tail // LANES)], axis=2
    )
    row = lax.broadcasted_iota(jnp.int32, (blocks.shape[0], SLOTS, tail), 1)
    end = jnp.where(row == 6, last, 0.0)
    for j in range(6):
        end = jnp.where(row == j, blocks[:, 7:8, j * tail : (j + 1) * tail], end)
    return end.reshape(packed.shape[0], -1)


def unpack(packed):
    return jnp.concatenate([packed[:, : packed.shape[1] - LANES], unpack_tail(packed)], axis=1)


def store(refs, rows):
    at = 0
    for ref in refs:
        ref[...] = rows[at : at + ref.shape[0]].astype(ref.dtype)
        at += ref.shape[0]


def dispatch_kernel(flight, tok_hbm, gain_hbm, ids_hbm, gw_hbm, mix_ref, *rest):
    *outs, tok, gain, ids, gw, sems = rest
    count = tok.shape[0]
    part = count // CHUNKS
    small = [
        pltpu.make_async_copy(ids_hbm, ids, sems.at[0]),
        pltpu.make_async_copy(gw_hbm, gw, sems.at[1]),
        pltpu.make_async_copy(gain_hbm, gain.at[0], sems.at[2]),
    ]
    large = [
        pltpu.make_async_copy(
            tok_hbm.at[pl.ds(i * part, part)], tok.at[pl.ds(i * part, part)], sems.at[3 + i]
        )
        for i in range(CHUNKS)
    ]
    for copy in small + large:
        copy.start()
    small[0].wait()
    small[1].wait()
    experts = lax.broadcasted_iota(jnp.int32, (flight, count), 0)
    if relative(flight):
        place = experts
        me = lax.axis_index("exp")
        for i, (even, odd) in enumerate(zip(block_order(flight, 0), block_order(flight, 1))):
            experts = jnp.where(place == i, jnp.where(me % 2 == 0, even, odd) ^ (me // 2), experts)
    chosen = jnp.zeros((flight, count), jnp.float32)
    gates = jnp.zeros((flight, count), jnp.float32)
    for k in range(ids.shape[0]):
        hit = ids[k : k + 1, :] == experts
        chosen = jnp.where(hit, 1.0, chosen)
        gates = jnp.where(hit, gw[k : k + 1, :], gates)
    before = (
        lax.broadcasted_iota(jnp.int32, (count, count), 0)
        < lax.broadcasted_iota(jnp.int32, (count, count), 1)
    ).astype(jnp.bfloat16)
    rank = jnp.dot(chosen.astype(jnp.bfloat16), before, preferred_element_type=jnp.float32)
    rank = jnp.where(chosen > 0.0, rank, -1.0)

    slot = lax.broadcasted_iota(jnp.int32, (flight, SLOTS, count), 1).astype(jnp.float32)
    taken = rank[:, None, :] == slot
    pick = jnp.where(taken, 1.0, 0.0).reshape(flight * SLOTS, count).astype(jnp.bfloat16)
    mix = jnp.where(taken, gates[:, None, :], 0.0).reshape(flight * SLOTS, count)
    high = mix.astype(jnp.bfloat16)
    mix_ref[: flight * SLOTS, :] = high
    mix_ref[flight * SLOTS :, :] = (mix - high.astype(jnp.float32)).astype(jnp.bfloat16)

    for copy in large:
        copy.wait()
    wide = jnp.dot(pick, tok[...], preferred_element_type=jnp.float32)
    mean_square = jnp.mean(wide * wide, axis=1, keepdims=True)
    small[2].wait()
    rows = (wide * lax.rsqrt(mean_square + 1e-06) * gain[...]).astype(jnp.bfloat16)
    rows = rows.astype(jnp.float32)
    blocks = pack(rows)
    if len(outs) == 1:
        store(outs, blocks)
    else:
        kept, given = 3 * SLOTS, 6 * SLOTS
        store(outs[:1], blocks[:kept])
        store(outs[1:2], jnp.concatenate([blocks[kept:given], blocks[given + SLOTS :]], axis=0))
        store(outs[2:], blocks[given:])


def stage_kernel(mix_ref, *refs):
    *refs, turned_ref, sems = refs
    sources, targets = refs[:3], refs[3:]
    copies = []
    for at, (source, target) in enumerate(zip(sources, targets)):
        rows = source.shape[0] // PIECES
        for i in range(PIECES):
            here = pl.ds(i * rows, rows)
            copies.append(
                pltpu.make_async_copy(source.at[here], target.at[here], sems.at[at * PIECES + i])
            )
    for copy in copies:
        copy.start()
    turned_ref[...] = mix_ref[...].T
    for copy in copies:
        copy.wait()


def together(refs):
    return jnp.concatenate([b[...].astype(jnp.float32) for b in refs], axis=0)


def merge_kernel(kept_ref, got_ref, *outs):
    *outs, own_out = outs
    kept, got = kept_ref[...].astype(jnp.float32), got_ref[...].astype(jnp.float32)
    for i, out in enumerate(outs):
        here = slice(i * SLOTS, (i + 1) * SLOTS)
        out[...] = jnp.concatenate([kept[here], got[here]], axis=0).astype(jnp.bfloat16)
    own_out[...] = got[len(outs) * SLOTS :].astype(jnp.bfloat16)


def gather_kernel(count, *refs):
    store(refs[-count:], together(refs[:-count]))


def sift_kernel(*refs):
    count = len(refs) // 2
    for ref, out in zip(refs[:count], refs[count:]):
        out[...] = ref[...].astype(jnp.float32)[SLOTS:].astype(jnp.bfloat16)


def expert_kernel(*refs):
    *rows, gate_ref, up_ref, down_ref, own_one, own_two, other_one, other_two = refs
    x = unpack(together(rows)).astype(jnp.bfloat16)
    gate_v = jnp.dot(x, gate_ref[...], preferred_element_type=jnp.float32)
    up_v = jnp.dot(x, up_ref[...], preferred_element_type=jnp.float32)
    hidden = (gate_v / (1.0 + jnp.exp(-gate_v)) * up_v).astype(jnp.bfloat16)
    part = jnp.dot(hidden, down_ref[...], preferred_element_type=jnp.float32)
    store((own_one, own_two, other_one, other_two), part)


def join_kernel(mine_ref, got_ref, *outs):
    store(outs, pack(mine_ref[...].astype(jnp.float32) + got_ref[...].astype(jnp.float32)))


def combine_kernel(paired, mix_ref, *refs):
    *refs, out_hbm, out, sems = refs
    blocks = [r[...].astype(jnp.float32) for r in refs]
    rows = jnp.concatenate([b[:SLOTS] for b in blocks[:paired]] + blocks[paired:], axis=0)
    mix = mix_ref[...]
    tail = out.shape[1] // 7
    copies = []
    for i in range(7):
        here = pl.ds(i * tail, tail)
        piece = rows[:, i * tail : (i + 1) * tail] if i < 6 else unpack_tail(rows)
        piece = piece.astype(jnp.bfloat16)
        both = jnp.concatenate([piece, piece], axis=0)
        out[:, here] = jnp.dot(mix, both, preferred_element_type=jnp.float32).astype(jnp.bfloat16)
        copies.append(pltpu.make_async_copy(out.at[:, here], out_hbm.at[:, here], sems.at[i]))
        copies[-1].start()
    for copy in copies:
        copy.wait()


def per_device(tokens, norm_gain, expert_ids, gate_weights, w_gate, w_up, w_down):
    owners = lax.axis_size("exp")
    flight = owners // 2
    count, width = tokens.shape
    few = relative(flight)

    def local(kernel, outs, name, *args, limit=16):
        return pl.pallas_call(
            kernel,
            out_shape=outs,
            in_specs=[VMEM] * len(args),
            out_specs=(VMEM,) * len(outs),
            compiler_params=pltpu.CompilerParams(vmem_limit_bytes=limit * 2**20),
            cost_estimate=SMALL,
            name=name,
        )(*args)

    def full(*counts):
        return tuple(jax.ShapeDtypeStruct((n * SLOTS, width), jnp.bfloat16) for n in counts)

    def packed(*counts):
        shapes = [(n * SLOTS, packed_width(width)) for n in counts]
        return tuple(jax.ShapeDtypeStruct(shape, jnp.bfloat16) for shape in shapes)

    def swap(rows):
        return lax.ppermute(rows, "exp", [(n, n ^ 1) for n in range(owners)])

    def travel(rows, distances, across=0):
        pairs = [(n, n ^ (2 * distances[n % 2]) ^ across) for n in range(owners)]
        return lax.ppermute(rows, "exp", pairs)

    def stage(mix):
        weights = w_gate[0], w_up[0], w_down[0]
        outs = [jax.ShapeDtypeStruct(w.shape, w.dtype) for w in weights]
        return pl.pallas_call(
            stage_kernel,
            out_shape=(*outs, jax.ShapeDtypeStruct(mix.shape[::-1], mix.dtype)),
            in_specs=[VMEM] + [HBM] * 3,
            out_specs=(VMEM,) * 4,
            scratch_shapes=[pltpu.SemaphoreType.DMA((3 * PIECES,))],
            compiler_params=pltpu.CompilerParams(vmem_limit_bytes=16 * 2**20),
            cost_estimate=SMALL,
            name="stage",
        )(mix, *in_hbm(*weights))

    def experts(rows, weights):
        outs = full(*[flight // 2] * 4)
        return local(expert_kernel, outs, "experts", *rows, *weights, limit=24)

    def join(outs, mine, theirs):
        return local(join_kernel, packed(*outs), "join", mine, swap(theirs))

    def combine(mix, arrays, paired):
        return pl.pallas_call(
            functools.partial(combine_kernel, paired),
            out_shape=jax.ShapeDtypeStruct((count, width), jnp.bfloat16),
            in_specs=[VMEM] * (len(arrays) + 1),
            out_specs=HBM,
            scratch_shapes=[
                pltpu.VMEM((count, width), jnp.bfloat16),
                pltpu.SemaphoreType.DMA((7,)),
            ],
            compiler_params=pltpu.CompilerParams(vmem_limit_bytes=24 * 2**20),
            name="combine",
        )(mix, *arrays)

    first = packed(3, 4, 1, 1) if few else packed(flight)
    mix, *outgoing = pl.pallas_call(
        functools.partial(dispatch_kernel, flight),
        out_shape=(jax.ShapeDtypeStruct((2 * flight * SLOTS, count), jnp.bfloat16),) + first,
        in_specs=[HBM] * 4,
        out_specs=(VMEM,) * (len(first) + 1),
        scratch_shapes=[
            pltpu.VMEM((count, width), jnp.bfloat16),
            pltpu.VMEM((1, width), jnp.float32),
            pltpu.VMEM(expert_ids.shape[::-1], jnp.int32),
            pltpu.VMEM(gate_weights.shape[::-1], jnp.float32),
            pltpu.SemaphoreType.DMA((3 + CHUNKS,)),
        ],
        compiler_params=pltpu.CompilerParams(vmem_limit_bytes=24 * 2**20),
        name="dispatch",
    )(*in_hbm(tokens, norm_gain, expert_ids.T, gate_weights.T))
    if not few:
        *weights, mix = stage(mix)
        groups = [list(range(core, owners, 2)) for core in range(2)]
        exchange = functools.partial(
            lax.all_to_all,
            axis_name="exp",
            split_axis=0,
            concat_axis=0,
            axis_index_groups=groups,
            tiled=True,
        )
        own = exchange(outgoing[0])
        mine_one, mine_two, theirs_one, theirs_two = experts([own, swap(own)], weights)
        half = flight // 2
        (joined_one,) = join([half], mine_one, theirs_one)
        (joined_two,) = join([half], mine_two, theirs_two)
        return combine(mix, [exchange(jnp.concatenate([joined_one, joined_two]))], 0)

    one, two, three = zip(*CARRIED)
    four = (SHARED, SHARED)
    kept, given, shared, own = outgoing
    *pairs, other_own = local(merge_kernel, packed(2, 2, 2, 1), "merge", kept, swap(given))
    shared = travel(shared, four)
    arrived = [travel(a, r) for a, r in zip(pairs, (one, two, three))] + [shared]
    *arrived, gate, up, down, mix = lax.optimization_barrier((*arrived, *stage(mix)))
    kernel = functools.partial(gather_kernel, 2)
    rows = local(kernel, packed(4, 3), "gather", *arrived)
    mine_one, mine_two, theirs_one, theirs_two = experts(
        (*rows, own, *[swap(a) for a in rows], other_own), (gate, up, down)
    )

    first, second = join((2, 2), mine_one, theirs_one)
    third, third_across, shared, own = join((1, 1, 1, 1), mine_two, theirs_two)
    first, second, shared = travel(first, one), travel(second, two), travel(shared, four)
    third, third_across = travel(third, three), travel(third_across, three, 1)
    shared, third, third_across = lax.optimization_barrier((shared, third, third_across))
    others = local(sift_kernel, packed(1, 1), "sift", first, second)
    others = [swap(a) for a in others]
    return combine(mix, [first, second, third, *others, third_across, shared, own], 2)


def solution(mesh):
    placed = (
        P(("group", "exp"), None),
        P(),
        P(("group", "exp"), None),
        P(("group", "exp"), None),
        P("exp", None, None),
        P("exp", None, None),
        P("exp", None, None),
    )
    return jax.shard_map(
        per_device, mesh=mesh, in_specs=placed, out_specs=P(("group", "exp"), None), check_vma=False
    )
```

```python
import functools

import jax
import jax.numpy as jnp
from jax import lax
from jax.experimental import pallas as pl
from jax.experimental.pallas import tpu as pltpu
from jax.sharding import PartitionSpec as P

SLOTS = 8
CHUNKS = 4
PIECES = 4
LANES = 128

VMEM = pl.BlockSpec(memory_space=pltpu.VMEM)
SMALL = pl.CostEstimate(flops=1, bytes_accessed=1, transcendentals=0)
HBM = pl.BlockSpec(memory_space=pltpu.HBM)


def in_hbm(*arrays):
    return [pltpu.with_memory_space_constraint(a, pltpu.HBM) for a in arrays]


def relative(flight):
    return flight == 8


CARRIED = ((4, 1, 5), (6, 2, 7))
SHARED = 3


def block_order(flight, core):
    if not relative(flight):
        return range(flight)
    return CARRIED[core] + CARRIED[1 - core] + (SHARED, 0)


def packed_width(width):
    return width // 7 * 6 + LANES


def pack(rows):
    blocks = rows.reshape(-1, SLOTS, rows.shape[1])
    tail = rows.shape[1] // 7
    main = blocks[:, :, : 6 * tail]
    moved = jnp.concatenate([blocks[:, j : j + 1, 6 * tail :] for j in range(6)], axis=2)
    row = lax.broadcasted_iota(jnp.int32, main.shape, 1)
    main = jnp.where(row == SLOTS - 1, moved, main)
    row = row[:, :, :LANES]
    extra = jnp.zeros(row.shape, rows.dtype)
    for k in range(tail // LANES):
        start = 6 * tail + k * LANES
        extra = jnp.where(row == k, blocks[:, 6:7, start : start + LANES], extra)
    return jnp.concatenate([main, extra], axis=2).reshape(rows.shape[0], -1)


def unpack_tail(packed):
    blocks = packed.reshape(-1, SLOTS, packed.shape[1])
    tail = (packed.shape[1] - LANES) // 6
    last = jnp.concatenate(
        [blocks[:, k : k + 1, 6 * tail :] for k in range(tail // LANES)], axis=2
    )
    row = lax.broadcasted_iota(jnp.int32, (blocks.shape[0], SLOTS, tail), 1)
    end = jnp.where(row == 6, last, 0.0)
    for j in range(6):
        end = jnp.where(row == j, blocks[:, 7:8, j * tail : (j + 1) * tail], end)
    return end.reshape(packed.shape[0], -1)


def unpack(packed):
    return jnp.concatenate([packed[:, : packed.shape[1] - LANES], unpack_tail(packed)], axis=1)


def store(refs, rows):
    at = 0
    for ref in refs:
        ref[...] = rows[at : at + ref.shape[0]].astype(ref.dtype)
        at += ref.shape[0]


def dispatch_kernel(flight, tok_hbm, gain_hbm, ids_hbm, gw_hbm, mix_ref, *rest):
    *outs, tok, gain, ids, gw, sems = rest
    count = tok.shape[0]
    part = count // CHUNKS
    small = [
        pltpu.make_async_copy(ids_hbm, ids, sems.at[0]),
        pltpu.make_async_copy(gw_hbm, gw, sems.at[1]),
        pltpu.make_async_copy(gain_hbm, gain.at[0], sems.at[2]),
    ]
    large = [
        pltpu.make_async_copy(
            tok_hbm.at[pl.ds(i * part, part)], tok.at[pl.ds(i * part, part)], sems.at[3 + i]
        )
        for i in range(CHUNKS)
    ]
    for copy in small + large:
        copy.start()
    small[0].wait()
    small[1].wait()
    experts = lax.broadcasted_iota(jnp.int32, (flight, count), 0)
    if relative(flight):
        place = experts
        me = lax.axis_index("exp")
        for i, (even, odd) in enumerate(zip(block_order(flight, 0), block_order(flight, 1))):
            experts = jnp.where(place == i, jnp.where(me % 2 == 0, even, odd) ^ (me // 2), experts)
    chosen = jnp.zeros((flight, count), jnp.float32)
    gates = jnp.zeros((flight, count), jnp.float32)
    for k in range(ids.shape[0]):
        hit = ids[k : k + 1, :] == experts
        chosen = jnp.where(hit, 1.0, chosen)
        gates = jnp.where(hit, gw[k : k + 1, :], gates)
    before = (
        lax.broadcasted_iota(jnp.int32, (count, count), 0)
        < lax.broadcasted_iota(jnp.int32, (count, count), 1)
    ).astype(jnp.bfloat16)
    rank = jnp.dot(chosen.astype(jnp.bfloat16), before, preferred_element_type=jnp.float32)
    rank = jnp.where(chosen > 0.0, rank, -1.0)

    slot = lax.broadcasted_iota(jnp.int32, (flight, SLOTS, count), 1).astype(jnp.float32)
    taken = rank[:, None, :] == slot
    pick = jnp.where(taken, 1.0, 0.0).reshape(flight * SLOTS, count).astype(jnp.bfloat16)
    mix = jnp.where(taken, gates[:, None, :], 0.0).reshape(flight * SLOTS, count)
    high = mix.astype(jnp.bfloat16)
    mix_ref[: flight * SLOTS, :] = high
    mix_ref[flight * SLOTS :, :] = (mix - high.astype(jnp.float32)).astype(jnp.bfloat16)

    for copy in large:
        copy.wait()
    wide = jnp.dot(pick, tok[...], preferred_element_type=jnp.float32)
    mean_square = jnp.mean(wide * wide, axis=1, keepdims=True)
    small[2].wait()
    rows = (wide * lax.rsqrt(mean_square + 1e-06) * gain[...]).astype(jnp.bfloat16)
    rows = rows.astype(jnp.float32)
    blocks = pack(rows)
    if len(outs) == 1:
        store(outs, blocks)
    else:
        kept, given = 3 * SLOTS, 6 * SLOTS
        store(outs[:1], blocks[:kept])
        store(outs[1:2], jnp.concatenate([blocks[kept:given], blocks[given + SLOTS :]], axis=0))
        store(outs[2:], blocks[given:])


def stage_kernel(mix_ref, *refs):
    *refs, turned_ref, sems = refs
    sources, targets = refs[:3], refs[3:]
    copies = []
    for at, (source, target) in enumerate(zip(sources, targets)):
        rows = source.shape[0] // PIECES
        for i in range(PIECES):
            here = pl.ds(i * rows, rows)
            copies.append(
                pltpu.make_async_copy(source.at[here], target.at[here], sems.at[at * PIECES + i])
            )
    for copy in copies:
        copy.start()
    turned_ref[...] = mix_ref[...].T
    for copy in copies:
        copy.wait()


def together(refs):
    return jnp.concatenate([b[...].astype(jnp.float32) for b in refs], axis=0)


def merge_kernel(kept_ref, got_ref, *outs):
    *outs, own_out = outs
    kept, got = kept_ref[...].astype(jnp.float32), got_ref[...].astype(jnp.float32)
    for i, out in enumerate(outs):
        here = slice(i * SLOTS, (i + 1) * SLOTS)
        out[...] = jnp.concatenate([kept[here], got[here]], axis=0).astype(jnp.bfloat16)
    own_out[...] = got[len(outs) * SLOTS :].astype(jnp.bfloat16)


def gather_kernel(count, *refs):
    store(refs[-count:], together(refs[:-count]))


def sift_kernel(*refs):
    count = len(refs) // 2
    for ref, out in zip(refs[:count], refs[count + 1 :]):
        out[...] = ref[...].astype(jnp.float32)[SLOTS:].astype(jnp.bfloat16)


def expert_kernel(*refs):
    *rows, gate_ref, up_ref, down_ref, own_one, own_two, other_one, other_two = refs
    x = unpack(together(rows)).astype(jnp.bfloat16)
    gate_v = jnp.dot(x, gate_ref[...], preferred_element_type=jnp.float32)
    up_v = jnp.dot(x, up_ref[...], preferred_element_type=jnp.float32)
    hidden = (gate_v / (1.0 + jnp.exp(-gate_v)) * up_v).astype(jnp.bfloat16)
    part = jnp.dot(hidden, down_ref[...], preferred_element_type=jnp.float32)
    store((own_one, own_two, other_one, other_two), part)


def join_kernel(mine_ref, got_ref, *outs):
    store(outs, pack(mine_ref[...].astype(jnp.float32) + got_ref[...].astype(jnp.float32)))


def combine_kernel(paired, mix_ref, *refs):
    *refs, out_hbm, out, sems = refs
    blocks = [r[...].astype(jnp.float32) for r in refs]
    rows = jnp.concatenate([b[:SLOTS] for b in blocks[:paired]] + blocks[paired:], axis=0)
    mix = mix_ref[...]
    tail = out.shape[1] // 7
    copies = []
    for i in range(7):
        here = pl.ds(i * tail, tail)
        piece = rows[:, i * tail : (i + 1) * tail] if i < 6 else unpack_tail(rows)
        piece = piece.astype(jnp.bfloat16)
        both = jnp.concatenate([piece, piece], axis=0)
        out[:, here] = jnp.dot(mix, both, preferred_element_type=jnp.float32).astype(jnp.bfloat16)
        copies.append(pltpu.make_async_copy(out.at[:, here], out_hbm.at[:, here], sems.at[i]))
        copies[-1].start()
    for copy in copies:
        copy.wait()


def per_device(tokens, norm_gain, expert_ids, gate_weights, w_gate, w_up, w_down):
    owners = lax.axis_size("exp")
    flight = owners // 2
    count, width = tokens.shape
    few = relative(flight)

    def local(kernel, outs, name, *args, limit=16):
        return pl.pallas_call(
            kernel,
            out_shape=outs,
            in_specs=[VMEM] * len(args),
            out_specs=(VMEM,) * len(outs),
            compiler_params=pltpu.CompilerParams(vmem_limit_bytes=limit * 2**20),
            cost_estimate=SMALL,
            name=name,
        )(*args)

    def full(*counts):
        return tuple(jax.ShapeDtypeStruct((n * SLOTS, width), jnp.bfloat16) for n in counts)

    def packed(*counts):
        shapes = [(n * SLOTS, packed_width(width)) for n in counts]
        return tuple(jax.ShapeDtypeStruct(shape, jnp.bfloat16) for shape in shapes)

    def swap(rows):
        return lax.ppermute(rows, "exp", [(n, n ^ 1) for n in range(owners)])

    def travel(rows, distances, across=0):
        pairs = [(n, n ^ (2 * distances[n % 2]) ^ across) for n in range(owners)]
        return lax.ppermute(rows, "exp", pairs)

    def stage(mix):
        weights = w_gate[0], w_up[0], w_down[0]
        outs = [jax.ShapeDtypeStruct(w.shape, w.dtype) for w in weights]
        return pl.pallas_call(
            stage_kernel,
            out_shape=(*outs, jax.ShapeDtypeStruct(mix.shape[::-1], mix.dtype)),
            in_specs=[VMEM] + [HBM] * 3,
            out_specs=(VMEM,) * 4,
            scratch_shapes=[pltpu.SemaphoreType.DMA((3 * PIECES,))],
            compiler_params=pltpu.CompilerParams(vmem_limit_bytes=16 * 2**20),
            cost_estimate=SMALL,
            name="stage",
        )(mix, *in_hbm(*weights))

    def experts(rows, weights):
        outs = full(*[flight // 2] * 4)
        return local(expert_kernel, outs, "experts", *rows, *weights, limit=24)

    def join(outs, mine, theirs):
        return local(join_kernel, packed(*outs), "join", mine, theirs)

    def combine(mix, arrays, paired):
        return pl.pallas_call(
            functools.partial(combine_kernel, paired),
            out_shape=jax.ShapeDtypeStruct((count, width), jnp.bfloat16),
            in_specs=[VMEM] * (len(arrays) + 1),
            out_specs=HBM,
            scratch_shapes=[
                pltpu.VMEM((count, width), jnp.bfloat16),
                pltpu.SemaphoreType.DMA((7,)),
            ],
            compiler_params=pltpu.CompilerParams(vmem_limit_bytes=24 * 2**20),
            name="combine",
        )(mix, *arrays)

    first = packed(3, 4, 1, 1) if few else packed(flight)
    mix, *outgoing = pl.pallas_call(
        functools.partial(dispatch_kernel, flight),
        out_shape=(jax.ShapeDtypeStruct((2 * flight * SLOTS, count), jnp.bfloat16),) + first,
        in_specs=[HBM] * 4,
        out_specs=(VMEM,) * (len(first) + 1),
        scratch_shapes=[
            pltpu.VMEM((count, width), jnp.bfloat16),
            pltpu.VMEM((1, width), jnp.float32),
            pltpu.VMEM(expert_ids.shape[::-1], jnp.int32),
            pltpu.VMEM(gate_weights.shape[::-1], jnp.float32),
            pltpu.SemaphoreType.DMA((3 + CHUNKS,)),
        ],
        compiler_params=pltpu.CompilerParams(vmem_limit_bytes=24 * 2**20),
        name="dispatch",
    )(*in_hbm(tokens, norm_gain, expert_ids.T, gate_weights.T))
    if not few:
        *weights, mix = stage(mix)
        groups = [list(range(core, owners, 2)) for core in range(2)]
        exchange = functools.partial(
            lax.all_to_all,
            axis_name="exp",
            split_axis=0,
            concat_axis=0,
            axis_index_groups=groups,
            tiled=True,
        )
        own = exchange(outgoing[0])
        mine_one, mine_two, theirs_one, theirs_two = experts([own, swap(own)], weights)
        half = flight // 2
        (joined_one,) = join([half], mine_one, swap(theirs_one))
        (joined_two,) = join([half], mine_two, swap(theirs_two))
        return combine(mix, [exchange(jnp.concatenate([joined_one, joined_two]))], 0)

    one, two, three = zip(*CARRIED)
    four = (SHARED, SHARED)
    kept, given, shared, own = outgoing
    *pairs, other_own = local(merge_kernel, packed(2, 2, 2, 1), "merge", kept, swap(given))
    shared = travel(shared, four)
    arrived = [travel(a, r) for a, r in zip(pairs, (one, two, three))] + [shared]
    *arrived, gate, up, down, mix = lax.optimization_barrier((*arrived, *stage(mix)))
    kernel = functools.partial(gather_kernel, 2)
    rows = local(kernel, packed(4, 3), "gather", *arrived)
    mine_one, mine_two, theirs_one, theirs_two = experts(
        (*rows, own, *[swap(a) for a in rows], other_own), (gate, up, down)
    )

    theirs_one = swap(theirs_one)
    theirs_two, theirs_one = lax.optimization_barrier((theirs_two, theirs_one))
    first, second = join((2, 2), mine_one, theirs_one)
    third, third_across, shared, own = join((1, 1, 1, 1), mine_two, swap(theirs_two))
    first, second, shared = travel(first, one), travel(second, two), travel(shared, four)
    before = third
    third, third_across = travel(third, three), travel(third_across, three, 1)
    others = local(sift_kernel, packed(1, 1), "sift", first, second, before)
    others = [swap(a) for a in others]
    return combine(mix, [first, second, third, *others, third_across, shared, own], 2)


def solution(mesh):
    placed = (
        P(("group", "exp"), None),
        P(),
        P(("group", "exp"), None),
        P(("group", "exp"), None),
        P("exp", None, None),
        P("exp", None, None),
        P("exp", None, None),
    )
    return jax.shard_map(
        per_device, mesh=mesh, in_specs=placed, out_specs=P(("group", "exp"), None), check_vma=False
    )
```

```python
import functools

import jax
import jax.numpy as jnp
from jax import lax
from jax.experimental import pallas as pl
from jax.experimental.pallas import tpu as pltpu
from jax.sharding import PartitionSpec as P

SLOTS = 8
CHUNKS = 4
PIECES = 4
LANES = 128

VMEM = pl.BlockSpec(memory_space=pltpu.VMEM)
SMALL = pl.CostEstimate(flops=1, bytes_accessed=1, transcendentals=0)
HBM = pl.BlockSpec(memory_space=pltpu.HBM)


def in_hbm(*arrays):
    return [pltpu.with_memory_space_constraint(a, pltpu.HBM) for a in arrays]


def relative(flight):
    return flight == 8


CARRIED = ((4, 1, 5), (6, 2, 7))
SHARED = 3


def block_order(flight, core):
    if not relative(flight):
        return range(flight)
    return CARRIED[core] + CARRIED[1 - core] + (SHARED, 0)


def packed_width(width):
    return width // 7 * 6 + LANES


def pack(rows):
    blocks = rows.reshape(-1, SLOTS, rows.shape[1])
    tail = rows.shape[1] // 7
    main = blocks[:, :, : 6 * tail]
    moved = jnp.concatenate([blocks[:, j : j + 1, 6 * tail :] for j in range(6)], axis=2)
    row = lax.broadcasted_iota(jnp.int32, main.shape, 1)
    main = jnp.where(row == SLOTS - 1, moved, main)
    row = row[:, :, :LANES]
    extra = jnp.zeros(row.shape, rows.dtype)
    for k in range(tail // LANES):
        start = 6 * tail + k * LANES
        extra = jnp.where(row == k, blocks[:, 6:7, start : start + LANES], extra)
    return jnp.concatenate([main, extra], axis=2).reshape(rows.shape[0], -1)


def unpack_tail(packed):
    blocks = packed.reshape(-1, SLOTS, packed.shape[1])
    tail = (packed.shape[1] - LANES) // 6
    last = jnp.concatenate(
        [blocks[:, k : k + 1, 6 * tail :] for k in range(tail // LANES)], axis=2
    )
    row = lax.broadcasted_iota(jnp.int32, (blocks.shape[0], SLOTS, tail), 1)
    end = jnp.where(row == 6, last, 0.0)
    for j in range(6):
        end = jnp.where(row == j, blocks[:, 7:8, j * tail : (j + 1) * tail], end)
    return end.reshape(packed.shape[0], -1)


def unpack(packed):
    return jnp.concatenate([packed[:, : packed.shape[1] - LANES], unpack_tail(packed)], axis=1)


def store(refs, rows):
    at = 0
    for ref in refs:
        ref[...] = rows[at : at + ref.shape[0]].astype(ref.dtype)
        at += ref.shape[0]


def dispatch_kernel(flight, tok_hbm, gain_hbm, ids_hbm, gw_hbm, mix_ref, *rest):
    *outs, tok, gain, ids, gw, sems = rest
    count = tok.shape[0]
    part = count // CHUNKS
    small = [
        pltpu.make_async_copy(ids_hbm, ids, sems.at[0]),
        pltpu.make_async_copy(gw_hbm, gw, sems.at[1]),
        pltpu.make_async_copy(gain_hbm, gain.at[0], sems.at[2]),
    ]
    large = [
        pltpu.make_async_copy(
            tok_hbm.at[pl.ds(i * part, part)], tok.at[pl.ds(i * part, part)], sems.at[3 + i]
        )
        for i in range(CHUNKS)
    ]
    for copy in small + large:
        copy.start()
    small[0].wait()
    small[1].wait()
    experts = lax.broadcasted_iota(jnp.int32, (flight, count), 0)
    if relative(flight):
        place = experts
        me = lax.axis_index("exp")
        for i, (even, odd) in enumerate(zip(block_order(flight, 0), block_order(flight, 1))):
            experts = jnp.where(place == i, jnp.where(me % 2 == 0, even, odd) ^ (me // 2), experts)
    chosen = jnp.zeros((flight, count), jnp.float32)
    gates = jnp.zeros((flight, count), jnp.float32)
    for k in range(ids.shape[0]):
        hit = ids[k : k + 1, :] == experts
        chosen = jnp.where(hit, 1.0, chosen)
        gates = jnp.where(hit, gw[k : k + 1, :], gates)
    before = (
        lax.broadcasted_iota(jnp.int32, (count, count), 0)
        < lax.broadcasted_iota(jnp.int32, (count, count), 1)
    ).astype(jnp.bfloat16)
    rank = jnp.dot(chosen.astype(jnp.bfloat16), before, preferred_element_type=jnp.float32)
    rank = jnp.where(chosen > 0.0, rank, -1.0)

    slot = lax.broadcasted_iota(jnp.int32, (flight, SLOTS, count), 1).astype(jnp.float32)
    taken = rank[:, None, :] == slot
    pick = jnp.where(taken, 1.0, 0.0).reshape(flight * SLOTS, count).astype(jnp.bfloat16)
    mix = jnp.where(taken, gates[:, None, :], 0.0).reshape(flight * SLOTS, count)
    high = mix.astype(jnp.bfloat16)
    mix_ref[: flight * SLOTS, :] = high
    mix_ref[flight * SLOTS :, :] = (mix - high.astype(jnp.float32)).astype(jnp.bfloat16)

    for copy in large:
        copy.wait()
    wide = jnp.dot(pick, tok[...], preferred_element_type=jnp.float32)
    mean_square = jnp.mean(wide * wide, axis=1, keepdims=True)
    small[2].wait()
    rows = (wide * lax.rsqrt(mean_square + 1e-06) * gain[...]).astype(jnp.bfloat16)
    rows = rows.astype(jnp.float32)
    blocks = pack(rows)
    if len(outs) == 1:
        store(outs, blocks)
    else:
        kept, given = 3 * SLOTS, 6 * SLOTS
        store(outs[:1], blocks[:kept])
        store(outs[1:2], jnp.concatenate([blocks[kept:given], blocks[given + SLOTS :]], axis=0))
        store(outs[2:], blocks[given:])


def stage_kernel(mix_ref, *refs):
    *refs, turned_ref, sems = refs
    sources, targets = refs[:3], refs[3:]
    copies = []
    for at, (source, target) in enumerate(zip(sources, targets)):
        rows = source.shape[0] // PIECES
        for i in range(PIECES):
            here = pl.ds(i * rows, rows)
            copies.append(
                pltpu.make_async_copy(source.at[here], target.at[here], sems.at[at * PIECES + i])
            )
    for copy in copies:
        copy.start()
    turned_ref[...] = mix_ref[...].T
    for copy in copies:
        copy.wait()


def together(refs):
    return jnp.concatenate([b[...].astype(jnp.float32) for b in refs], axis=0)


def merge_kernel(kept_ref, got_ref, *outs):
    *outs, own_out = outs
    kept, got = kept_ref[...].astype(jnp.float32), got_ref[...].astype(jnp.float32)
    for i, out in enumerate(outs):
        here = slice(i * SLOTS, (i + 1) * SLOTS)
        out[...] = jnp.concatenate([kept[here], got[here]], axis=0).astype(jnp.bfloat16)
    own_out[...] = got[len(outs) * SLOTS :].astype(jnp.bfloat16)


def gather_kernel(count, *refs):
    store(refs[-count:], together(refs[:-count]))


def sift_kernel(*refs):
    count = len(refs) // 2
    for ref, out in zip(refs[:count], refs[count:]):
        out[...] = ref[...].astype(jnp.float32)[SLOTS:].astype(jnp.bfloat16)


def expert_kernel(*refs):
    *rows, gate_ref, up_ref, down_ref, own_one, own_two, other_one, other_two = refs
    x = unpack(together(rows)).astype(jnp.bfloat16)
    gate_v = jnp.dot(x, gate_ref[...], preferred_element_type=jnp.float32)
    up_v = jnp.dot(x, up_ref[...], preferred_element_type=jnp.float32)
    hidden = (gate_v / (1.0 + jnp.exp(-gate_v)) * up_v).astype(jnp.bfloat16)
    part = jnp.dot(hidden, down_ref[...], preferred_element_type=jnp.float32)
    store((own_one, own_two, other_one, other_two), part)


def join_kernel(mine_ref, got_ref, *outs):
    store(outs, pack(mine_ref[...].astype(jnp.float32) + got_ref[...].astype(jnp.float32)))


def combine_kernel(paired, mix_ref, *refs):
    *refs, out_hbm, out, sems = refs
    blocks = [r[...].astype(jnp.float32) for r in refs]
    rows = jnp.concatenate([b[:SLOTS] for b in blocks[:paired]] + blocks[paired:], axis=0)
    mix = mix_ref[...]
    tail = out.shape[1] // 7
    copies = []
    for i in range(7):
        here = pl.ds(i * tail, tail)
        piece = rows[:, i * tail : (i + 1) * tail] if i < 6 else unpack_tail(rows)
        piece = piece.astype(jnp.bfloat16)
        both = jnp.concatenate([piece, piece], axis=0)
        out[:, here] = jnp.dot(mix, both, preferred_element_type=jnp.float32).astype(jnp.bfloat16)
        copies.append(pltpu.make_async_copy(out.at[:, here], out_hbm.at[:, here], sems.at[i]))
        copies[-1].start()
    for copy in copies:
        copy.wait()


def per_device(tokens, norm_gain, expert_ids, gate_weights, w_gate, w_up, w_down):
    owners = lax.axis_size("exp")
    flight = owners // 2
    count, width = tokens.shape
    few = relative(flight)

    def local(kernel, outs, name, *args, limit=16):
        return pl.pallas_call(
            kernel,
            out_shape=outs,
            in_specs=[VMEM] * len(args),
            out_specs=(VMEM,) * len(outs),
            compiler_params=pltpu.CompilerParams(vmem_limit_bytes=limit * 2**20),
            cost_estimate=SMALL,
            name=name,
        )(*args)

    def full(*counts):
        return tuple(jax.ShapeDtypeStruct((n * SLOTS, width), jnp.bfloat16) for n in counts)

    def packed(*counts):
        shapes = [(n * SLOTS, packed_width(width)) for n in counts]
        return tuple(jax.ShapeDtypeStruct(shape, jnp.bfloat16) for shape in shapes)

    def swap(rows):
        return lax.ppermute(rows, "exp", [(n, n ^ 1) for n in range(owners)])

    def travel(rows, distances, across=0):
        pairs = [(n, n ^ (2 * distances[n % 2]) ^ across) for n in range(owners)]
        return lax.ppermute(rows, "exp", pairs)

    def stage(mix):
        weights = w_gate[0], w_up[0], w_down[0]
        outs = [jax.ShapeDtypeStruct(w.shape, w.dtype) for w in weights]
        return pl.pallas_call(
            stage_kernel,
            out_shape=(*outs, jax.ShapeDtypeStruct(mix.shape[::-1], mix.dtype)),
            in_specs=[VMEM] + [HBM] * 3,
            out_specs=(VMEM,) * 4,
            scratch_shapes=[pltpu.SemaphoreType.DMA((3 * PIECES,))],
            compiler_params=pltpu.CompilerParams(vmem_limit_bytes=16 * 2**20),
            cost_estimate=SMALL,
            name="stage",
        )(mix, *in_hbm(*weights))

    def experts(rows, weights):
        outs = full(*[flight // 2] * 4)
        return local(expert_kernel, outs, "experts", *rows, *weights, limit=24)

    def join(outs, mine, theirs):
        return local(join_kernel, packed(*outs), "join", mine, swap(theirs))

    def combine(mix, arrays, paired):
        return pl.pallas_call(
            functools.partial(combine_kernel, paired),
            out_shape=jax.ShapeDtypeStruct((count, width), jnp.bfloat16),
            in_specs=[VMEM] * (len(arrays) + 1),
            out_specs=HBM,
            scratch_shapes=[
                pltpu.VMEM((count, width), jnp.bfloat16),
                pltpu.SemaphoreType.DMA((7,)),
            ],
            compiler_params=pltpu.CompilerParams(vmem_limit_bytes=24 * 2**20),
            name="combine",
        )(mix, *arrays)

    first = packed(3, 4, 1, 1) if few else packed(flight)
    mix, *outgoing = pl.pallas_call(
        functools.partial(dispatch_kernel, flight),
        out_shape=(jax.ShapeDtypeStruct((2 * flight * SLOTS, count), jnp.bfloat16),) + first,
        in_specs=[HBM] * 4,
        out_specs=(VMEM,) * (len(first) + 1),
        scratch_shapes=[
            pltpu.VMEM((count, width), jnp.bfloat16),
            pltpu.VMEM((1, width), jnp.float32),
            pltpu.VMEM(expert_ids.shape[::-1], jnp.int32),
            pltpu.VMEM(gate_weights.shape[::-1], jnp.float32),
            pltpu.SemaphoreType.DMA((3 + CHUNKS,)),
        ],
        compiler_params=pltpu.CompilerParams(vmem_limit_bytes=24 * 2**20),
        name="dispatch",
    )(*in_hbm(tokens, norm_gain, expert_ids.T, gate_weights.T))
    if not few:
        *weights, mix = stage(mix)
        groups = [list(range(core, owners, 2)) for core in range(2)]
        exchange = functools.partial(
            lax.all_to_all,
            axis_name="exp",
            split_axis=0,
            concat_axis=0,
            axis_index_groups=groups,
            tiled=True,
        )
        own = exchange(outgoing[0])
        mine_one, mine_two, theirs_one, theirs_two = experts([own, swap(own)], weights)
        half = flight // 2
        (joined_one,) = join([half], mine_one, theirs_one)
        (joined_two,) = join([half], mine_two, theirs_two)
        return combine(mix, [exchange(jnp.concatenate([joined_one, joined_two]))], 0)

    one, two, three = zip(*CARRIED)
    four = (SHARED, SHARED)
    kept, given, shared, own = outgoing
    *pairs, other_own = local(merge_kernel, packed(2, 2, 2, 1), "merge", kept, swap(given))
    shared = travel(shared, four)
    arrived = [travel(a, r) for a, r in zip(pairs, (one, two, three))] + [shared]
    *arrived, gate, up, down, mix = lax.optimization_barrier((*arrived, *stage(mix)))
    kernel = functools.partial(gather_kernel, 1)
    rows = local(kernel, packed(7), "gather", *arrived)
    mine_one, mine_two, theirs_one, theirs_two = experts(
        (*rows, own, *[swap(a) for a in rows], other_own), (gate, up, down)
    )

    first, second = join((2, 2), mine_one, theirs_one)
    third, third_across, shared, own = join((1, 1, 1, 1), mine_two, theirs_two)
    first, second, shared = travel(first, one), travel(second, two), travel(shared, four)
    third, third_across = travel(third, three), travel(third_across, three, 1)
    others = local(sift_kernel, packed(1, 1), "sift", first, second)
    others = [swap(a) for a in others]
    return combine(mix, [first, second, third, *others, third_across, shared, own], 2)


def solution(mesh):
    placed = (
        P(("group", "exp"), None),
        P(),
        P(("group", "exp"), None),
        P(("group", "exp"), None),
        P("exp", None, None),
        P("exp", None, None),
        P("exp", None, None),
    )
    return jax.shard_map(
        per_device, mesh=mesh, in_specs=placed, out_specs=P(("group", "exp"), None), check_vma=False
    )
```
